256 devices in a mesh: dp: 64 (over z, y, core), mp: 4 (over x).
Axes of the slice: x: 4, y: 4, z: 8, core: 2. Of those that a mesh axis runs over, the one named last changes fastest.
Arguments:
- last_query: bfloat16 [2048, 4096], P('dp', 'mp'), may hold values from -6 to 6
- key_cache: bfloat16 [131072, 1024], P('dp', 'mp'), may hold values from -6 to 6
- value_cache: bfloat16 [131072, 1024], P('dp', 'mp'), may hold values from -6 to 6
- residual: bfloat16 [2048, 4096], P('dp', 'mp'), may hold values from -6 to 6
- out_weight: bfloat16 [4096, 4096], P('mp'), may hold values from -0.09375 to 0.09375
- query_emb: bfloat16 [2048, 4096], P('dp', 'mp'), may hold values from -1 to 1
- lengths: int32 [64, 32], P('dp'), may hold values from 1 to 256, 2048 in all within a row
- positives: int32 [2048], P('dp'), may hold values from 0 to 2047, each once
Outputs:
- query_loss: float32 [2048], P('dp')
- query_grad: float32 [2048, 4096], P('dp', 'mp')
- residual_grad: float32 [2048, 4096], P('dp', 'mp')
- lastq_grad: float32 [2048, 4096], P('dp', 'mp')
- key_grad: bfloat16 [131072, 1024], P('dp', 'mp')
- value_grad: bfloat16 [131072, 1024], P('dp', 'mp')
The draws below stay inside these ranges and needn't reach their ends.
Inputs may be any that keep to these rules, and one draw needn't show every extreme that they name: Each row of lengths sums to 2048; its largest entry is 256. `positives`: each passage is the positive of exactly one query.
All inputs are finite; a program needn't handle non-finite values.
Results may differ from the reference program's by a relative error of at most 0.029.
Values may be sent and summed in bfloat16 or wider, within the bound.
A program may use at most 128 MiB of HBM per device.

```python
import math
import jax
import jax.numpy as jnp
import numpy as np
from jax import lax

HEADS = 32
KV_HEADS = 8
HEAD_DIM = 128
D = 4096
PDEV = 32
TOK_DEV = 2048
LMAX = 256
PAIRS = 2048
TOKENS = 131072
N_DP = 64


def column_scale(width, ratio):
    place = jnp.arange(width, dtype=jnp.float32) / max(width - 1, 1)
    return jnp.exp(jnp.log(ratio) * (place - 0.5))


def draw_last_query(key, part):
    key = jax.random.fold_in(key, 1)
    base = jnp.clip(jax.random.normal(key, (PAIRS, HEADS * HEAD_DIM), jnp.float32), -6.0, 6.0)
    return base.astype(jnp.bfloat16)


def draw_key_cache(key, part):
    key = jax.random.fold_in(key, 5)
    base = jnp.clip(jax.random.normal(key, (TOKENS, KV_HEADS * HEAD_DIM), jnp.float32), -6.0, 6.0)
    return base.astype(jnp.bfloat16)


def draw_residual(key, part):
    key = jax.random.fold_in(key, 7)
    ratio = 5.0
    base = jnp.clip(jax.random.normal(key, (PAIRS, D), jnp.float32), -6.0, 6.0)
    return jnp.clip(0.3 * base * column_scale(D, ratio)[None, :], -6.0, 6.0).astype(jnp.bfloat16)


def draw_query_emb(key, part):
    key = jax.random.fold_in(key, 9)
    ratio = 5.0
    base = jnp.clip(jax.random.normal(key, (PAIRS, D), jnp.float32), -6.0, 6.0)
    return jnp.clip(0.015625 * base * column_scale(D, ratio)[None, :], -1.0, 1.0).astype(jnp.bfloat16)


def block_levels(own_key, shape, cuts, smallest, largest):
    level, own = 1.0, jax.random.fold_in(own_key, 6)
    for axis_at, blocks in cuts:
        steps = jnp.exp(jax.random.uniform(jax.random.fold_in(own, axis_at), (blocks,), jnp.float32, smallest / len(cuts), largest / len(cuts)))
        level = level * jnp.repeat(steps, shape[axis_at] // blocks).reshape([-1 if axis == axis_at else 1 for axis in range(len(shape))])
    return level


def profile(count, total, limit, skew):
    weights = [(1 << 20) // math.isqrt(standing ** skew) + 1 for standing in range(2, count + 1)]
    surplus, holding = total - limit - (count - 1), [1] * (count - 1)
    while surplus > 0:
        movable = [i for i in range(count - 1) if holding[i] < limit]
        pool, left = sum([weights[i] for i in movable]), surplus
        for i in movable:
            addition = min(limit - holding[i], max(1, left * weights[i] // pool), surplus)
            holding[i] = holding[i] + addition
            surplus = surplus - addition
    return np.array([limit] + holding)


def uneven_parts(rng, amount, total, limit, skew):
    if amount == 2:
        one = jax.random.randint(rng, (), max(1, total - limit), min(limit, total - 1) + 1)
        return jnp.stack([one, total - one])
    sizes = jnp.asarray(profile(amount, total, limit, skew), jnp.int32)
    pairs = (amount - 1) // 2
    source_of, taker = sizes[1:1 + 2 * pairs:2], sizes[2:2 + 2 * pairs:2]
    margin = jnp.minimum(source_of - 1, limit - taker)
    shifted = jax.random.randint(jax.random.fold_in(rng, 1), (pairs,), 0, 1 << 20) % (margin + 1)
    sizes = sizes.at[1:1 + 2 * pairs:2].set(source_of - shifted).at[2:2 + 2 * pairs:2].set(taker + shifted)
    return sizes[jax.random.permutation(jax.random.fold_in(rng, 2), amount)]


def bell_draw(stream_key, dims, scale, most, split=(), kind=jnp.bfloat16):
    drawn = scale * jax.random.normal(stream_key, dims, jnp.float32)
    if split:
        drawn = drawn * block_levels(stream_key, dims, split, -0.22, 0.18)
    return jnp.clip(drawn, -most, most).astype(kind)


def setup_inputs(seed: int = 0) -> dict:
    seeds = jax.random.split(jax.random.key(seed), 9)
    return {
        "last_query": draw_last_query(jax.random.fold_in(seeds[8], 71), 0),
        "key_cache": draw_key_cache(jax.random.fold_in(seeds[8], 71), 0),
        "value_cache": bell_draw(seeds[2], (TOKENS, KV_HEADS * HEAD_DIM), 1.0, 6.0, ((0, 64), (1, 4))),
        "residual": draw_residual(jax.random.fold_in(seeds[8], 71), 0),
        "out_weight": bell_draw(seeds[4], (HEADS * HEAD_DIM, D), (HEADS * HEAD_DIM) ** -0.5, 0.09375, ((0, 4),)),
        "query_emb": draw_query_emb(jax.random.fold_in(seeds[8], 71), 0),
        "lengths": jax.vmap(lambda own: uneven_parts(own, PDEV, TOK_DEV, LMAX, 2))(jax.random.split(seeds[6], N_DP)).reshape((N_DP, PDEV)).astype(jnp.int32),
        "positives": jax.random.permutation(seeds[7], PAIRS).astype(jnp.int32),
    }


inv_temp = 50.0
epsilon = 1e-06

def slot_table(length_row):
    starts = jnp.cumsum(length_row) - length_row
    offsets = jnp.arange(LMAX, dtype=jnp.int32)
    table = starts[:, None] + offsets[None, :]
    usable = offsets[None, :] < length_row[:, None]
    return (jnp.where(usable, table, 0).astype(jnp.int32), usable)

def attend(queries, key_block, value_block, table, usable):
    rows = queries.shape[0]
    groups = key_block.shape[1] // HEAD_DIM
    key_slots = key_block[table].reshape(rows, LMAX, groups, HEAD_DIM)
    value_slots = value_block[table].reshape(rows, LMAX, groups, HEAD_DIM)
    grouped = queries.reshape(rows, groups, -1, HEAD_DIM)
    scale = 1.0 / HEAD_DIM ** 0.5
    scores = jnp.einsum('pkgd,plkd->pkgl', grouped.astype(jnp.float32), key_slots.astype(jnp.float32)) * scale
    scores = jnp.where(usable[:, None, None, :], scores, -1e+30)
    weights = jax.nn.softmax(scores, axis=-1)
    probs = weights.astype(jnp.bfloat16)
    output = jnp.einsum('pkgl,plkd->pkgd', probs.astype(jnp.float32), value_slots.astype(jnp.float32))
    return (output.reshape(rows, -1), weights, probs, grouped, key_slots, value_slots)

def attend_back(upstream, weights, probs, grouped, key_slots, value_slots, table, token_count):
    rows = grouped.shape[0]
    groups = grouped.shape[1]
    scale = 1.0 / HEAD_DIM ** 0.5
    heads_up = upstream.reshape(rows, groups, -1, HEAD_DIM).astype(jnp.float32)
    weight_slope = jnp.einsum('pkgd,plkd->pkgl', heads_up, value_slots.astype(jnp.float32))
    score_grad = weights * (weight_slope - lax.optimization_barrier(jnp.sum(weights * weight_slope, axis=-1, keepdims=True)))
    score_slope = score_grad.astype(jnp.bfloat16).astype(jnp.float32)
    query_part = jnp.einsum('pkgl,plkd->pkgd', score_slope, key_slots.astype(jnp.float32)) * scale
    key_part = jnp.einsum('pkgl,pkgd->plkd', score_slope, grouped.astype(jnp.float32)) * scale
    value_part = jnp.einsum('pkgl,pkgd->plkd', probs.astype(jnp.float32), heads_up)
    flat = table.reshape(-1)
    width = groups * HEAD_DIM
    key_total = jnp.zeros((token_count, width), jnp.float32).at[flat].add(key_part.reshape(-1, width))
    value_total = jnp.zeros((token_count, width), jnp.float32).at[flat].add(value_part.reshape(-1, width))
    return (query_part.reshape(rows, -1), key_total.astype(jnp.bfloat16), value_total.astype(jnp.bfloat16))

def reference(last_query, key_cache, value_cache, residual, out_weight, query_emb, lengths, positives):
    query_blocks = last_query.reshape(N_DP, PDEV, -1)
    key_blocks = key_cache.reshape(N_DP, TOK_DEV, -1)
    value_blocks = value_cache.reshape(N_DP, TOK_DEV, -1)

    def forward_block(pieces):
        queries, key_block, value_block, length_row = pieces
        table, usable = slot_table(length_row)
        return attend(queries, key_block, value_block, table, usable)[0].astype(jnp.bfloat16)
    attended = lax.map(forward_block, (query_blocks, key_blocks, value_blocks, lengths)).reshape(PAIRS, -1)
    hidden = residual.astype(jnp.float32) + jnp.dot(attended, out_weight, preferred_element_type=jnp.float32)
    norm = jnp.sqrt(lax.optimization_barrier(jnp.sum(hidden * hidden, axis=1)) + epsilon)
    passage_emb = (hidden / norm[:, None]).astype(jnp.bfloat16)
    scores = jnp.dot(query_emb, passage_emb.T, preferred_element_type=jnp.float32) * inv_temp
    totals = jax.nn.logsumexp(scores, axis=1)
    match = positives[:, None] == jnp.arange(PAIRS, dtype=jnp.int32)[None, :]
    query_loss = totals - lax.optimization_barrier(jnp.sum(jnp.where(match, scores, 0.0), axis=1))
    pair_weights = (jnp.exp(scores - totals[:, None]) - match.astype(jnp.float32)).astype(jnp.bfloat16)
    query_grad = jnp.dot(pair_weights, passage_emb, preferred_element_type=jnp.float32) * inv_temp
    emb_grad = jnp.dot(pair_weights.T, query_emb, preferred_element_type=jnp.float32) * inv_temp
    emb_float = passage_emb.astype(jnp.float32)
    along = lax.optimization_barrier(jnp.sum(emb_float * emb_grad, axis=1))
    residual_grad = (emb_grad - emb_float * along[:, None]) / norm[:, None]
    slope = residual_grad.astype(jnp.bfloat16)
    attended_grad = jnp.dot(slope, out_weight.T, preferred_element_type=jnp.float32).astype(jnp.bfloat16)

    def backward_block(pieces):
        queries, key_block, value_block, length_row, upstream = pieces
        table, usable = slot_table(length_row)
        output, weights, probs, grouped, key_slots, value_slots = attend(queries, key_block, value_block, table, usable)
        return attend_back(upstream, weights, probs, grouped, key_slots, value_slots, table, TOK_DEV)
    lastq_grad, key_grad, value_grad = lax.map(backward_block, (query_blocks, key_blocks, value_blocks, lengths, attended_grad.reshape(N_DP, PDEV, -1)))
    return (query_loss, query_grad, residual_grad, lastq_grad.reshape(PAIRS, -1), key_grad.reshape(TOKENS, -1), value_grad.reshape(TOKENS, -1))
```

```python
import jax
import jax.numpy as jnp
from jax import lax
from jax.sharding import PartitionSpec as P

HEAD_DIM = 128

inv_temp = 50.0
epsilon = 1e-06


def row_mask(length_row, token_count, heads):
    ends = jnp.cumsum(length_row)
    starts = ends - length_row
    places = jnp.arange(token_count, dtype=jnp.int32)[None, None, :]
    mask = (places >= starts[:, None, None]) & (places < ends[:, None, None])
    rows = length_row.shape[0]
    return jnp.broadcast_to(mask, (rows, heads, token_count)).reshape(rows * heads, token_count)


def by_group(array, groups):
    rows = array.shape[0]
    split = array.reshape(rows, groups, -1, HEAD_DIM)
    return split.transpose(1, 0, 2, 3).reshape(groups, -1, HEAD_DIM)


def from_group(array, rows):
    groups = array.shape[0]
    return array.reshape(groups, rows, -1, HEAD_DIM).transpose(1, 0, 2, 3).reshape(rows, -1)


def on_device(
    last_query, key_cache, value_cache, residual, out_weight, query_emb, lengths, positives
):
    scale = 1.0 / HEAD_DIM**0.5
    token_count = key_cache.shape[0]
    rows = last_query.shape[0]
    groups = key_cache.shape[1] // HEAD_DIM
    heads = last_query.shape[1] // key_cache.shape[1]
    all_query = lax.all_gather(query_emb, "dp", axis=0, tiled=True)
    all_pos = lax.all_gather(positives, "dp", axis=0, tiled=True)
    mask = row_mask(lengths[0], token_count, heads)
    queries = by_group(last_query, groups)
    weights = []
    output = []
    for g in range(groups):
        key = key_cache[:, g * HEAD_DIM : (g + 1) * HEAD_DIM]
        value = value_cache[:, g * HEAD_DIM : (g + 1) * HEAD_DIM]
        scores = (
            lax.dot_general(
                queries[g], key, (((1,), (1,)), ((), ())), preferred_element_type=jnp.float32
            )
            * scale
        )
        weight = jax.nn.softmax(jnp.where(mask, scores, -1e30), axis=-1)
        weights.append(weight)
        output.append(
            jnp.dot(weight.astype(jnp.bfloat16), value, preferred_element_type=jnp.float32)
        )
    attended = from_group(jnp.stack(output), rows).astype(jnp.bfloat16)
    partial_value = jnp.dot(attended, out_weight, preferred_element_type=jnp.float32)
    hidden = lax.psum_scatter(
        partial_value, "mp", scatter_dimension=1, tiled=True
    ) + residual.astype(jnp.float32)
    squares = lax.psum(jnp.sum(hidden * hidden, axis=1), "mp")
    norm = jnp.sqrt(squares + epsilon)
    passage_emb = (hidden / norm[:, None]).astype(jnp.bfloat16)
    all_emb = lax.all_gather(passage_emb, "dp", axis=0, tiled=True)
    partial_t = lax.dot_general(
        passage_emb, all_query, (((1,), (1,)), ((), ())), preferred_element_type=jnp.float32
    )
    scores_t = lax.psum(partial_t, "mp") * inv_temp
    top = lax.pmax(jnp.max(scores_t, axis=0), "dp")
    totals = top + jnp.log(lax.psum(jnp.sum(jnp.exp(scores_t - top[None, :]), axis=0), "dp"))
    me = lax.axis_index("dp") * rows
    match_t = all_pos[None, :] == (me + jnp.arange(rows, dtype=jnp.int32))[:, None]
    pair_t = (jnp.exp(scores_t - totals[None, :]) - match_t.astype(jnp.float32)).astype(
        jnp.bfloat16
    )
    emb_grad = jnp.dot(pair_t, all_query, preferred_element_type=jnp.float32) * inv_temp
    along = jnp.sum(pair_t.astype(jnp.float32) * scores_t, axis=1)
    emb_float = passage_emb.astype(jnp.float32)
    residual_grad = (emb_grad - emb_float * along[:, None]) / norm[:, None]
    slope = residual_grad.astype(jnp.bfloat16)
    attended_grad = lax.dot_general(
        lax.all_gather(slope, "mp", axis=1, tiled=True),
        out_weight,
        (((1,), (1,)), ((), ())),
        preferred_element_type=jnp.float32,
    ).astype(jnp.bfloat16)
    upstream = by_group(attended_grad, groups)
    lastq, key_grad, value_grad = [], [], []
    for g in range(groups):
        key = key_cache[:, g * HEAD_DIM : (g + 1) * HEAD_DIM]
        value = value_cache[:, g * HEAD_DIM : (g + 1) * HEAD_DIM]
        weight = weights[g]
        slopes = lax.dot_general(
            upstream[g], value, (((1,), (1,)), ((), ())), preferred_element_type=jnp.float32
        )
        score_grad = weight * (slopes - jnp.sum(weight * slopes, axis=-1, keepdims=True))
        score_slope = score_grad.astype(jnp.bfloat16)
        lastq.append(jnp.dot(score_slope, key, preferred_element_type=jnp.float32) * scale)
        key_grad.append(
            lax.dot_general(
                score_slope, queries[g], (((0,), (0,)), ((), ())),
                preferred_element_type=jnp.float32,
            )
            * scale
        )
        value_grad.append(
            lax.dot_general(
                weight.astype(jnp.bfloat16), upstream[g], (((0,), (0,)), ((), ())),
                preferred_element_type=jnp.float32,
            )
        )
    lastq_grad = from_group(jnp.stack(lastq), rows)
    key_grad = jnp.concatenate(key_grad, axis=1).astype(jnp.bfloat16)
    value_grad = jnp.concatenate(value_grad, axis=1).astype(jnp.bfloat16)
    partial_scores = lax.dot_general(
        query_emb, all_emb, (((1,), (1,)), ((), ())), preferred_element_type=jnp.float32
    )
    scores = lax.psum(partial_scores, "mp") * inv_temp
    own_totals = lax.dynamic_slice(totals, (me,), (rows,))
    match = positives[:, None] == jnp.arange(scores.shape[1], dtype=jnp.int32)[None, :]
    query_loss = own_totals - jnp.sum(jnp.where(match, scores, 0.0), axis=1)
    pair_weights = (jnp.exp(scores - own_totals[:, None]) - match.astype(jnp.float32)).astype(
        jnp.bfloat16
    )
    query_grad = jnp.dot(pair_weights, all_emb, preferred_element_type=jnp.float32) * inv_temp
    return (query_loss, query_grad, residual_grad, lastq_grad, key_grad, value_grad)


def solution(mesh):
    in_specs = (
        P("dp", "mp"),
        P("dp", "mp"),
        P("dp", "mp"),
        P("dp", "mp"),
        P("mp", None),
        P("dp", "mp"),
        P("dp", None),
        P("dp"),
    )
    out_specs = (P("dp"), P("dp", "mp"), P("dp", "mp"), P("dp", "mp"), P("dp", "mp"), P("dp", "mp"))
    return jax.shard_map(
        on_device, mesh=mesh, in_specs=in_specs, out_specs=out_specs, check_vma=False
    )
```

```python
import functools

import jax
import jax.numpy as jnp
from jax import lax
from jax.experimental import pallas as pl
from jax.experimental.pallas import tpu as pltpu
from jax.sharding import PartitionSpec as P

HEAD_DIM = 128
INV_TEMP = 50.0
EPSILON = 1e-06
CORES = 2
PIECE = 16
MESH = pl.DeviceIdType.MESH
F32 = jnp.float32
BF16 = jnp.bfloat16


def dot_nn(a, b):
    return lax.dot_general(a, b, (((1,), (0,)), ((), ())), preferred_element_type=F32)


def dot_nt(a, b):
    return lax.dot_general(a, b, (((1,), (1,)), ((), ())), preferred_element_type=F32)


def dot_tn(a, b):
    return lax.dot_general(a, b, (((0,), (0,)), ((), ())), preferred_element_type=F32)


def drive(*steps):
    for step in steps:
        next(step, None)


def finish(step):
    for _ in step:
        pass


def kernel(
    sizes,
    lastq_ref, key_hbm, value_hbm, resid_ref, weight_hbm, query_ref, len_ref, pos_ref,
    loss_ref, qgrad_ref, rgrad_ref, lgrad_ref, kgrad_ref, vgrad_ref,
    q_all, p_all, weight, key, value, attn, probs, slopes,
    y_part, y_recv, sq_all, s_part, s_recv, stat_a, stat_b, w_all, c_all, slope_all,
    r_part, r_recv, rstat, wrow_all, load_sem, send_sem, recv_sem,
):
    nz, ny, nx = sizes
    rows, width = query_ref.shape
    tokens, kv_width = key_hbm.shape
    groups = kv_width // HEAD_DIM
    heads = width // kv_width
    cells = CORES * ny * nz
    chunk = s_part.shape[2]
    chunk_slots = chunk // PIECE
    scale = 1.0 / HEAD_DIM**0.5

    me = lax.axis_index("dp")
    x = lax.axis_index("mp")
    core = lax.rem(me, CORES)
    y = lax.rem(lax.div(me, CORES), ny)
    z = lax.div(me, CORES * ny)

    def place(z_at, y_at, core_at):
        return {"dp": (z_at * ny + y_at) * CORES + core_at}

    def around(at, step, size):
        return lax.rem(at + (step + size), size)

    xs = [around(x, k, nx) for k in range(nx)]
    plane = []
    for k in range(1, CORES * ny):
        inner = around(lax.rem(me, CORES * ny), k, CORES * ny)
        plane.append((inner, {"dp": z * (CORES * ny) + inner}))
    column = []
    for k in range(1, nz):
        other = around(z, k, nz)
        column.append((other, place(other, y, core)))

    loads = [
        pltpu.make_async_copy(key_hbm, key, load_sem.at[0]),
        pltpu.make_async_copy(value_hbm, value, load_sem.at[1]),
    ]
    for k in range(nx):
        columns = pl.ds(pl.multiple_of(xs[k] * width, width), width)
        loads.append(
            pltpu.make_async_copy(weight_hbm.at[:, columns], weight.at[k], load_sem.at[2 + k])
        )
    for load in loads:
        load.start()

    barrier = pltpu.get_barrier_semaphore()
    partners = [p for _, p in plane] + [p for _, p in column] + [{"mp": t} for t in xs[1:]]
    for partner in partners:
        pl.semaphore_signal(barrier, inc=1, device_id=partner, device_id_type=MESH)
    pl.semaphore_wait(barrier, len(partners))

    sent = []

    def push(src, dst, device):
        index = len(sent)
        copy = pltpu.make_async_remote_copy(
            src_ref=src,
            dst_ref=dst,
            send_sem=send_sem.at[index],
            recv_sem=recv_sem.at[index],
            device_id=device,
            device_id_type=MESH,
        )
        copy.start()
        sent.append(copy)
        return copy

    def ring(buf, size, at, neighbour, span, forward, shared):
        half = size // 2

        def chunk_of(j):
            start, count = span(j)
            return buf.at[pl.ds(start, count)]

        for k in range(1, half):
            behind, ahead = chunk_of(around(at, 1 - k, size)), chunk_of(around(at, k - 1, size))
            a = push(behind, behind, neighbour(around(at, 1, size)))
            b = push(ahead, ahead, neighbour(around(at, -1, size)))
            yield
            a.wait_recv()
            b.wait_recv()
            if shared is not None:
                shared(chunk_of(around(at, -k, size)))
                shared(chunk_of(around(at, k, size)))
        start, count = span(around(at, 1 - half, size))
        last = []
        if count > 1:
            part = buf.at[pl.ds(start, count // 2)]
            last.append(push(part, part, neighbour(around(at, 1, size))))
            start, count = span(around(at, half - 1, size))
            part = buf.at[pl.ds(start + count // 2, count // 2)]
            last.append(push(part, part, neighbour(around(at, -1, size))))
        elif forward:
            part = buf.at[pl.ds(start, 1)]
            last.append(push(part, part, neighbour(around(at, 1, size))))
        else:
            start, count = span(around(at, half - 1, size))
            part = buf.at[pl.ds(start, 1)]
            last.append(push(part, part, neighbour(around(at, -1, size))))
        yield
        for copy in last:
            copy.wait_recv()
        if shared is not None:
            shared(chunk_of(around(at, half, size)))

    def gather(buf, z_first):
        pending = []

        def share(part):
            pending.append(push(part, part, place(z, y, 1 - core)))

        def z_side(j):
            return place(j, y, core)

        def y_side(j):
            return place(z, j, core)

        if z_first:
            yield from ring(
                buf, nz, z, z_side, lambda j: ((core * ny + y) * nz + j, 1), True, None
            )
            share(buf.at[pl.ds((core * ny + y) * nz, nz)])
            yield from ring(
                buf, ny, y, y_side, lambda j: ((core * ny + j) * nz, nz), True, share
            )
        else:
            yield from ring(
                buf, ny, y, y_side, lambda j: (cells + (core * nz + z) * ny + j, 1), False, None
            )
            share(buf.at[pl.ds(cells + (core * nz + z) * ny, ny)])
            yield from ring(
                buf, nz, z, z_side, lambda j: (cells + (core * nz + j) * ny, ny), False, share
            )
        yield
        for copy in pending:
            copy.wait_recv()

    slot_a = (core * ny + y) * nz + z
    slot_b = cells + (core * nz + z) * ny + y

    def exchange(src, dst):
        copies = [None] * nx
        for k in [nx // 2] + [k for k in range(1, nx) if k != nx // 2]:
            copies[k] = push(src(k), dst.at[x], {"mp": xs[k]})
        return copies

    def received(copies, k):
        copies[k].wait_recv()
        return xs[nx - k]

    lane = lax.broadcasted_iota(jnp.int32, (rows, HEAD_DIM), 1)
    position = pos_ref[...]
    high, low = lax.shift_right_logical(position, 6), position & 63
    digits = jnp.where(lane == 0, high, jnp.where(lane == 1, low, 0)).astype(F32).astype(BF16)
    q_all[slot_a, :, :width] = query_ref[:PIECE, :]
    q_all[slot_b, :, :width] = query_ref[PIECE:, :]
    q_all[slot_a, :, width:] = digits[:PIECE]
    q_all[slot_b, :, width:] = digits[PIECE:]
    q_steps = [gather(q_all, False), gather(q_all, True)]
    drive(*q_steps)

    block = 16
    lengths = len_ref[...].astype(F32)

    def grouped(source, g):
        first = g * heads
        return jnp.concatenate(
            [
                source[:, (first + h) * HEAD_DIM : (first + h + 1) * HEAD_DIM]
                for h in range(heads)
            ],
            axis=0,
        )

    def softmax_rows(g):
        def body(i, carry):
            at = pl.ds(pl.multiple_of(i * block, block), block)
            passage = (lax.broadcasted_iota(jnp.int32, (block, rows), 0) + i * block) & (rows - 1)
            which = lax.broadcasted_iota(jnp.int32, (block, rows), 1)
            ends = jnp.sum(jnp.where(which <= passage, lengths, 0.0), axis=1, keepdims=True)
            starts = jnp.sum(jnp.where(which < passage, lengths, 0.0), axis=1, keepdims=True)
            token = lax.broadcasted_iota(jnp.int32, (block, tokens), 1)
            inside = (token >= starts.astype(jnp.int32)) & (token < ends.astype(jnp.int32))
            scores = jnp.where(inside, attn[g, at, :] * scale, -1e30)
            top = jnp.max(scores, axis=1, keepdims=True)
            powers = jnp.exp(scores - top)
            weights = powers / jnp.sum(powers, axis=1, keepdims=True)
            attn[g, at, :] = weights
            probs[g, at, :] = weights.astype(BF16)
            return carry

        lax.fori_loop(0, heads * rows // block, body, 0)

    loads[0].wait()
    loads[1].wait()
    attended = []
    for g in range(groups):
        side = slice(g * HEAD_DIM, (g + 1) * HEAD_DIM)
        attn[g] = dot_nt(grouped(lastq_ref, g), key[:, side])
        softmax_rows(g)
        out = dot_nn(probs[g], value[:, side]).astype(BF16)
        attended += [out[h * rows : (h + 1) * rows] for h in range(heads)]
        drive(*q_steps)
    attended = jnp.concatenate(attended, axis=1)

    def project(k):
        loads[2 + k].wait()
        y_part[k] = dot_nn(attended, weight[k]).astype(BF16)
        return y_part.at[k]

    y_copies = exchange(project, y_recv)
    loads[2].wait()
    hidden = dot_nn(attended, weight[0]) + resid_ref[...].astype(F32)
    drive(*q_steps)
    for k in range(1, nx):
        hidden = hidden + y_recv[received(y_copies, k)].astype(F32)
    sq_all[x] = jnp.broadcast_to(jnp.sum(hidden * hidden, axis=1, keepdims=True), (rows, HEAD_DIM))
    sq_copies = exchange(lambda k: sq_all.at[x], sq_all)
    hidden_16 = hidden.astype(BF16)
    for step in q_steps:
        finish(step)

    def chunk_rows(buf, t):
        return buf[pl.ds(t * chunk_slots, chunk_slots), :, :width].reshape(chunk, width)

    def partial_scores(k):
        s_part[k] = dot_nt(hidden_16, chunk_rows(q_all, xs[k]))
        return s_part.at[k]

    s_copies = exchange(partial_scores, s_recv)
    squares = sq_all[x]
    for k in range(1, nx):
        squares = squares + sq_all[received(sq_copies, k)]
    norm = jnp.sqrt(squares[:, :1] + EPSILON)
    emb = hidden / norm
    emb_16 = emb.astype(BF16)
    p_all[slot_a] = emb_16[:PIECE]
    p_all[slot_b] = emb_16[PIECE:]
    p_steps = [gather(p_all, False), gather(p_all, True)]
    drive(*p_steps)
    scores = dot_nt(hidden_16, chunk_rows(q_all, x))
    own_digits = q_all[pl.ds(x * chunk_slots, chunk_slots), :, width:].reshape(chunk, HEAD_DIM)
    unit = jnp.where(lane == 0, 64, jnp.where(lane == 1, 1, 0)).astype(F32).astype(BF16)
    positive = dot_nt(unit, own_digits)
    for k in range(1, nx):
        scores = scores + s_recv[received(s_copies, k)]
    scores = scores * (INV_TEMP / norm)

    lines = chunk // HEAD_DIM

    def fold(row):
        return [row[:, i * HEAD_DIM : (i + 1) * HEAD_DIM] for i in range(lines)]

    top = jnp.max(scores, axis=0, keepdims=True)
    total = jnp.sum(jnp.exp(scores - top), axis=0, keepdims=True)
    pair = jnp.concatenate(fold(top) + fold(total), axis=0)

    def merge(buf, own, at, others):
        buf[at] = own
        copies = [push(buf.at[at], buf.at[at], device) for _, device in others]
        drive(*p_steps)
        for copy in copies:
            copy.wait_recv()
        every = buf[...]
        high = jnp.max(every[:, :lines], axis=0)
        mass = jnp.sum(every[:, lines:] * jnp.exp(every[:, :lines] - high[None]), axis=0)
        return jnp.concatenate([high, mass], axis=0)

    pair = merge(stat_a, pair, lax.rem(me, CORES * ny), plane)
    pair = merge(stat_b, pair, z, column)
    lse = pair[:lines] + jnp.log(pair[lines:])
    lse = jnp.concatenate([lse[i : i + 1] for i in range(lines)], axis=1)

    own_passage = lax.broadcasted_iota(jnp.int32, (rows, chunk), 0) + me * rows
    match = (positive == own_passage.astype(F32)).astype(F32)
    pair_weights = (jnp.exp(scores - lse) - match).astype(BF16)
    w_all[x] = pair_weights
    w_copies = exchange(lambda k: w_all.at[x], w_all)
    along = jnp.sum(pair_weights.astype(F32) * scores, axis=1, keepdims=True)
    c_all[x] = jnp.broadcast_to(along, (rows, HEAD_DIM))
    c_copies = exchange(lambda k: c_all.at[x], c_all)
    emb_grad = dot_nn(pair_weights, chunk_rows(q_all, x))
    drive(*p_steps)
    for k in range(1, nx):
        t = received(w_copies, k)
        emb_grad = emb_grad + dot_nn(w_all[t], chunk_rows(q_all, t))
    along = c_all[x]
    for k in range(1, nx):
        along = along + c_all[received(c_copies, k)]
    residual_grad = (emb_grad * INV_TEMP - emb * along[:, :1]) / norm
    rgrad_ref[...] = residual_grad
    slope = residual_grad.astype(BF16)
    slope_all[x] = slope
    slope_copies = exchange(lambda k: slope_all.at[x], slope_all)
    upstream = dot_nt(slope, weight[0])
    drive(*p_steps)
    for k in range(1, nx):
        t = received(slope_copies, k)
        upstream = upstream + dot_nt(slope_all[t], weight[nx - k])
    upstream = upstream.astype(BF16)
    drive(*p_steps)

    def slope_rows(g):
        def body(i, carry):
            at = pl.ds(pl.multiple_of(i * block, block), block)
            weights = attn[g, at, :]
            slope_at = slopes[at, :]
            mean = jnp.sum(weights * slope_at, axis=1, keepdims=True)
            probs[groups, at, :] = (weights * (slope_at - mean)).astype(BF16)
            return carry

        lax.fori_loop(0, heads * rows // block, body, 0)

    def backward(g):
        side = slice(g * HEAD_DIM, (g + 1) * HEAD_DIM)
        up = grouped(upstream, g)
        slopes[...] = dot_nt(up, value[:, side])
        vgrad_ref[:, side] = dot_tn(probs[g], up).astype(BF16)
        slope_rows(g)
        score_slope = probs[groups]
        queries = grouped(lastq_ref, g)
        lastq = dot_nn(score_slope, key[:, side]) * scale
        for h in range(heads):
            first = (g * heads + h) * HEAD_DIM
            lgrad_ref[:, first : first + HEAD_DIM] = lastq[h * rows : (h + 1) * rows]
        kgrad_ref[:, side] = (dot_tn(score_slope, queries) * scale).astype(BF16)

    backward(0)
    for step in p_steps:
        finish(step)

    def partial_rows(k):
        r_part[k] = dot_nt(query_ref[...], chunk_rows(p_all, xs[k]))
        return r_part.at[k]

    r_copies = exchange(partial_rows, r_recv)
    row_scores = dot_nt(query_ref[...], chunk_rows(p_all, x))
    for g in range(1, groups):
        backward(g)
    for k in range(1, nx):
        row_scores = row_scores + r_recv[received(r_copies, k)]
    row_scores = row_scores * INV_TEMP
    index = lax.broadcasted_iota(jnp.int32, (rows, chunk), 1) + x * chunk
    second = index >= cells * PIECE
    slot = lax.shift_right_logical(index & (cells * PIECE - 1), 4)
    inner = slot & (ny * nz - 1)
    core_at = lax.div(slot, ny * nz)
    z_at = jnp.where(second, lax.div(inner, ny), inner & (nz - 1))
    y_at = jnp.where(second, inner & (ny - 1), lax.div(inner, nz))
    passage = ((z_at * ny + y_at) * CORES + core_at) * rows
    passage = passage + jnp.where(second, PIECE, 0) + (index & (PIECE - 1))
    row_match = passage == position
    top = jnp.max(row_scores, axis=1, keepdims=True)
    total = jnp.sum(jnp.exp(row_scores - top), axis=1, keepdims=True)
    hit = jnp.sum(jnp.where(row_match, row_scores, 0.0), axis=1, keepdims=True)
    rstat[x] = jnp.where(lane == 0, top, jnp.where(lane == 1, total, hit))
    rs_copies = exchange(lambda k: rstat.at[x], rstat)
    for k in range(1, nx):
        received(rs_copies, k)
    every = rstat[...]
    tops = every[:, :, 0:1]
    top = jnp.max(tops, axis=0)
    total = jnp.sum(every[:, :, 1:2] * jnp.exp(tops - top[None]), axis=0)
    row_lse = top + jnp.log(total)
    loss_ref[...] = row_lse - jnp.sum(every[:, :, 2:3], axis=0)
    row_weights = (jnp.exp(row_scores - row_lse) - row_match.astype(F32)).astype(BF16)
    wrow_all[x] = row_weights
    wr_copies = exchange(lambda k: wrow_all.at[x], wrow_all)
    query_grad = dot_nn(row_weights, chunk_rows(p_all, x))
    for k in range(1, nx):
        t = received(wr_copies, k)
        query_grad = query_grad + dot_nn(wrow_all[t], chunk_rows(p_all, t))
    qgrad_ref[...] = query_grad * INV_TEMP

    for copy in sent:
        copy.wait_send()


def on_device(
    sizes, last_query, key_cache, value_cache, residual, out_weight, query_emb, lengths, positives
):
    nz, ny, nx = sizes
    rows, width = query_emb.shape
    tokens, kv_width = key_cache.shape
    groups = kv_width // HEAD_DIM
    heads = width // kv_width
    cells = CORES * ny * nz
    chunk = cells * rows // nx
    lines = chunk // HEAD_DIM
    vmem = pl.BlockSpec(memory_space=pltpu.VMEM)
    hbm = pl.BlockSpec(memory_space=pl.ANY)
    copies = 160
    outs = pl.pallas_call(
        functools.partial(kernel, sizes),
        out_shape=(
            jax.ShapeDtypeStruct((rows, 1), F32),
            jax.ShapeDtypeStruct((rows, width), F32),
            jax.ShapeDtypeStruct((rows, width), F32),
            jax.ShapeDtypeStruct((rows, width), F32),
            jax.ShapeDtypeStruct((tokens, kv_width), BF16),
            jax.ShapeDtypeStruct((tokens, kv_width), BF16),
        ),
        in_specs=[vmem, hbm, hbm, vmem, hbm, vmem, vmem, vmem],
        out_specs=(vmem,) * 6,
        scratch_shapes=[
            pltpu.VMEM((2 * cells, PIECE, width + HEAD_DIM), BF16),
            pltpu.VMEM((2 * cells, PIECE, width), BF16),
            pltpu.VMEM((nx, width, width), BF16),
            pltpu.VMEM((tokens, kv_width), BF16),
            pltpu.VMEM((tokens, kv_width), BF16),
            pltpu.VMEM((groups, heads * rows, tokens), F32),
            pltpu.VMEM((groups + 1, heads * rows, tokens), BF16),
            pltpu.VMEM((heads * rows, tokens), F32),
            pltpu.VMEM((nx, rows, width), BF16),
            pltpu.VMEM((nx, rows, width), BF16),
            pltpu.VMEM((nx, rows, HEAD_DIM), F32),
            pltpu.VMEM((nx, rows, chunk), F32),
            pltpu.VMEM((nx, rows, chunk), F32),
            pltpu.VMEM((CORES * ny, 2 * lines, HEAD_DIM), F32),
            pltpu.VMEM((nz, 2 * lines, HEAD_DIM), F32),
            pltpu.VMEM((nx, rows, chunk), BF16),
            pltpu.VMEM((nx, rows, HEAD_DIM), F32),
            pltpu.VMEM((nx, rows, width), BF16),
            pltpu.VMEM((nx, rows, chunk), F32),
            pltpu.VMEM((nx, rows, chunk), F32),
            pltpu.VMEM((nx, rows, HEAD_DIM), F32),
            pltpu.VMEM((nx, rows, chunk), BF16),
            pltpu.SemaphoreType.DMA((2 + nx,)),
            pltpu.SemaphoreType.DMA((copies,)),
            pltpu.SemaphoreType.DMA((copies,)),
        ],
        compiler_params=pltpu.CompilerParams(
            collective_id=0, has_side_effects=True, vmem_limit_bytes=56 * 2**20
        ),
    )(
        last_query, key_cache, value_cache, residual, out_weight, query_emb,
        lengths, positives.reshape(rows, 1),
    )
    return (outs[0].reshape(rows),) + tuple(outs[1:])


def solution(mesh, nz=8, ny=4):
    in_specs = (
        P("dp", "mp"),
        P("dp", "mp"),
        P("dp", "mp"),
        P("dp", "mp"),
        P("mp", None),
        P("dp", "mp"),
        P("dp", None),
        P("dp"),
    )
    out_specs = (P("dp"), P("dp", "mp"), P("dp", "mp"), P("dp", "mp"), P("dp", "mp"), P("dp", "mp"))
    sizes = (nz, ny, mesh.shape["mp"])
    return jax.shard_map(
        functools.partial(on_device, sizes),
        mesh=mesh,
        in_specs=in_specs,
        out_specs=out_specs,
        check_vma=False,
    )
```

```python
import functools

import jax
import jax.numpy as jnp
from jax import lax
from jax.experimental import pallas as pl
from jax.experimental.pallas import tpu as pltpu
from jax.sharding import PartitionSpec as P

HEAD_DIM = 128
INV_TEMP = 50.0
EPSILON = 1e-06
CORES = 2
MESH = pl.DeviceIdType.MESH
F32 = jnp.float32
BF16 = jnp.bfloat16


def dot_nn(a, b):
    return lax.dot_general(a, b, (((1,), (0,)), ((), ())), preferred_element_type=F32)


def dot_nt(a, b):
    return lax.dot_general(a, b, (((1,), (1,)), ((), ())), preferred_element_type=F32)


def dot_tn(a, b):
    return lax.dot_general(a, b, (((0,), (0,)), ((), ())), preferred_element_type=F32)


def kernel(
    sizes,
    lastq_ref, key_hbm, value_hbm, resid_ref, weight_hbm, query_ref, len_ref, pos_ref,
    loss_ref, qgrad_ref, rgrad_ref, up_ref, attn_hbm,
    q_buf, p_buf, weight, key, value, attn, probs, y_part, y_recv, s_part, s_recv, sq_all, turned,
    stat, w_all, misc_all, eg_part, eg_own, eg_side, eg_out, eg_recv, slope_all, qg_part, qg_recv,
    load_sem, send_sem, recv_sem,
):
    nz, ny, nx = sizes
    rows, width = query_ref.shape
    tokens, kv_width = key_hbm.shape
    groups = kv_width // HEAD_DIM
    heads = width // kv_width
    inner = CORES * ny
    passages = inner * rows
    slots = nz // nx
    chunk = slots * rows
    scale = 1.0 / HEAD_DIM**0.5

    me = lax.axis_index("dp")
    x = lax.axis_index("mp")
    core = lax.rem(me, CORES)
    y = lax.rem(lax.div(me, CORES), ny)
    z = lax.div(me, inner)

    def place(z_at, y_at, core_at):
        return {"dp": (z_at * ny + y_at) * CORES + core_at}

    def around(at, step, size):
        return lax.rem(at + (step + size), size)

    def far_first(size):
        return sorted(range(1, size), key=lambda k: -min(k, size - k))

    xs = [around(x, k, nx) for k in range(nx)]
    ys = [around(y, k, ny) for k in range(ny)]
    zs = [around(z, k, nz) for k in range(nz)]
    twin = place(z, y, 1 - core)
    partners = [place(t, y, core) for t in zs[1:]] + [place(z, t, core) for t in ys[1:]]
    partners += [twin] + [{"mp": t} for t in xs[1:]]

    barrier = pltpu.get_barrier_semaphore()
    for partner in partners:
        pl.semaphore_signal(barrier, inc=1, device_id=partner, device_id_type=MESH)

    loads = [
        pltpu.make_async_copy(key_hbm, key, load_sem.at[0]),
        pltpu.make_async_copy(value_hbm, value, load_sem.at[1]),
    ]
    for k in far_first(nx) + [0]:
        columns = pl.ds(pl.multiple_of(xs[k] * width, width), width)
        loads.append(
            pltpu.make_async_copy(weight_hbm.at[:, columns], weight.at[k], load_sem.at[2 + k])
        )
    for load in loads:
        load.start()

    sent = []

    def push(src, dst, device):
        index = len(sent)
        copy = pltpu.make_async_remote_copy(
            src_ref=src,
            dst_ref=dst,
            send_sem=send_sem.at[index],
            recv_sem=recv_sem.at[index],
            device_id=device,
            device_id_type=MESH,
        )
        copy.start()
        sent.append(copy)
        return copy

    def exchange(src, dst):
        copies = [None] * nx
        for k in far_first(nx):
            copies[k] = push(src(k), dst.at[x], {"mp": xs[k]})
        return copies

    def received(copies, k):
        copies[k].wait_recv()
        return xs[nx - k]

    lane = lax.broadcasted_iota(jnp.int32, (rows, HEAD_DIM), 1)

    def three_parts(column):
        high = column.astype(BF16).astype(F32)
        middle = (column - high).astype(BF16).astype(F32)
        low = column - high - middle
        parts = jnp.where(lane == 0, high, jnp.where(lane == 1, middle, low))
        return jnp.where(lane < 3, parts, 0.0).astype(BF16)

    position = jnp.broadcast_to(pos_ref[...].astype(F32), (rows, rows))
    diagonal = lax.broadcasted_iota(jnp.int32, (rows, rows), 0) == lax.broadcasted_iota(
        jnp.int32, (rows, rows), 1
    )
    position = jnp.sum(jnp.where(diagonal, position, 0.0), axis=1, keepdims=True).astype(jnp.int32)
    high, low = lax.shift_right_logical(position, 6), position & 63
    digits = jnp.where(lane == 0, high, jnp.where(lane == 1, low, 0)).astype(F32).astype(BF16)
    q_buf[z, :, :width] = query_ref[...]
    q_buf[z, :, width:] = digits
    pl.semaphore_wait(barrier, len(partners))
    q_copies = [push(q_buf.at[z], q_buf.at[z], place(zs[k], y, core)) for k in far_first(nz)]

    block = 16
    lengths = len_ref[...].astype(F32)

    def softmax_rows(g):
        def body(i, carry):
            at = pl.ds(pl.multiple_of(i * block, block), block)
            passage = (lax.broadcasted_iota(jnp.int32, (block, rows), 0) + i * block) & (rows - 1)
            which = lax.broadcasted_iota(jnp.int32, (block, rows), 1)
            ends = jnp.sum(jnp.where(which <= passage, lengths, 0.0), axis=1, keepdims=True)
            starts = jnp.sum(jnp.where(which < passage, lengths, 0.0), axis=1, keepdims=True)
            token = lax.broadcasted_iota(jnp.int32, (block, tokens), 1)
            inside = (token >= starts.astype(jnp.int32)) & (token < ends.astype(jnp.int32))
            scores = jnp.where(inside, attn[g, at, :], -1e30)
            top = jnp.max(scores, axis=1, keepdims=True)
            powers = jnp.exp((scores - top) * scale)
            weights = powers * (1.0 / jnp.sum(powers, axis=1, keepdims=True))
            attn[g, at, :] = weights
            probs[at, :] = weights.astype(BF16)
            return carry

        lax.fori_loop(0, heads * rows // block, body, 0)

    loads[0].wait()
    loads[1].wait()
    attended = []
    saves = []
    for g in range(groups):
        side = slice(g * HEAD_DIM, (g + 1) * HEAD_DIM)
        attn[g] = dot_nt(grouped(lastq_ref, g, heads), key[:, side])
        softmax_rows(g)
        saves.append(pltpu.make_async_copy(attn.at[g], attn_hbm.at[g], load_sem.at[2 + nx + g]))
        saves[-1].start()
        out = dot_nn(probs[...], value[:, side]).astype(BF16)
        attended += [out[h * rows : (h + 1) * rows] for h in range(heads)]
    attended = jnp.concatenate(attended, axis=1)

    for load in loads[2:]:
        load.wait()

    def project(k):
        y_part[k] = dot_nn(attended, weight[k]).astype(BF16)
        return y_part.at[k]

    y_copies = exchange(project, y_recv)
    hidden = dot_nn(attended, weight[0]) + resid_ref[...].astype(F32)
    for k in range(1, nx):
        hidden = hidden + y_recv[received(y_copies, k)].astype(F32)

    own = core * ny + y
    p_buf[own, :, :width] = hidden.astype(BF16)
    p_buf[own, :, width:] = three_parts(jnp.sum(hidden * hidden, axis=1, keepdims=True))
    p_copies = [None] * ny
    for k in far_first(ny):
        p_copies[k] = push(p_buf.at[own], p_buf.at[own], place(z, ys[k], core))
    passed = [push(p_buf.at[own], p_buf.at[own], twin)]
    for k in sorted(range(1, ny), key=lambda k: min(k, ny - k)):
        p_copies[k].wait_recv()
        part = p_buf.at[core * ny + ys[ny - k]]
        passed.append(push(part, part, twin))
    for copy in q_copies + passed:
        copy.wait_recv()

    all_passages = p_buf[:, :, :width].reshape(passages, width)

    def partial_scores(t):
        part = q_buf[pl.ds(t * slots, slots), :, :width].reshape(chunk, width)
        return dot_nt(part, all_passages)

    def send_scores(k):
        s_part[k] = partial_scores(xs[k])
        return s_part.at[k]

    unit = (lax.broadcasted_iota(jnp.int32, (8, HEAD_DIM), 1) < 3).astype(F32).astype(BF16)
    sq_all[x] = dot_nt(unit, p_buf[:, :, width:].reshape(passages, HEAD_DIM))
    sq_copies = exchange(lambda k: sq_all.at[x], sq_all)
    s_copies = exchange(send_scores, s_recv)
    scores = partial_scores(x)
    squares = sq_all[x]
    for k in range(1, nx):
        squares = squares + sq_all[received(sq_copies, k)]
    norms = jnp.sqrt(squares[:1] + EPSILON)
    turned[...] = jnp.broadcast_to(norms, (HEAD_DIM, passages)).T
    norm = turned[pl.ds(pl.multiple_of(own * rows, rows), rows), :][:, :1]
    emb = hidden / norm
    digits = q_buf[pl.ds(x * slots, slots), :, width:].reshape(chunk, HEAD_DIM).astype(F32)
    positive = (digits[:, 0:1] * 64.0 + digits[:, 1:2]).astype(jnp.int32)
    index = lax.broadcasted_iota(jnp.int32, (chunk, passages), 1)
    slot = lax.div(index, rows)
    cell = lax.rem(slot, ny) * CORES + lax.div(slot, ny)
    match = positive == (z * inner + cell) * rows + lax.rem(index, rows)
    for k in range(1, nx):
        scores = scores + s_recv[received(s_copies, k)]
    scores = scores * (INV_TEMP / norms)

    top = jnp.max(scores, axis=1, keepdims=True)
    total = jnp.sum(jnp.exp(scores - top), axis=1, keepdims=True)
    hit = jnp.sum(jnp.where(match, scores, 0.0), axis=1, keepdims=True)
    chunk_lane = lax.broadcasted_iota(jnp.int32, (chunk, HEAD_DIM), 1)
    columns = jnp.where(chunk_lane == 0, top, jnp.where(chunk_lane == 1, total, hit))
    stat[z] = jnp.concatenate([columns] * (HEAD_DIM // chunk), axis=0).T[:8]
    stat_copies = [push(stat.at[z], stat.at[z], place(zs[k], y, core)) for k in far_first(nz)]
    for copy in stat_copies:
        copy.wait_recv()
    every = stat[...]
    top = jnp.max(every[:, 0:1], axis=0)
    total = jnp.sum(every[:, 1:2] * jnp.exp(every[:, 0:1] - top[None]), axis=0)
    lse = top + jnp.log(total)
    loss = lse - jnp.sum(every[:, 2:3], axis=0)
    lse = jnp.broadcast_to(lse, (HEAD_DIM, HEAD_DIM)).T[:chunk, :1]

    pairs = (jnp.exp(scores - lse) - match.astype(F32)).astype(BF16)
    w_all[x] = pairs
    w_copies = exchange(lambda k: w_all.at[x], w_all)
    along = jnp.sum(pairs.astype(F32) * scores, axis=0, keepdims=True)
    line = lax.broadcasted_iota(jnp.int32, (8, passages), 0)
    losses = jnp.concatenate([loss] * (passages // HEAD_DIM), axis=1)
    misc_all[x] = jnp.where(line == 0, along, losses)
    misc_copies = exchange(lambda k: misc_all.at[x], misc_all)
    for k in range(1, nx):
        received(w_copies, k)
        received(misc_copies, k)
    losses = misc_all[lax.div(z, slots)][1:2]
    own_loss = losses[:, :rows]
    for k in range(1, slots):
        own_loss = jnp.where(lax.rem(z, slots) == k, losses[:, k * rows : (k + 1) * rows], own_loss)
    loss_ref[...] = own_loss
    along = misc_all[0][:1]
    for k in range(1, nx):
        along = along + misc_all[k][:1]
    turned[...] = jnp.broadcast_to(along, (HEAD_DIM, passages)).T

    share = ny * rows

    def emb_share(core_at):
        part = w_all[:, :, pl.ds(pl.multiple_of(core_at * share, share), share)]
        part = part.reshape(nx * chunk, share)
        return dot_tn(part, q_buf[:, :, :width].reshape(nz * rows, width)) * INV_TEMP

    def along_of(core_at, y_at):
        first = pl.multiple_of((core_at * ny + y_at) * rows, rows)
        return turned[pl.ds(first, rows), :][:, :1]

    grads = emb_share(1 - core).reshape(ny, rows, width)
    eg_part[:, :, :width] = grads.astype(BF16)
    for j in range(ny):
        eg_part[j, :, width:] = three_parts(along_of(1 - core, j))
    side_copy = push(eg_part, eg_side, twin)
    eg_own[...] = emb_share(core).reshape(ny, rows, width)

    pairs = w_all[...].reshape(nx * chunk, passages).astype(F32) * (INV_TEMP / norms)
    grads = dot_nn(pairs.astype(BF16), all_passages)
    qg_part[...] = grads.astype(BF16).reshape(nz, rows, width)
    qg_copies = [
        push(qg_part.at[zs[k]], qg_recv.at[z], place(zs[k], y, core)) for k in far_first(nz)
    ]
    side_copy.wait_recv()

    def emb_sum(y_at):
        side = eg_side[y_at]
        parts = side[:, width:].astype(F32)
        total = eg_own[y_at] + side[:, :width].astype(F32)
        return total, along_of(core, y_at) + (parts[:, 0:1] + parts[:, 1:2] + parts[:, 2:3])

    eg_copies = [None] * ny
    for k in far_first(ny):
        total, along = emb_sum(ys[k])
        eg_out[k, :, :width] = total.astype(BF16)
        eg_out[k, :, width:] = three_parts(along)
        eg_copies[k] = push(eg_out.at[k], eg_recv.at[y], place(z, ys[k], core))
    emb_grad, along = emb_sum(y)
    for k in range(1, ny):
        eg_copies[k].wait_recv()
        side = eg_recv[ys[ny - k]]
        parts = side[:, width:].astype(F32)
        emb_grad = emb_grad + side[:, :width].astype(F32)
        along = along + (parts[:, 0:1] + parts[:, 1:2] + parts[:, 2:3])
    residual_grad = (emb_grad - emb * along) / norm
    rgrad_ref[...] = residual_grad

    slope = residual_grad.astype(BF16)
    slope_all[x] = slope
    slope_copies = exchange(lambda k: slope_all.at[x], slope_all)
    upstream = dot_nt(slope, weight[0])
    for k in range(1, nx):
        t = received(slope_copies, k)
        upstream = upstream + dot_nt(slope_all[t], weight[nx - k])
    up_ref[...] = upstream.astype(BF16)

    query_grad = qg_part[z].astype(F32)
    for copy in qg_copies:
        copy.wait_recv()
    for k in range(1, nz):
        query_grad = query_grad + qg_recv[zs[k]].astype(F32)
    qgrad_ref[...] = query_grad
    for save in saves:
        save.wait()
    for copy in sent:
        copy.wait_send()


def grouped(source, g, heads):
    first = g * heads
    return jnp.concatenate(
        [source[:, (first + h) * HEAD_DIM : (first + h + 1) * HEAD_DIM] for h in range(heads)],
        axis=0,
    )


def backward(
    lastq_ref, up_ref, key_ref, value_ref, attn_ref, loss_in, qgrad_in, rgrad_in,
    loss_ref, qgrad_ref, rgrad_ref, lgrad_ref, kgrad_ref, vgrad_ref, slopes, probs, score_slope,
):
    loss_ref[...] = loss_in[...]
    qgrad_ref[...] = qgrad_in[...]
    rgrad_ref[...] = rgrad_in[...]
    rows = lastq_ref.shape[0]
    heads = lastq_ref.shape[1] // HEAD_DIM
    scale = 1.0 / HEAD_DIM**0.5
    block = 16
    up = grouped(up_ref, 0, heads)
    slopes[...] = dot_nt(up, value_ref[...])

    def body(i, carry):
        at = pl.ds(pl.multiple_of(i * block, block), block)
        weights = attn_ref[0, at, :]
        slope_at = slopes[at, :]
        mean = jnp.sum(weights * slope_at, axis=1, keepdims=True)
        score_slope[at, :] = (weights * (slope_at - mean)).astype(BF16)
        probs[at, :] = weights.astype(BF16)
        return carry

    lax.fori_loop(0, heads * rows // block, body, 0)
    vgrad_ref[...] = dot_tn(probs[...], up).astype(BF16)
    lastq = dot_nn(score_slope[...], key_ref[...]) * scale
    for h in range(heads):
        lgrad_ref[:, h * HEAD_DIM : (h + 1) * HEAD_DIM] = lastq[h * rows : (h + 1) * rows]
    queries = grouped(lastq_ref, 0, heads)
    kgrad_ref[...] = (dot_tn(score_slope[...], queries) * scale).astype(BF16)


def on_device(
    sizes, last_query, key_cache, value_cache, residual, out_weight, query_emb, lengths, positives
):
    nz, ny, nx = sizes
    rows, width = query_emb.shape
    tokens, kv_width = key_cache.shape
    groups = kv_width // HEAD_DIM
    heads = width // kv_width
    inner = CORES * ny
    passages = inner * rows
    chunk = nz // nx * rows
    wide = width + HEAD_DIM
    vmem = pl.BlockSpec(memory_space=pltpu.VMEM)
    hbm = pl.BlockSpec(memory_space=pl.ANY)
    copies = 3 * (nz - 1) + 3 * ny + 7 * (nx - 1)
    loss, query_grad, residual_grad, upstream, attn = pl.pallas_call(
        functools.partial(kernel, sizes),
        out_shape=(
            jax.ShapeDtypeStruct((1, rows), F32),
            jax.ShapeDtypeStruct((rows, width), F32),
            jax.ShapeDtypeStruct((rows, width), F32),
            jax.ShapeDtypeStruct((rows, width), BF16),
            jax.ShapeDtypeStruct((groups, heads * rows, tokens), F32),
        ),
        in_specs=[vmem, hbm, hbm, vmem, hbm, vmem, vmem, vmem],
        out_specs=(vmem, vmem, vmem, vmem, hbm),
        scratch_shapes=[
            pltpu.VMEM((nz, rows, wide), BF16),
            pltpu.VMEM((inner, rows, wide), BF16),
            pltpu.VMEM((nx, width, width), BF16),
            pltpu.VMEM((tokens, kv_width), BF16),
            pltpu.VMEM((tokens, kv_width), BF16),
            pltpu.VMEM((groups, heads * rows, tokens), F32),
            pltpu.VMEM((heads * rows, tokens), BF16),
            pltpu.VMEM((nx, rows, width), BF16),
            pltpu.VMEM((nx, rows, width), BF16),
            pltpu.VMEM((nx, chunk, passages), F32),
            pltpu.VMEM((nx, chunk, passages), F32),
            pltpu.VMEM((nx, 8, passages), F32),
            pltpu.VMEM((passages, HEAD_DIM), F32),
            pltpu.VMEM((nz, 8, HEAD_DIM), F32),
            pltpu.VMEM((nx, chunk, passages), BF16),
            pltpu.VMEM((nx, 8, passages), F32),
            pltpu.VMEM((ny, rows, wide), BF16),
            pltpu.VMEM((ny, rows, width), F32),
            pltpu.VMEM((ny, rows, wide), BF16),
            pltpu.VMEM((ny, rows, wide), BF16),
            pltpu.VMEM((ny, rows, wide), BF16),
            pltpu.VMEM((nx, rows, width), BF16),
            pltpu.VMEM((nz, rows, width), BF16),
            pltpu.VMEM((nz, rows, width), BF16),
            pltpu.SemaphoreType.DMA((2 + nx + groups,)),
            pltpu.SemaphoreType.DMA((copies,)),
            pltpu.SemaphoreType.DMA((copies,)),
        ],
        compiler_params=pltpu.CompilerParams(
            collective_id=0, has_side_effects=True, vmem_limit_bytes=48 * 2**20
        ),
    )(
        last_query, key_cache, value_cache, residual, out_weight, query_emb,
        lengths, positives.reshape(1, rows),
    )
    side = heads * HEAD_DIM
    by_heads = pl.BlockSpec((rows, side), lambda g: (0, g))
    by_group = pl.BlockSpec((tokens, HEAD_DIM), lambda g: (0, g))
    whole = pl.BlockSpec((1, rows), lambda g: (0, 0))
    loss, query_grad, residual_grad, lastq_grad, key_grad, value_grad = pl.pallas_call(
        backward,
        grid=(groups,),
        out_shape=(
            jax.ShapeDtypeStruct((1, rows), F32),
            jax.ShapeDtypeStruct((rows, width), F32),
            jax.ShapeDtypeStruct((rows, width), F32),
            jax.ShapeDtypeStruct((rows, width), F32),
            jax.ShapeDtypeStruct((tokens, kv_width), BF16),
            jax.ShapeDtypeStruct((tokens, kv_width), BF16),
        ),
        in_specs=[
            by_heads, by_heads, by_group, by_group,
            pl.BlockSpec((1, heads * rows, tokens), lambda g: (g, 0, 0)),
            whole, by_heads, by_heads,
        ],
        out_specs=(whole, by_heads, by_heads, by_heads, by_group, by_group),
        scratch_shapes=[
            pltpu.VMEM((heads * rows, tokens), F32),
            pltpu.VMEM((heads * rows, tokens), BF16),
            pltpu.VMEM((heads * rows, tokens), BF16),
        ],
        compiler_params=pltpu.CompilerParams(vmem_limit_bytes=32 * 2**20),
    )(last_query, upstream, key_cache, value_cache, attn, loss, query_grad, residual_grad)
    return (loss.reshape(rows), query_grad, residual_grad, lastq_grad, key_grad, value_grad)


def solution(mesh, nz=8, ny=4):
    in_specs = (
        P("dp", "mp"),
        P("dp", "mp"),
        P("dp", "mp"),
        P("dp", "mp"),
        P("mp", None),
        P("dp", "mp"),
        P("dp", None),
        P("dp"),
    )
    out_specs = (P("dp"), P("dp", "mp"), P("dp", "mp"), P("dp", "mp"), P("dp", "mp"), P("dp", "mp"))
    sizes = (nz, ny, mesh.shape["mp"])
    return jax.shard_map(
        functools.partial(on_device, sizes),
        mesh=mesh,
        in_specs=in_specs,
        out_specs=out_specs,
        check_vma=False,
    )
```

```python
import functools

import jax
import jax.numpy as jnp
from jax import lax
from jax.experimental import pallas as pl
from jax.experimental.pallas import tpu as pltpu
from jax.sharding import PartitionSpec as P

HEAD_DIM = 128
INV_TEMP = 50.0
EPSILON = 1e-06
CORES = 2
MESH = pl.DeviceIdType.MESH
F32 = jnp.float32
BF16 = jnp.bfloat16


def dot_nn(a, b):
    return lax.dot_general(a, b, (((1,), (0,)), ((), ())), preferred_element_type=F32)


def dot_nt(a, b):
    return lax.dot_general(a, b, (((1,), (1,)), ((), ())), preferred_element_type=F32)


def dot_tn(a, b):
    return lax.dot_general(a, b, (((0,), (0,)), ((), ())), preferred_element_type=F32)


def kernel(
    sizes,
    lastq_hbm, key_hbm, value_hbm, resid_hbm, weight_hbm, query_hbm, len_ref, pos_ref,
    loss_ref, qgrad_ref, rgrad_ref, up_ref, attn_hbm,
    q_buf, p_buf, weight, key, value, lastq, resid, ranges, attn, probs, y_part, y_recv, s_part, s_recv, sq_all, turned,
    stat, w_all, misc_all, eg_part, eg_own, eg_side, eg_out, eg_recv, slope_all, qg_part, qg_recv,
    relay, relay_half, load_sem, send_sem, recv_sem,
):
    nz, ny, nx = sizes
    rows, width = query_hbm.shape
    tokens, kv_width = key_hbm.shape
    groups = kv_width // HEAD_DIM
    heads = width // kv_width
    inner = CORES * ny
    passages = inner * rows
    slots = nz // nx
    chunk = slots * rows
    scale = 1.0 / HEAD_DIM**0.5

    me = lax.axis_index("dp")
    x = lax.axis_index("mp")
    core = lax.rem(me, CORES)
    y = lax.rem(lax.div(me, CORES), ny)
    z = lax.div(me, inner)

    def place(z_at, y_at, core_at):
        return {"dp": (z_at * ny + y_at) * CORES + core_at}

    def around(at, step, size):
        return lax.rem(at + (step + size), size)

    def far_first(size):
        return sorted(range(1, size), key=lambda k: -min(k, size - k))

    xs = [around(x, k, nx) for k in range(nx)]
    ys = [around(y, k, ny) for k in range(ny)]
    zs = [around(z, k, nz) for k in range(nz)]
    twin = place(z, y, 1 - core)
    partners = [place(t, y, core) for t in zs[1:]] + [place(z, t, core) for t in ys[1:]]
    partners += [twin] + [{"mp": t} for t in xs[1:]]

    barrier = pltpu.get_barrier_semaphore()
    for partner in partners:
        pl.semaphore_signal(barrier, inc=1, device_id=partner, device_id_type=MESH)

    loads = [
        pltpu.make_async_copy(query_hbm, q_buf.at[z, :, pl.ds(0, width)], load_sem.at[0]),
        pltpu.make_async_copy(lastq_hbm, lastq, load_sem.at[1]),
        pltpu.make_async_copy(key_hbm, key, load_sem.at[2]),
        pltpu.make_async_copy(value_hbm, value, load_sem.at[3]),
        pltpu.make_async_copy(resid_hbm, resid, load_sem.at[4]),
    ]
    for k in far_first(nx) + [0]:
        columns = pl.ds(pl.multiple_of(xs[k] * width, width), width)
        loads.append(
            pltpu.make_async_copy(weight_hbm.at[:, columns], weight.at[k], load_sem.at[5 + k])
        )
    for load in loads:
        load.start()

    sent = []

    def push(src, dst, device):
        index = len(sent)
        copy = pltpu.make_async_remote_copy(
            src_ref=src,
            dst_ref=dst,
            send_sem=send_sem.at[index],
            recv_sem=recv_sem.at[index],
            device_id=device,
            device_id_type=MESH,
        )
        copy.start()
        sent.append(copy)
        return copy

    def exchange(src, dst):
        copies = [None] * nx
        for k in far_first(nx):
            copies[k] = push(src(k), dst.at[x], {"mp": xs[k]})
        return copies

    def received(copies, k):
        copies[k].wait_recv()
        return xs[nx - k]

    lane = lax.broadcasted_iota(jnp.int32, (rows, HEAD_DIM), 1)

    def three_parts(column):
        high = column.astype(BF16).astype(F32)
        middle = (column - high).astype(BF16).astype(F32)
        low = column - high - middle
        parts = jnp.where(lane == 0, high, jnp.where(lane == 1, middle, low))
        return jnp.where(lane < 3, parts, 0.0).astype(BF16)

    position = jnp.broadcast_to(pos_ref[...].astype(F32), (rows, rows))
    diagonal = lax.broadcasted_iota(jnp.int32, (rows, rows), 0) == lax.broadcasted_iota(
        jnp.int32, (rows, rows), 1
    )
    position = jnp.sum(jnp.where(diagonal, position, 0.0), axis=1, keepdims=True).astype(jnp.int32)
    high, low = lax.shift_right_logical(position, 6), position & 63
    digits = jnp.where(lane == 0, high, jnp.where(lane == 1, low, 0)).astype(F32).astype(BF16)
    q_buf[z, :, width:] = digits
    lengths = len_ref[...].astype(F32)
    passage = lax.broadcasted_iota(jnp.int32, (rows, rows), 0)
    which = lax.broadcasted_iota(jnp.int32, (rows, rows), 1)
    for i, before in enumerate((which < passage, which <= passage)):
        bound = jnp.sum(jnp.where(before, lengths, 0.0), axis=1, keepdims=True)
        ranges[i] = jnp.broadcast_to(bound, (rows, HEAD_DIM)).astype(jnp.int32)
    loads[0].wait()
    pl.semaphore_wait(barrier, len(partners))
    q_copies = {
        k: push(q_buf.at[z], q_buf.at[z], place(zs[k], y, core)) for k in (2, nz - 2, 1, nz - 1)
    }

    block = 16

    def softmax_rows(i, carry):
        at = pl.ds(pl.multiple_of(i * block, block), block)
        bounds = pl.ds(pl.multiple_of(lax.rem(i, rows // block) * block, block), block)
        token = lax.broadcasted_iota(jnp.int32, (block, tokens), 1)
        inside = (token >= ranges[0, bounds, :][:, :1]) & (token < ranges[1, bounds, :][:, :1])
        scores = jnp.where(inside, attn[at, :], -1e30)
        top = jnp.max(scores, axis=1, keepdims=True)
        powers = jnp.exp((scores - top) * scale)
        weights = powers * (1.0 / jnp.sum(powers, axis=1, keepdims=True))
        attn[at, :] = weights
        probs[at, :] = weights.astype(BF16)
        return carry

    for load in loads[1:4]:
        load.wait()
    group_rows = heads * rows
    blocks = groups * group_rows // block
    attn[...] = dot_nt(spread(lastq, groups, heads), key[...])
    lax.fori_loop(0, blocks, softmax_rows, 0, unroll=blocks)
    save = pltpu.make_async_copy(attn, attn_hbm, load_sem.at[5 + nx])
    save.start()
    out = dot_nn(probs[...], value[...]).astype(BF16)
    attended = [
        out[g * group_rows + h * rows : g * group_rows + (h + 1) * rows, g * HEAD_DIM :][:, :HEAD_DIM]
        for g in range(groups)
        for h in range(heads)
    ]
    attended = jnp.concatenate(attended, axis=1)

    for load in loads[4:]:
        load.wait()

    def project(k):
        y_part[k] = dot_nn(attended, weight[k]).astype(BF16)
        return y_part.at[k]

    y_copies = exchange(project, y_recv)
    hidden = dot_nn(attended, weight[0]) + resid[...].astype(F32)
    half = rows // 2
    onward = []
    for k, first in ((2, 0), (nz - 2, half)):
        q_copies[k].wait_recv()
        step = 1 if k == 2 else nz - 1
        part = q_buf.at[zs[nz - k]]
        onward.append(push(part, part, place(zs[step], y, core)))
        part = q_buf.at[zs[nz - k], pl.ds(first, half)]
        onward.append(push(part, part, place(zs[k], y, core)))
    for k in range(1, nx):
        hidden = hidden + y_recv[received(y_copies, k)].astype(F32)

    own = core * ny + y
    p_buf[own, :, :width] = hidden.astype(BF16)
    p_buf[own, :, width:] = three_parts(jnp.sum(hidden * hidden, axis=1, keepdims=True))
    p_copies = [None] * ny
    for k in far_first(ny):
        p_copies[k] = push(p_buf.at[own], p_buf.at[own], place(z, ys[k], core))
    passed = [push(p_buf.at[own], p_buf.at[own], twin)]
    for k in sorted(range(1, ny), key=lambda k: min(k, ny - k)):
        p_copies[k].wait_recv()
        part = p_buf.at[core * ny + ys[ny - k]]
        passed.append(push(part, part, twin))
    for copy in [q_copies[1], q_copies[nz - 1]] + onward + passed:
        copy.wait_recv()

    all_passages = p_buf[:, :, :width].reshape(passages, width)

    def partial_scores(t):
        part = q_buf[pl.ds(t * slots, slots), :, :width].reshape(chunk, width)
        return dot_nt(part, all_passages)

    def send_scores(k):
        s_part[k] = partial_scores(xs[k])
        return s_part.at[k]

    unit = (lax.broadcasted_iota(jnp.int32, (8, HEAD_DIM), 1) < 3).astype(F32).astype(BF16)
    sq_all[x] = dot_nt(unit, p_buf[:, :, width:].reshape(passages, HEAD_DIM))
    sq_copies = exchange(lambda k: sq_all.at[x], sq_all)
    s_copies = exchange(send_scores, s_recv)
    scores = partial_scores(x)
    squares = sq_all[x]
    for k in range(1, nx):
        squares = squares + sq_all[received(sq_copies, k)]
    norms = jnp.sqrt(squares[:1] + EPSILON)
    turned[...] = jnp.broadcast_to(norms, (HEAD_DIM, passages)).T
    norm = turned[pl.ds(pl.multiple_of(own * rows, rows), rows), :][:, :1]
    emb = hidden / norm
    digits = q_buf[pl.ds(x * slots, slots), :, width:].reshape(chunk, HEAD_DIM).astype(F32)
    positive = (digits[:, 0:1] * 64.0 + digits[:, 1:2]).astype(jnp.int32)
    index = lax.broadcasted_iota(jnp.int32, (chunk, passages), 1)
    slot = lax.div(index, rows)
    cell = lax.rem(slot, ny) * CORES + lax.div(slot, ny)
    match = positive == (z * inner + cell) * rows + lax.rem(index, rows)
    for k in range(1, nx):
        scores = scores + s_recv[received(s_copies, k)]
    scores = scores * (INV_TEMP / norms)

    top = jnp.max(scores, axis=1, keepdims=True)
    total = jnp.sum(jnp.exp(scores - top), axis=1, keepdims=True)
    hit = jnp.sum(jnp.where(match, scores, 0.0), axis=1, keepdims=True)
    chunk_lane = lax.broadcasted_iota(jnp.int32, (chunk, HEAD_DIM), 1)
    columns = jnp.where(chunk_lane == 0, top, jnp.where(chunk_lane == 1, total, hit))
    stat[z] = jnp.concatenate([columns] * (HEAD_DIM // chunk), axis=0).T[:8]
    stat_copies = [push(stat.at[z], stat.at[z], place(zs[k], y, core)) for k in far_first(nz)]
    for copy in stat_copies:
        copy.wait_recv()
    every = stat[...]
    top = jnp.max(every[:, 0:1], axis=0)
    total = jnp.sum(every[:, 1:2] * jnp.exp(every[:, 0:1] - top[None]), axis=0)
    lse = top + jnp.log(total)
    loss = lse - jnp.sum(every[:, 2:3], axis=0)
    lse = jnp.broadcast_to(lse, (HEAD_DIM, HEAD_DIM)).T[:chunk, :1]

    pairs = (jnp.exp(scores - lse) - match.astype(F32)).astype(BF16)
    w_all[x] = pairs
    w_copies = exchange(lambda k: w_all.at[x], w_all)
    along = jnp.sum(pairs.astype(F32) * scores, axis=0, keepdims=True)
    line = lax.broadcasted_iota(jnp.int32, (8, passages), 0)
    losses = jnp.concatenate([loss] * (passages // HEAD_DIM), axis=1)
    misc_all[x] = jnp.where(line == 0, along, losses)
    misc_copies = exchange(lambda k: misc_all.at[x], misc_all)
    for k in range(1, nx):
        received(w_copies, k)
        received(misc_copies, k)
    losses = misc_all[lax.div(z, slots)][1:2]
    own_loss = losses[:, :rows]
    for k in range(1, slots):
        own_loss = jnp.where(lax.rem(z, slots) == k, losses[:, k * rows : (k + 1) * rows], own_loss)
    loss_ref[...] = own_loss
    along = misc_all[0][:1]
    for k in range(1, nx):
        along = along + misc_all[k][:1]
    turned[...] = jnp.broadcast_to(along, (HEAD_DIM, passages)).T

    share = ny * rows

    def emb_share(core_at):
        part = w_all[:, :, pl.ds(pl.multiple_of(core_at * share, share), share)]
        part = part.reshape(nx * chunk, share)
        return dot_tn(part, q_buf[:, :, :width].reshape(nz * rows, width)) * INV_TEMP

    def along_of(core_at, y_at):
        first = pl.multiple_of((core_at * ny + y_at) * rows, rows)
        return turned[pl.ds(first, rows), :][:, :1]

    grads = emb_share(1 - core).reshape(ny, rows, width)
    eg_part[:, :, :width] = grads.astype(BF16)
    for j in range(ny):
        eg_part[j, :, width:] = three_parts(along_of(1 - core, j))
    side_copy = push(eg_part, eg_side, twin)
    eg_own[...] = emb_share(core).reshape(ny, rows, width)

    pairs = w_all[...].reshape(nx * chunk, passages).astype(F32) * (INV_TEMP / norms)
    grads = dot_nn(pairs.astype(BF16), all_passages)
    qg_part[...] = grads.astype(BF16).reshape(nz, rows, width)
    one, last, two, other = 1, nz - 1, 2, nz - 2
    near = [push(qg_part.at[zs[one]], qg_recv.at[0], place(zs[one], y, core))]
    near.append(push(qg_part.at[zs[last]], qg_recv.at[1], place(zs[last], y, core)))
    far = [push(qg_part.at[zs[4], pl.ds(0, half)], relay_half.at[0], place(zs[other], y, core))]
    far.append(push(qg_part.at[zs[4], pl.ds(half, half)], relay_half.at[1], place(zs[two], y, core)))
    far.append(push(qg_part.at[zs[nz - 3]], relay.at[0], place(zs[last], y, core)))
    far.append(push(qg_part.at[zs[3]], relay.at[1], place(zs[one], y, core)))
    side_copy.wait_recv()

    def emb_sum(y_at):
        side = eg_side[y_at]
        parts = side[:, width:].astype(F32)
        total = eg_own[y_at] + side[:, :width].astype(F32)
        return total, along_of(core, y_at) + (parts[:, 0:1] + parts[:, 1:2] + parts[:, 2:3])

    eg_copies = [None] * ny
    for k in far_first(ny):
        total, along = emb_sum(ys[k])
        eg_out[k, :, :width] = total.astype(BF16)
        eg_out[k, :, width:] = three_parts(along)
        eg_copies[k] = push(eg_out.at[k], eg_recv.at[y], place(z, ys[k], core))
    emb_grad, along = emb_sum(y)
    for copy in far:
        copy.wait_recv()
    for i, k in enumerate((other, two)):
        total = qg_part[zs[k]].astype(F32) + relay[i].astype(F32)
        extra = relay_half[i].astype(F32)
        parts = [total[:half], total[half:]]
        parts[i] = parts[i] + extra
        relay[i] = jnp.concatenate(parts, axis=0).astype(BF16)
        near.append(push(relay.at[i], qg_recv.at[2 + i], place(zs[k], y, core)))
    for k in range(1, ny):
        eg_copies[k].wait_recv()
        side = eg_recv[ys[ny - k]]
        parts = side[:, width:].astype(F32)
        emb_grad = emb_grad + side[:, :width].astype(F32)
        along = along + (parts[:, 0:1] + parts[:, 1:2] + parts[:, 2:3])
    residual_grad = (emb_grad - emb * along) / norm
    rgrad_ref[...] = residual_grad

    slope = residual_grad.astype(BF16)
    slope_all[x] = slope
    slope_copies = exchange(lambda k: slope_all.at[x], slope_all)
    upstream = dot_nt(slope, weight[0])
    for k in range(1, nx):
        t = received(slope_copies, k)
        upstream = upstream + dot_nt(slope_all[t], weight[nx - k])
    up_ref[...] = upstream.astype(BF16)

    query_grad = qg_part[z].astype(F32)
    for i, copy in enumerate(near):
        copy.wait_recv()
        query_grad = query_grad + qg_recv[i].astype(F32)
    qgrad_ref[...] = query_grad
    save.wait()
    for copy in sent:
        copy.wait_send()


def grouped(source, g, heads):
    first = g * heads
    return jnp.concatenate(
        [source[:, (first + h) * HEAD_DIM : (first + h + 1) * HEAD_DIM] for h in range(heads)],
        axis=0,
    )


def spread(source, groups, heads):
    parts = [grouped(source, g, heads) for g in range(groups)]
    empty = jnp.zeros_like(parts[0])
    lines = [
        jnp.concatenate([part if i == g else empty for i in range(groups)], axis=1)
        for g, part in enumerate(parts)
    ]
    return jnp.concatenate(lines, axis=0)


def backward(
    lastq_ref, up_ref, key_ref, value_ref, attn_ref, loss_in, qgrad_in, rgrad_in,
    loss_ref, qgrad_ref, rgrad_ref, lgrad_ref, kgrad_ref, vgrad_ref, slopes, probs, score_slope,
):
    loss_ref[...] = loss_in[...]
    qgrad_ref[...] = qgrad_in[...]
    rgrad_ref[...] = rgrad_in[...]
    rows = lastq_ref.shape[0]
    heads = lastq_ref.shape[1] // HEAD_DIM
    scale = 1.0 / HEAD_DIM**0.5
    block = 16
    up = grouped(up_ref, 0, heads)
    slopes[...] = dot_nt(up, value_ref[...])

    def body(i, carry):
        at = pl.ds(pl.multiple_of(i * block, block), block)
        weights = attn_ref[at, :]
        slope_at = slopes[at, :]
        mean = jnp.sum(weights * slope_at, axis=1, keepdims=True)
        score_slope[at, :] = (weights * (slope_at - mean)).astype(BF16)
        probs[at, :] = weights.astype(BF16)
        return carry

    lax.fori_loop(0, heads * rows // block, body, 0, unroll=heads * rows // block)
    vgrad_ref[...] = dot_tn(probs[...], up).astype(BF16)
    lastq = dot_nn(score_slope[...], key_ref[...]) * scale
    for h in range(heads):
        lgrad_ref[:, h * HEAD_DIM : (h + 1) * HEAD_DIM] = lastq[h * rows : (h + 1) * rows]
    queries = grouped(lastq_ref, 0, heads)
    kgrad_ref[...] = (dot_tn(score_slope[...], queries) * scale).astype(BF16)


def on_device(
    sizes, last_query, key_cache, value_cache, residual, out_weight, query_emb, lengths, positives
):
    nz, ny, nx = sizes
    rows, width = query_emb.shape
    tokens, kv_width = key_cache.shape
    groups = kv_width // HEAD_DIM
    heads = width // kv_width
    inner = CORES * ny
    passages = inner * rows
    chunk = nz // nx * rows
    wide = width + HEAD_DIM
    vmem = pl.BlockSpec(memory_space=pltpu.VMEM)
    hbm = pl.BlockSpec(memory_space=pl.ANY)
    copies = 3 * (nz - 1) + 3 * ny + 7 * (nx - 1)
    loss, query_grad, residual_grad, upstream, attn = pl.pallas_call(
        functools.partial(kernel, sizes),
        out_shape=(
            jax.ShapeDtypeStruct((1, rows), F32),
            jax.ShapeDtypeStruct((rows, width), F32),
            jax.ShapeDtypeStruct((rows, width), F32),
            jax.ShapeDtypeStruct((rows, width), BF16),
            jax.ShapeDtypeStruct((groups * heads * rows, tokens), F32),
        ),
        in_specs=[hbm, hbm, hbm, hbm, hbm, hbm, vmem, vmem],
        out_specs=(vmem, vmem, vmem, vmem, hbm),
        scratch_shapes=[
            pltpu.VMEM((nz, rows, wide), BF16),
            pltpu.VMEM((inner, rows, wide), BF16),
            pltpu.VMEM((nx, width, width), BF16),
            pltpu.VMEM((tokens, kv_width), BF16),
            pltpu.VMEM((tokens, kv_width), BF16),
            pltpu.VMEM((rows, width), BF16),
            pltpu.VMEM((rows, width), BF16),
            pltpu.VMEM((2, rows, HEAD_DIM), jnp.int32),
            pltpu.VMEM((groups * heads * rows, tokens), F32),
            pltpu.VMEM((groups * heads * rows, tokens), BF16),
            pltpu.VMEM((nx, rows, width), BF16),
            pltpu.VMEM((nx, rows, width), BF16),
            pltpu.VMEM((nx, chunk, passages), F32),
            pltpu.VMEM((nx, chunk, passages), F32),
            pltpu.VMEM((nx, 8, passages), F32),
            pltpu.VMEM((passages, HEAD_DIM), F32),
            pltpu.VMEM((nz, 8, HEAD_DIM), F32),
            pltpu.VMEM((nx, chunk, passages), BF16),
            pltpu.VMEM((nx, 8, passages), F32),
            pltpu.VMEM((ny, rows, wide), BF16),
            pltpu.VMEM((ny, rows, width), F32),
            pltpu.VMEM((ny, rows, wide), BF16),
            pltpu.VMEM((ny, rows, wide), BF16),
            pltpu.VMEM((ny, rows, wide), BF16),
            pltpu.VMEM((nx, rows, width), BF16),
            pltpu.VMEM((nz, rows, width), BF16),
            pltpu.VMEM((4, rows, width), BF16),
            pltpu.VMEM((2, rows, width), BF16),
            pltpu.VMEM((2, rows // 2, width), BF16),
            pltpu.SemaphoreType.DMA((6 + nx,)),
            pltpu.SemaphoreType.DMA((copies,)),
            pltpu.SemaphoreType.DMA((copies,)),
        ],
        compiler_params=pltpu.CompilerParams(
            collective_id=0, has_side_effects=True, vmem_limit_bytes=60 * 2**20
        ),
    )(
        last_query, key_cache, value_cache, residual, out_weight, query_emb,
        lengths, positives.reshape(1, rows),
    )
    side = heads * HEAD_DIM
    by_heads = pl.BlockSpec((rows, side), lambda g: (0, g))
    by_group = pl.BlockSpec((tokens, HEAD_DIM), lambda g: (0, g))
    whole = pl.BlockSpec((1, rows), lambda g: (0, 0))
    loss, query_grad, residual_grad, lastq_grad, key_grad, value_grad = pl.pallas_call(
        backward,
        grid=(groups,),
        out_shape=(
            jax.ShapeDtypeStruct((1, rows), F32),
            jax.ShapeDtypeStruct((rows, width), F32),
            jax.ShapeDtypeStruct((rows, width), F32),
            jax.ShapeDtypeStruct((rows, width), F32),
            jax.ShapeDtypeStruct((tokens, kv_width), BF16),
            jax.ShapeDtypeStruct((tokens, kv_width), BF16),
        ),
        in_specs=[
            by_heads, by_heads, by_group, by_group,
            pl.BlockSpec((heads * rows, tokens), lambda g: (g, 0)),
            whole, by_heads, by_heads,
        ],
        out_specs=(whole, by_heads, by_heads, by_heads, by_group, by_group),
        scratch_shapes=[
            pltpu.VMEM((heads * rows, tokens), F32),
            pltpu.VMEM((heads * rows, tokens), BF16),
            pltpu.VMEM((heads * rows, tokens), BF16),
        ],
        compiler_params=pltpu.CompilerParams(vmem_limit_bytes=60 * 2**20),
    )(last_query, upstream, key_cache, value_cache, attn, loss, query_grad, residual_grad)
    return (loss.reshape(rows), query_grad, residual_grad, lastq_grad, key_grad, value_grad)


def solution(mesh, nz=8, ny=4):
    in_specs = (
        P("dp", "mp"),
        P("dp", "mp"),
        P("dp", "mp"),
        P("dp", "mp"),
        P("mp", None),
        P("dp", "mp"),
        P("dp", None),
        P("dp"),
    )
    out_specs = (P("dp"), P("dp", "mp"), P("dp", "mp"), P("dp", "mp"), P("dp", "mp"), P("dp", "mp"))
    sizes = (nz, ny, mesh.shape["mp"])
    return jax.shard_map(
        functools.partial(on_device, sizes),
        mesh=mesh,
        in_specs=in_specs,
        out_specs=out_specs,
        check_vma=False,
    )
```

```python
import functools

import jax
import jax.numpy as jnp
from jax import lax
from jax.experimental import pallas as pl
from jax.experimental.pallas import tpu as pltpu
from jax.sharding import PartitionSpec as P

HEAD_DIM = 128
INV_TEMP = 50.0
EPSILON = 1e-06
CORES = 2
MESH = pl.DeviceIdType.MESH
F32 = jnp.float32
BF16 = jnp.bfloat16


def dot_nn(a, b):
    return lax.dot_general(a, b, (((1,), (0,)), ((), ())), preferred_element_type=F32)


def dot_nt(a, b):
    return lax.dot_general(a, b, (((1,), (1,)), ((), ())), preferred_element_type=F32)


def dot_tn(a, b):
    return lax.dot_general(a, b, (((0,), (0,)), ((), ())), preferred_element_type=F32)


def kernel(
    sizes,
    lastq_hbm, key_hbm, value_hbm, resid_hbm, weight_hbm, query_hbm, len_ref, pos_ref,
    loss_ref, qgrad_ref, rgrad_ref, up_ref, out_ref, probs_hbm,
    q_buf, p_buf, weight, key, value, lastq, resid, ranges, attn, probs, y_part, y_recv, s_part, s_recv, sq_all, turned,
    stat, s_all, w_all, misc_all, eg_part, eg_own, eg_side, eg_out, eg_recv, slope_all, qg_part, qg_recv,
    relay, relay_half, load_sem, send_sem, recv_sem,
):
    nz, ny, nx = sizes
    rows, width = query_hbm.shape
    tokens, kv_width = key_hbm.shape
    groups = kv_width // HEAD_DIM
    heads = width // kv_width
    inner = CORES * ny
    passages = inner * rows
    slots = nz // nx
    chunk = slots * rows
    scale = 1.0 / HEAD_DIM**0.5

    me = lax.axis_index("dp")
    x = lax.axis_index("mp")
    core = lax.rem(me, CORES)
    y = lax.rem(lax.div(me, CORES), ny)
    z = lax.div(me, inner)

    def place(z_at, y_at, core_at):
        return {"dp": (z_at * ny + y_at) * CORES + core_at}

    def around(at, step, size):
        return lax.rem(at + (step + size), size)

    def far_first(size):
        return sorted(range(1, size), key=lambda k: -min(k, size - k))

    xs = [around(x, k, nx) for k in range(nx)]
    ys = [around(y, k, ny) for k in range(ny)]
    zs = [around(z, k, nz) for k in range(nz)]
    twin = place(z, y, 1 - core)
    partners = [place(t, y, core) for t in zs[1:]] + [place(z, t, core) for t in ys[1:]]
    partners += [twin] + [{"mp": t} for t in xs[1:]]

    barrier = pltpu.get_barrier_semaphore()
    for partner in partners:
        pl.semaphore_signal(barrier, inc=1, device_id=partner, device_id_type=MESH)

    loads = [
        pltpu.make_async_copy(query_hbm, q_buf.at[z, :, pl.ds(0, width)], load_sem.at[0]),
        pltpu.make_async_copy(lastq_hbm, lastq, load_sem.at[1]),
        pltpu.make_async_copy(key_hbm, key, load_sem.at[2]),
        pltpu.make_async_copy(value_hbm, value, load_sem.at[3]),
        pltpu.make_async_copy(resid_hbm, resid, load_sem.at[4]),
    ]
    waits = {}
    for k in far_first(nx) + [0]:
        waits[k] = len(loads)
        columns = pl.ds(pl.multiple_of(xs[k] * width, width), width)
        loads.append(
            pltpu.make_async_copy(weight_hbm.at[:, columns], weight.at[k], load_sem.at[5 + k])
        )
    for load in loads[:4]:
        load.start()

    sent = []

    def push(src, dst, device):
        index = len(sent)
        copy = pltpu.make_async_remote_copy(
            src_ref=src,
            dst_ref=dst,
            send_sem=send_sem.at[index],
            recv_sem=recv_sem.at[index],
            device_id=device,
            device_id_type=MESH,
        )
        copy.start()
        sent.append(copy)
        return copy

    def exchange(src, dst):
        copies = [None] * nx
        for k in far_first(nx):
            copies[k] = push(src(k), dst.at[x], {"mp": xs[k]})
        return copies

    def received(copies, k):
        copies[k].wait_recv()
        return xs[nx - k]

    lane = lax.broadcasted_iota(jnp.int32, (rows, HEAD_DIM), 1)

    def three_parts(column):
        high = column.astype(BF16).astype(F32)
        middle = (column - high).astype(BF16).astype(F32)
        low = column - high - middle
        parts = jnp.where(lane == 0, high, jnp.where(lane == 1, middle, low))
        return jnp.where(lane < 3, parts, 0.0).astype(BF16)

    position = jnp.broadcast_to(pos_ref[...].astype(F32), (rows, rows))
    diagonal = lax.broadcasted_iota(jnp.int32, (rows, rows), 0) == lax.broadcasted_iota(
        jnp.int32, (rows, rows), 1
    )
    position = jnp.sum(jnp.where(diagonal, position, 0.0), axis=1, keepdims=True).astype(jnp.int32)
    high, low = lax.shift_right_logical(position, 6), position & 63
    digits = jnp.where(lane == 0, high, jnp.where(lane == 1, low, 0)).astype(F32).astype(BF16)
    q_buf[z, :, width:] = digits
    lengths = len_ref[...].astype(F32)
    passage = lax.broadcasted_iota(jnp.int32, (rows, rows), 0)
    which = lax.broadcasted_iota(jnp.int32, (rows, rows), 1)
    for i, before in enumerate((which < passage, which <= passage)):
        bound = jnp.sum(jnp.where(before, lengths, 0.0), axis=1, keepdims=True)
        ranges[i] = jnp.broadcast_to(bound, (rows, HEAD_DIM)).astype(jnp.int32)
    loads[0].wait()
    pl.semaphore_wait(barrier, len(partners))
    q_copies = {
        k: push(q_buf.at[z], q_buf.at[z], place(zs[k], y, core)) for k in (2, nz - 2, 1, nz - 1)
    }

    block = 16

    def softmax_rows(i, carry):
        at = pl.ds(pl.multiple_of(i * block, block), block)
        bounds = pl.ds(pl.multiple_of(lax.rem(i, rows // block) * block, block), block)
        token = lax.broadcasted_iota(jnp.int32, (block, tokens), 1)
        inside = (token >= ranges[0, bounds, :][:, :1]) & (token < ranges[1, bounds, :][:, :1])
        scores = jnp.where(inside, attn[at, :], -1e30)
        top = jnp.max(scores, axis=1, keepdims=True)
        powers = jnp.exp((scores - top) * scale)
        weights = powers * (1.0 / jnp.sum(powers, axis=1, keepdims=True))
        probs[at, :] = weights.astype(BF16)
        return carry

    for load in loads[1:4]:
        load.wait()
    for load in loads[4:]:
        load.start()
    group_rows = heads * rows
    blocks = groups * group_rows // block
    attn[...] = dot_nt(spread(lastq, groups, heads), key[...])
    lax.fori_loop(0, blocks, softmax_rows, 0, unroll=blocks)
    out = dot_nn(probs[...], value[...])
    attended = [
        out[g * group_rows + h * rows : g * group_rows + (h + 1) * rows, g * HEAD_DIM :][:, :HEAD_DIM]
        for g in range(groups)
        for h in range(heads)
    ]
    attended = jnp.concatenate(attended, axis=1)
    out_ref[...] = attended
    attended = attended.astype(BF16)

    side_width = width // 2
    sides = [slice(i * side_width, (i + 1) * side_width) for i in range(2)]

    def project(k, i):
        if i == 0:
            loads[waits[k]].wait()
        y_part[k, :, sides[i]] = dot_nn(attended, weight[k, :, sides[i]]).astype(BF16)
        return y_part.at[k, :, pl.ds(i * side_width, side_width)]

    y_copies = []
    for i in range(2):
        target = y_recv.at[:, :, pl.ds(i * side_width, side_width)]
        y_copies.append(exchange(lambda k: project(k, i), target))
    save = pltpu.make_async_copy(probs, probs_hbm, load_sem.at[5 + nx])
    save.start()
    loads[4].wait()
    loads[waits[0]].wait()
    hiddens = [
        dot_nn(attended, weight[0, :, part]) + resid[:, part].astype(F32) for part in sides
    ]
    half = rows // 2
    onward = []
    for k, first in ((2, 0), (nz - 2, half)):
        q_copies[k].wait_recv()
        step = 1 if k == 2 else nz - 1
        part = q_buf.at[zs[nz - k]]
        onward.append(push(part, part, place(zs[step], y, core)))
        part = q_buf.at[zs[nz - k], pl.ds(first, half)]
        onward.append(push(part, part, place(zs[k], y, core)))

    own = core * ny + y
    spans = (pl.ds(0, side_width), pl.ds(side_width, side_width + HEAD_DIM))
    p_copies = [[None] * ny, [None] * ny]
    passed = [[], []]
    for i, part in enumerate(sides):
        for k in range(1, nx):
            t = received(y_copies[i], k)
            hiddens[i] = hiddens[i] + y_recv[t, :, part].astype(F32)
        p_buf[own, :, part] = hiddens[i].astype(BF16)
        if i == 1:
            squares = [jnp.sum(hidden * hidden, axis=1, keepdims=True) for hidden in hiddens]
            p_buf[own, :, width:] = three_parts(squares[0] + squares[1])
        block_at = p_buf.at[own, :, spans[i]]
        for k in far_first(ny):
            p_copies[i][k] = push(block_at, block_at, place(z, ys[k], core))
        passed[i].append(push(block_at, block_at, twin))
    for i in range(2):
        for k in sorted(range(1, ny), key=lambda k: min(k, ny - k)):
            p_copies[i][k].wait_recv()
            block_at = p_buf.at[core * ny + ys[ny - k], :, spans[i]]
            passed[i].append(push(block_at, block_at, twin))
    for copy in [q_copies[1], q_copies[nz - 1]] + onward:
        copy.wait_recv()

    def partial_scores(t, i):
        part = q_buf[pl.ds(t * slots, slots), :, sides[i]].reshape(chunk, side_width)
        return dot_nt(part, p_buf[:, :, sides[i]].reshape(passages, side_width))

    for copy in passed[0]:
        copy.wait_recv()
    for k in range(nx):
        s_part[k] = partial_scores(xs[k], 0)
    for copy in passed[1]:
        copy.wait_recv()

    def send_scores(k):
        s_part[k] += partial_scores(xs[k], 1)
        return s_part.at[k]

    unit = (lax.broadcasted_iota(jnp.int32, (8, HEAD_DIM), 1) < 3).astype(F32).astype(BF16)
    sq_all[x] = dot_nt(unit, p_buf[:, :, width:].reshape(passages, HEAD_DIM))
    sq_copies = exchange(lambda k: sq_all.at[x], sq_all)
    s_copies = exchange(send_scores, s_recv)
    scores = s_part[0] + partial_scores(x, 1)
    squares = sq_all[x]
    for k in range(1, nx):
        squares = squares + sq_all[received(sq_copies, k)]
    norms = jnp.sqrt(squares[:1] + EPSILON)
    turned[...] = jnp.broadcast_to(norms, (HEAD_DIM, passages)).T
    norm = turned[pl.ds(pl.multiple_of(own * rows, rows), rows), :][:, :1]
    embs = [hidden / norm for hidden in hiddens]
    digits = q_buf[:, :, width:].reshape(nz * rows, HEAD_DIM).astype(F32)
    positive = (digits[:, 0:1] * 64.0 + digits[:, 1:2]).astype(jnp.int32)
    index = lax.broadcasted_iota(jnp.int32, (nz * rows, passages), 1)
    slot = lax.div(index, rows)
    cell = lax.rem(slot, ny) * CORES + lax.div(slot, ny)
    passage_of = (z * inner + cell) * rows + lax.rem(index, rows)
    match = positive == passage_of
    for k in range(1, nx):
        scores = scores + s_recv[received(s_copies, k)]
    scores = scores * (INV_TEMP / norms)
    s_all[x] = scores
    all_copies = exchange(lambda k: s_all.at[x], s_all)

    top = jnp.max(scores, axis=1, keepdims=True)
    total = jnp.sum(jnp.exp(scores - top), axis=1, keepdims=True)
    own_digits = q_buf[pl.ds(x * slots, slots), :, width:].reshape(chunk, HEAD_DIM).astype(F32)
    own_positive = (own_digits[:, 0:1] * 64.0 + own_digits[:, 1:2]).astype(jnp.int32)
    own_match = own_positive == passage_of[:chunk]
    hit = jnp.sum(jnp.where(own_match, scores, 0.0), axis=1, keepdims=True)
    chunk_lane = lax.broadcasted_iota(jnp.int32, (chunk, HEAD_DIM), 1)
    columns = jnp.where(chunk_lane == 0, top, jnp.where(chunk_lane == 1, total, hit))
    stat[z] = jnp.concatenate([columns] * (HEAD_DIM // chunk), axis=0).T[:8]
    stat_copies = [push(stat.at[z], stat.at[z], place(zs[k], y, core)) for k in far_first(nz)]
    for copy in stat_copies:
        copy.wait_recv()
    every = stat[...]
    top = jnp.max(every[:, 0:1], axis=0)
    total = jnp.sum(every[:, 1:2] * jnp.exp(every[:, 0:1] - top[None]), axis=0)
    lse = top + jnp.log(total)
    loss = lse - jnp.sum(every[:, 2:3], axis=0)
    line = lax.broadcasted_iota(jnp.int32, (8, HEAD_DIM), 0)
    misc_all[x] = jnp.where(line == 0, lse, loss)
    misc_copies = exchange(lambda k: misc_all.at[x], misc_all)
    for k in range(1, nx):
        received(all_copies, k)
    for k in range(1, nx):
        received(misc_copies, k)
    losses = misc_all[lax.div(z, slots)][1:2]
    own_loss = losses[:, :rows]
    for k in range(1, slots):
        own_loss = jnp.where(lax.rem(z, slots) == k, losses[:, k * rows : (k + 1) * rows], own_loss)
    loss_ref[...] = own_loss

    lines = [misc_all[t][:1] for t in range(nx)] + [jnp.zeros((HEAD_DIM - nx, HEAD_DIM), F32)]
    turned_lse = jnp.concatenate(lines, axis=0).T
    lse = jnp.concatenate([turned_lse[:chunk, t : t + 1] for t in range(nx)], axis=0)
    scores = s_all[...].reshape(nx * chunk, passages)
    pairs = jnp.exp(scores - lse) - match.astype(F32)
    along = jnp.sum(pairs.astype(BF16).astype(F32) * scores, axis=0, keepdims=True)
    w_all[...] = pairs.astype(BF16)
    turned[...] = jnp.broadcast_to(along, (HEAD_DIM, passages)).T

    share = ny * rows
    spans = ((0, HEAD_DIM + side_width), (HEAD_DIM + side_width, side_width))

    def emb_share(core_at, i):
        part = w_all[:, pl.ds(pl.multiple_of(core_at * share, share), share)]
        queries = q_buf[:, :, i * side_width : (i + 1) * side_width].reshape(nz * rows, side_width)
        return (dot_tn(part, queries) * INV_TEMP).reshape(ny, rows, side_width)

    def along_of(core_at, y_at):
        first = pl.multiple_of((core_at * ny + y_at) * rows, rows)
        return turned[pl.ds(first, rows), :][:, :1]

    def columns_of(i):
        return slice(HEAD_DIM + i * side_width, HEAD_DIM + (i + 1) * side_width)

    def span(buf, i):
        return buf.at[:, pl.ds(*spans[i])] if len(buf.shape) == 2 else buf.at[:, :, pl.ds(*spans[i])]

    for j in range(ny):
        eg_part[j, :, :HEAD_DIM] = three_parts(along_of(1 - core, j))
    side_copies = []
    for i in range(2):
        eg_part[:, :, columns_of(i)] = emb_share(1 - core, i).astype(BF16)
        side_copies.append(push(span(eg_part, i), span(eg_side, i), twin))
    for i in range(2):
        eg_own[:, :, i * side_width : (i + 1) * side_width] = emb_share(core, i)

    pairs = (pairs * (INV_TEMP / norms)).astype(BF16)
    grads = dot_nn(pairs, p_buf[:, :, :width].reshape(passages, width))
    qg_part[...] = grads.astype(BF16).reshape(nz, rows, width)
    one, last, two, other = 1, nz - 1, 2, nz - 2
    near = [push(qg_part.at[zs[one]], qg_recv.at[0], place(zs[one], y, core))]
    near.append(push(qg_part.at[zs[last]], qg_recv.at[1], place(zs[last], y, core)))
    far = [push(qg_part.at[zs[4], pl.ds(0, half)], relay_half.at[0], place(zs[other], y, core))]
    far.append(push(qg_part.at[zs[4], pl.ds(half, half)], relay_half.at[1], place(zs[two], y, core)))
    far.append(push(qg_part.at[zs[nz - 3]], relay.at[0], place(zs[last], y, core)))
    far.append(push(qg_part.at[zs[3]], relay.at[1], place(zs[one], y, core)))

    def emb_sum(y_at, i):
        own_part = eg_own[y_at, :, i * side_width : (i + 1) * side_width]
        return own_part + eg_side[y_at, :, columns_of(i)].astype(F32)

    def along_parts(buf, at):
        parts = buf[at, :, :HEAD_DIM].astype(F32)
        return parts[:, 0:1] + parts[:, 1:2] + parts[:, 2:3]

    eg_copies = []
    for i in range(2):
        side_copies[i].wait_recv()
        copies = [None] * ny
        for k in far_first(ny):
            eg_out[k, :, columns_of(i)] = emb_sum(ys[k], i).astype(BF16)
            if i == 0:
                along = along_of(core, ys[k]) + along_parts(eg_side, ys[k])
                eg_out[k, :, :HEAD_DIM] = three_parts(along)
            copies[k] = push(
                span(eg_out.at[k], i), span(eg_recv.at[y], i), place(z, ys[k], core)
            )
        eg_copies.append(copies)
    for copy in far:
        copy.wait_recv()
    for i, k in enumerate((other, two)):
        total = qg_part[zs[k]].astype(F32) + relay[i].astype(F32)
        extra = relay_half[i].astype(F32)
        parts = [total[:half], total[half:]]
        parts[i] = parts[i] + extra
        relay[i] = jnp.concatenate(parts, axis=0).astype(BF16)
        near.append(push(relay.at[i], qg_recv.at[2 + i], place(zs[k], y, core)))
    along = along_of(core, y) + along_parts(eg_side, y)
    slope_copies = []
    slopes = []
    for i in range(2):
        emb_grad = emb_sum(y, i)
        for k in range(1, ny):
            eg_copies[i][k].wait_recv()
            emb_grad = emb_grad + eg_recv[ys[ny - k], :, columns_of(i)].astype(F32)
            if i == 0:
                along = along + along_parts(eg_recv, ys[ny - k])
        part = slice(i * side_width, (i + 1) * side_width)
        residual_grad = (emb_grad - embs[i] * along) / norm
        rgrad_ref[:, part] = residual_grad
        slopes.append(residual_grad.astype(BF16))
        slope_all[x, :, part] = slopes[-1]
        place_at = slope_all.at[:, :, pl.ds(i * side_width, side_width)]
        slope_copies.append(exchange(lambda k: place_at.at[x], place_at))

    upstream = dot_nt(jnp.concatenate(slopes, axis=1), weight[0])
    for i in range(2):
        part = slice(i * side_width, (i + 1) * side_width)
        for k in sorted(range(1, nx), key=lambda k: min(k, nx - k)):
            t = received(slope_copies[i], k)
            upstream = upstream + dot_nt(slope_all[t, :, part], weight[nx - k, :, part])
    up_ref[...] = upstream.astype(BF16)

    query_grad = qg_part[z].astype(F32)
    for i, copy in enumerate(near):
        copy.wait_recv()
        query_grad = query_grad + qg_recv[i].astype(F32)
    qgrad_ref[...] = query_grad
    save.wait()
    for copy in sent:
        copy.wait_send()


def grouped(source, g, heads):
    first = g * heads
    return jnp.concatenate(
        [source[:, (first + h) * HEAD_DIM : (first + h + 1) * HEAD_DIM] for h in range(heads)],
        axis=0,
    )


def spread(source, groups, heads):
    parts = [grouped(source, g, heads) for g in range(groups)]
    empty = jnp.zeros_like(parts[0])
    lines = [
        jnp.concatenate([part if i == g else empty for i in range(groups)], axis=1)
        for g, part in enumerate(parts)
    ]
    return jnp.concatenate(lines, axis=0)


def backward(
    lastq_ref, up_ref, out_ref, key_ref, value_ref, probs_ref, loss_in, qgrad_in, rgrad_in,
    loss_ref, qgrad_ref, rgrad_ref, lgrad_ref, kgrad_ref, vgrad_ref,
):
    loss_ref[...] = loss_in[...]
    qgrad_ref[...] = qgrad_in[...]
    rgrad_ref[...] = rgrad_in[...]
    rows = lastq_ref.shape[0]
    heads = lastq_ref.shape[1] // HEAD_DIM
    scale = 1.0 / HEAD_DIM**0.5
    up = grouped(up_ref, 0, heads)
    mean = jnp.sum(up.astype(F32) * grouped(out_ref, 0, heads), axis=1, keepdims=True)
    probs = probs_ref[...]
    slopes = dot_nt(up, value_ref[...])
    score_slope = (probs.astype(F32) * (slopes - mean)).astype(BF16)
    vgrad_ref[...] = dot_tn(probs, up).astype(BF16)
    lastq = dot_nn(score_slope, key_ref[...]) * scale
    for h in range(heads):
        lgrad_ref[:, h * HEAD_DIM : (h + 1) * HEAD_DIM] = lastq[h * rows : (h + 1) * rows]
    kgrad_ref[...] = (dot_tn(score_slope, grouped(lastq_ref, 0, heads)) * scale).astype(BF16)


def on_device(
    sizes, last_query, key_cache, value_cache, residual, out_weight, query_emb, lengths, positives
):
    nz, ny, nx = sizes
    rows, width = query_emb.shape
    tokens, kv_width = key_cache.shape
    groups = kv_width // HEAD_DIM
    heads = width // kv_width
    inner = CORES * ny
    passages = inner * rows
    chunk = nz // nx * rows
    wide = width + HEAD_DIM
    vmem = pl.BlockSpec(memory_space=pltpu.VMEM)
    hbm = pl.BlockSpec(memory_space=pl.ANY)
    copies = 3 * (nz - 1) + 7 * ny + 8 * (nx - 1)
    loss, query_grad, residual_grad, upstream, attended, probs = pl.pallas_call(
        functools.partial(kernel, sizes),
        out_shape=(
            jax.ShapeDtypeStruct((1, rows), F32),
            jax.ShapeDtypeStruct((rows, width), F32),
            jax.ShapeDtypeStruct((rows, width), F32),
            jax.ShapeDtypeStruct((rows, width), BF16),
            jax.ShapeDtypeStruct((rows, width), F32),
            jax.ShapeDtypeStruct((groups * heads * rows, tokens), BF16),
        ),
        in_specs=[hbm, hbm, hbm, hbm, hbm, hbm, vmem, vmem],
        out_specs=(vmem, vmem, vmem, vmem, vmem, hbm),
        scratch_shapes=[
            pltpu.VMEM((nz, rows, wide), BF16),
            pltpu.VMEM((inner, rows, wide), BF16),
            pltpu.VMEM((nx, width, width), BF16),
            pltpu.VMEM((tokens, kv_width), BF16),
            pltpu.VMEM((tokens, kv_width), BF16),
            pltpu.VMEM((rows, width), BF16),
            pltpu.VMEM((rows, width), BF16),
            pltpu.VMEM((2, rows, HEAD_DIM), jnp.int32),
            pltpu.VMEM((groups * heads * rows, tokens), F32),
            pltpu.VMEM((groups * heads * rows, tokens), BF16),
            pltpu.VMEM((nx, rows, width), BF16),
            pltpu.VMEM((nx, rows, width), BF16),
            pltpu.VMEM((nx, chunk, passages), F32),
            pltpu.VMEM((nx, chunk, passages), F32),
            pltpu.VMEM((nx, 8, passages), F32),
            pltpu.VMEM((passages, HEAD_DIM), F32),
            pltpu.VMEM((nz, 8, HEAD_DIM), F32),
            pltpu.VMEM((nx, chunk, passages), F32),
            pltpu.VMEM((nx * chunk, passages), BF16),
            pltpu.VMEM((nx, 8, HEAD_DIM), F32),
            pltpu.VMEM((ny, rows, wide), BF16),
            pltpu.VMEM((ny, rows, width), F32),
            pltpu.VMEM((ny, rows, wide), BF16),
            pltpu.VMEM((ny, rows, wide), BF16),
            pltpu.VMEM((ny, rows, wide), BF16),
            pltpu.VMEM((nx, rows, width), BF16),
            pltpu.VMEM((nz, rows, width), BF16),
            pltpu.VMEM((4, rows, width), BF16),
            pltpu.VMEM((2, rows, width), BF16),
            pltpu.VMEM((2, rows // 2, width), BF16),
            pltpu.SemaphoreType.DMA((6 + nx,)),
            pltpu.SemaphoreType.DMA((copies,)),
            pltpu.SemaphoreType.DMA((copies,)),
        ],
        compiler_params=pltpu.CompilerParams(
            collective_id=0, has_side_effects=True, vmem_limit_bytes=60 * 2**20
        ),
    )(
        last_query, key_cache, value_cache, residual, out_weight, query_emb,
        lengths, positives.reshape(1, rows),
    )
    side = heads * HEAD_DIM
    by_heads = pl.BlockSpec((rows, side), lambda g: (0, g))
    by_group = pl.BlockSpec((tokens, HEAD_DIM), lambda g: (0, g))
    line = pl.BlockSpec((1, rows), lambda g: (0, 0))
    loss, query_grad, residual_grad, lastq_grad, key_grad, value_grad = pl.pallas_call(
        backward,
        grid=(groups,),
        out_shape=(
            jax.ShapeDtypeStruct((1, rows), F32),
            jax.ShapeDtypeStruct((rows, width), F32),
            jax.ShapeDtypeStruct((rows, width), F32),
            jax.ShapeDtypeStruct((rows, width), F32),
            jax.ShapeDtypeStruct((tokens, kv_width), BF16),
            jax.ShapeDtypeStruct((tokens, kv_width), BF16),
        ),
        in_specs=[
            by_heads, by_heads, by_heads, by_group, by_group,
            pl.BlockSpec((heads * rows, tokens), lambda g: (g, 0)),
            line, by_heads, by_heads,
        ],
        out_specs=(line, by_heads, by_heads, by_heads, by_group, by_group),
        compiler_params=pltpu.CompilerParams(vmem_limit_bytes=60 * 2**20),
    )(
        last_query, upstream, attended, key_cache, value_cache, probs, loss, query_grad,
        residual_grad,
    )
    return (loss.reshape(rows), query_grad, residual_grad, lastq_grad, key_grad, value_grad)


def solution(mesh, nz=8, ny=4):
    in_specs = (
        P("dp", "mp"),
        P("dp", "mp"),
        P("dp", "mp"),
        P("dp", "mp"),
        P("mp", None),
        P("dp", "mp"),
        P("dp", None),
        P("dp"),
    )
    out_specs = (P("dp"), P("dp", "mp"), P("dp", "mp"), P("dp", "mp"), P("dp", "mp"), P("dp", "mp"))
    sizes = (nz, ny, mesh.shape["mp"])
    return jax.shard_map(
        functools.partial(on_device, sizes),
        mesh=mesh,
        in_specs=in_specs,
        out_specs=out_specs,
        check_vma=False,
    )
```

```python
import functools

import jax
import jax.numpy as jnp
from jax import lax
from jax.experimental import pallas as pl
from jax.experimental.pallas import tpu as pltpu
from jax.sharding import PartitionSpec as P

HEAD_DIM = 128
INV_TEMP = 50.0
EPSILON = 1e-06
CORES = 2
MESH = pl.DeviceIdType.MESH
F32 = jnp.float32
BF16 = jnp.bfloat16


def dot_nn(a, b):
    return lax.dot_general(a, b, (((1,), (0,)), ((), ())), preferred_element_type=F32)


def dot_nt(a, b):
    return lax.dot_general(a, b, (((1,), (1,)), ((), ())), preferred_element_type=F32)


def dot_tn(a, b):
    return lax.dot_general(a, b, (((0,), (0,)), ((), ())), preferred_element_type=F32)


def kernel(
    sizes,
    lastq_hbm, key_hbm, value_hbm, resid_hbm, weight_hbm, query_hbm, len_ref, pos_ref,
    loss_hbm, qgrad_hbm, rgrad_hbm, up_hbm, out_hbm, probs_hbm,
    q_buf, p_buf, weight, key, value, lastq, resid, ranges, attn, probs, y_part, y_recv, s_part, s_recv, sq_all, turned,
    stat, s_all, w_all, misc_all, eg_part, eg_own, eg_side, eg_out, eg_recv, slope_all, qg_part, qg_recv,
    relay, relay_half, loss_ref, qgrad_ref, rgrad_ref, up_ref, out_ref,
    load_sem, save_sem, send_sem, recv_sem,
):
    nz, ny, nx = sizes
    rows, width = query_hbm.shape
    tokens, kv_width = key_hbm.shape
    groups = kv_width // HEAD_DIM
    heads = width // kv_width
    inner = CORES * ny
    passages = inner * rows
    slots = nz // nx
    chunk = slots * rows
    scale = 1.0 / HEAD_DIM**0.5

    me = lax.axis_index("dp")
    x = lax.axis_index("mp")
    core = lax.rem(me, CORES)
    y = lax.rem(lax.div(me, CORES), ny)
    z = lax.div(me, inner)

    def place(z_at, y_at, core_at):
        return {"dp": (z_at * ny + y_at) * CORES + core_at}

    def around(at, step, size):
        return lax.rem(at + (step + size), size)

    def far_first(size):
        return sorted(range(1, size), key=lambda k: -min(k, size - k))

    xs = [around(x, k, nx) for k in range(nx)]
    ys = [around(y, k, ny) for k in range(ny)]
    zs = [around(z, k, nz) for k in range(nz)]
    twin = place(z, y, 1 - core)
    partners = [place(t, y, core) for t in zs[1:]] + [place(z, t, core) for t in ys[1:]]
    partners += [twin] + [{"mp": t} for t in xs[1:]]

    barrier = pltpu.get_barrier_semaphore()
    for partner in partners:
        pl.semaphore_signal(barrier, inc=1, device_id=partner, device_id_type=MESH)

    loads = [
        pltpu.make_async_copy(query_hbm, q_buf.at[z, :, pl.ds(0, width)], load_sem.at[0]),
        pltpu.make_async_copy(lastq_hbm, lastq, load_sem.at[1]),
        pltpu.make_async_copy(key_hbm, key, load_sem.at[2]),
        pltpu.make_async_copy(value_hbm, value, load_sem.at[3]),
        pltpu.make_async_copy(resid_hbm, resid, load_sem.at[4]),
    ]
    waits = {}
    for k in far_first(nx) + [0]:
        waits[k] = len(loads)
        columns = pl.ds(pl.multiple_of(xs[k] * width, width), width)
        loads.append(
            pltpu.make_async_copy(weight_hbm.at[:, columns], weight.at[k], load_sem.at[5 + k])
        )
    for load in loads[:4]:
        load.start()

    saves = []

    def save(source, target):
        saves.append(pltpu.make_async_copy(source, target, save_sem.at[len(saves)]))
        saves[-1].start()

    sent = []

    def push(src, dst, device):
        index = len(sent)
        copy = pltpu.make_async_remote_copy(
            src_ref=src,
            dst_ref=dst,
            send_sem=send_sem.at[index],
            recv_sem=recv_sem.at[index],
            device_id=device,
            device_id_type=MESH,
        )
        copy.start()
        sent.append(copy)
        return copy

    def exchange(src, dst):
        copies = [None] * nx
        for k in far_first(nx):
            copies[k] = push(src(k), dst.at[x], {"mp": xs[k]})
        return copies

    def received(copies, k):
        copies[k].wait_recv()
        return xs[nx - k]

    lane = lax.broadcasted_iota(jnp.int32, (rows, HEAD_DIM), 1)

    def three_parts(column):
        high = column.astype(BF16).astype(F32)
        middle = (column - high).astype(BF16).astype(F32)
        low = column - high - middle
        parts = jnp.where(lane == 0, high, jnp.where(lane == 1, middle, low))
        return jnp.where(lane < 3, parts, 0.0).astype(BF16)

    position = jnp.broadcast_to(pos_ref[...].astype(F32), (rows, rows))
    diagonal = lax.broadcasted_iota(jnp.int32, (rows, rows), 0) == lax.broadcasted_iota(
        jnp.int32, (rows, rows), 1
    )
    position = jnp.sum(jnp.where(diagonal, position, 0.0), axis=1, keepdims=True).astype(jnp.int32)
    high, low = lax.shift_right_logical(position, 6), position & 63
    digits = jnp.where(lane == 0, high, jnp.where(lane == 1, low, 0)).astype(F32).astype(BF16)
    q_buf[z, :, width:] = digits
    lengths = len_ref[...].astype(F32)
    passage = lax.broadcasted_iota(jnp.int32, (rows, rows), 0)
    which = lax.broadcasted_iota(jnp.int32, (rows, rows), 1)
    for i, before in enumerate((which < passage, which <= passage)):
        bound = jnp.sum(jnp.where(before, lengths, 0.0), axis=1, keepdims=True)
        ranges[i] = jnp.broadcast_to(bound, (rows, HEAD_DIM)).astype(jnp.int32)
    loads[0].wait()
    pl.semaphore_wait(barrier, len(partners))
    q_copies = {
        k: push(q_buf.at[z], q_buf.at[z], place(zs[k], y, core)) for k in (2, nz - 2, 1, nz - 1)
    }

    block = 16

    def softmax_rows(i, carry):
        at = pl.ds(pl.multiple_of(i * block, block), block)
        bounds = pl.ds(pl.multiple_of(lax.rem(i, rows // block) * block, block), block)
        token = lax.broadcasted_iota(jnp.int32, (block, tokens), 1)
        inside = (token >= ranges[0, bounds, :][:, :1]) & (token < ranges[1, bounds, :][:, :1])
        scores = jnp.where(inside, attn[at, :], -1e30)
        top = jnp.max(scores, axis=1, keepdims=True)
        powers = jnp.exp((scores - top) * scale)
        weights = powers * (1.0 / jnp.sum(powers, axis=1, keepdims=True))
        probs[at, :] = weights.astype(BF16)
        return carry

    for load in loads[1:4]:
        load.wait()
    for load in loads[4:]:
        load.start()
    group_rows = heads * rows
    blocks = groups * group_rows // block
    attn[...] = dot_nt(spread(lastq, groups, heads), key[...])
    lax.fori_loop(0, blocks, softmax_rows, 0, unroll=blocks)
    out = dot_nn(probs[...], value[...])
    attended = [
        out[g * group_rows + h * rows : g * group_rows + (h + 1) * rows, g * HEAD_DIM :][:, :HEAD_DIM]
        for g in range(groups)
        for h in range(heads)
    ]
    attended = jnp.concatenate(attended, axis=1)
    out_ref[...] = attended
    attended = attended.astype(BF16)

    side_width = width // 2
    sides = [slice(i * side_width, (i + 1) * side_width) for i in range(2)]

    def project(k, i):
        if i == 0:
            loads[waits[k]].wait()
        y_part[k, :, sides[i]] = dot_nn(attended, weight[k, :, sides[i]]).astype(BF16)
        return y_part.at[k, :, pl.ds(i * side_width, side_width)]

    y_copies = []
    for i in range(2):
        target = y_recv.at[:, :, pl.ds(i * side_width, side_width)]
        y_copies.append(exchange(lambda k: project(k, i), target))
    save(probs, probs_hbm)
    save(out_ref, out_hbm)
    loads[4].wait()
    loads[waits[0]].wait()
    hiddens = [
        dot_nn(attended, weight[0, :, part]) + resid[:, part].astype(F32) for part in sides
    ]
    half = rows // 2
    onward = []
    for k, first in ((2, 0), (nz - 2, half)):
        q_copies[k].wait_recv()
        step = 1 if k == 2 else nz - 1
        part = q_buf.at[zs[nz - k]]
        onward.append(push(part, part, place(zs[step], y, core)))
        part = q_buf.at[zs[nz - k], pl.ds(first, half)]
        onward.append(push(part, part, place(zs[k], y, core)))

    own = core * ny + y
    spans = (pl.ds(0, side_width), pl.ds(side_width, side_width + HEAD_DIM))
    p_copies = [[None] * ny, [None] * ny]
    passed = [[], []]
    for i, part in enumerate(sides):
        for k in range(1, nx):
            t = received(y_copies[i], k)
            hiddens[i] = hiddens[i] + y_recv[t, :, part].astype(F32)
        p_buf[own, :, part] = hiddens[i].astype(BF16)
        if i == 1:
            squares = [jnp.sum(hidden * hidden, axis=1, keepdims=True) for hidden in hiddens]
            p_buf[own, :, width:] = three_parts(squares[0] + squares[1])
        block_at = p_buf.at[own, :, spans[i]]
        for k in far_first(ny):
            p_copies[i][k] = push(block_at, block_at, place(z, ys[k], core))
        passed[i].append(push(block_at, block_at, twin))
    for i in range(2):
        for k in sorted(range(1, ny), key=lambda k: min(k, ny - k)):
            p_copies[i][k].wait_recv()
            block_at = p_buf.at[core * ny + ys[ny - k], :, spans[i]]
            passed[i].append(push(block_at, block_at, twin))
    for copy in [q_copies[1], q_copies[nz - 1]] + onward:
        copy.wait_recv()

    def partial_scores(t, i):
        part = q_buf[pl.ds(t * slots, slots), :, sides[i]].reshape(chunk, side_width)
        return dot_nt(part, p_buf[:, :, sides[i]].reshape(passages, side_width))

    for copy in passed[0]:
        copy.wait_recv()
    for k in range(nx):
        s_part[k] = partial_scores(xs[k], 0)
    for copy in passed[1]:
        copy.wait_recv()

    def send_scores(k):
        s_part[k] += partial_scores(xs[k], 1)
        return s_part.at[k]

    unit = (lax.broadcasted_iota(jnp.int32, (8, HEAD_DIM), 1) < 3).astype(F32).astype(BF16)
    sq_all[x] = dot_nt(unit, p_buf[:, :, width:].reshape(passages, HEAD_DIM))
    sq_copies = exchange(lambda k: sq_all.at[x], sq_all)
    s_copies = exchange(send_scores, s_recv)
    scores = s_part[0] + partial_scores(x, 1)
    squares = sq_all[x]
    for k in range(1, nx):
        squares = squares + sq_all[received(sq_copies, k)]
    norms = jnp.sqrt(squares[:1] + EPSILON)
    turned[...] = jnp.broadcast_to(norms, (HEAD_DIM, passages)).T
    norm = turned[pl.ds(pl.multiple_of(own * rows, rows), rows), :][:, :1]
    embs = [hidden / norm for hidden in hiddens]
    digits = q_buf[:, :, width:].reshape(nz * rows, HEAD_DIM).astype(F32)
    positive = (digits[:, 0:1] * 64.0 + digits[:, 1:2]).astype(jnp.int32)
    index = lax.broadcasted_iota(jnp.int32, (nz * rows, passages), 1)
    slot = lax.div(index, rows)
    cell = lax.rem(slot, ny) * CORES + lax.div(slot, ny)
    passage_of = (z * inner + cell) * rows + lax.rem(index, rows)
    match = positive == passage_of
    for k in range(1, nx):
        scores = scores + s_recv[received(s_copies, k)]
    scores = scores * (INV_TEMP / norms)
    s_all[x] = scores
    all_copies = exchange(lambda k: s_all.at[x], s_all)

    top = jnp.max(scores, axis=1, keepdims=True)
    total = jnp.sum(jnp.exp(scores - top), axis=1, keepdims=True)
    own_digits = q_buf[pl.ds(x * slots, slots), :, width:].reshape(chunk, HEAD_DIM).astype(F32)
    own_positive = (own_digits[:, 0:1] * 64.0 + own_digits[:, 1:2]).astype(jnp.int32)
    own_match = own_positive == passage_of[:chunk]
    hit = jnp.sum(jnp.where(own_match, scores, 0.0), axis=1, keepdims=True)
    chunk_lane = lax.broadcasted_iota(jnp.int32, (chunk, HEAD_DIM), 1)
    columns = jnp.where(chunk_lane == 0, top, jnp.where(chunk_lane == 1, total, hit))
    stat[z] = jnp.concatenate([columns] * (HEAD_DIM // chunk), axis=0).T[:8]
    stat_copies = [push(stat.at[z], stat.at[z], place(zs[k], y, core)) for k in far_first(nz)]
    for copy in stat_copies:
        copy.wait_recv()
    every = stat[...]
    top = jnp.max(every[:, 0:1], axis=0)
    total = jnp.sum(every[:, 1:2] * jnp.exp(every[:, 0:1] - top[None]), axis=0)
    lse = top + jnp.log(total)
    loss = lse - jnp.sum(every[:, 2:3], axis=0)
    line = lax.broadcasted_iota(jnp.int32, (8, HEAD_DIM), 0)
    misc_all[x] = jnp.where(line == 0, lse, loss)
    misc_copies = exchange(lambda k: misc_all.at[x], misc_all)
    for k in range(1, nx):
        received(all_copies, k)
    for k in range(1, nx):
        received(misc_copies, k)
    losses = misc_all[lax.div(z, slots)][1:2]
    own_loss = losses[:, :rows]
    for k in range(1, slots):
        own_loss = jnp.where(lax.rem(z, slots) == k, losses[:, k * rows : (k + 1) * rows], own_loss)
    loss_ref[...] = own_loss
    save(loss_ref, loss_hbm)

    lines = [misc_all[t][:1] for t in range(nx)] + [jnp.zeros((HEAD_DIM - nx, HEAD_DIM), F32)]
    turned_lse = jnp.concatenate(lines, axis=0).T
    lse = jnp.concatenate([turned_lse[:chunk, t : t + 1] for t in range(nx)], axis=0)
    scores = s_all[...].reshape(nx * chunk, passages)
    pairs = jnp.exp(scores - lse) - match.astype(F32)
    along = jnp.sum(pairs.astype(BF16).astype(F32) * scores, axis=0, keepdims=True)
    w_all[...] = pairs.astype(BF16)
    turned[...] = jnp.broadcast_to(along, (HEAD_DIM, passages)).T

    share = ny * rows
    spans = ((0, HEAD_DIM + side_width), (HEAD_DIM + side_width, side_width))

    def emb_share(core_at, i):
        part = w_all[:, pl.ds(pl.multiple_of(core_at * share, share), share)]
        queries = q_buf[:, :, i * side_width : (i + 1) * side_width].reshape(nz * rows, side_width)
        return (dot_tn(part, queries) * INV_TEMP).reshape(ny, rows, side_width)

    def along_of(core_at, y_at):
        first = pl.multiple_of((core_at * ny + y_at) * rows, rows)
        return turned[pl.ds(first, rows), :][:, :1]

    def columns_of(i):
        return slice(HEAD_DIM + i * side_width, HEAD_DIM + (i + 1) * side_width)

    def span(buf, i):
        return buf.at[:, pl.ds(*spans[i])] if len(buf.shape) == 2 else buf.at[:, :, pl.ds(*spans[i])]

    for j in range(ny):
        eg_part[j, :, :HEAD_DIM] = three_parts(along_of(1 - core, j))
    side_copies = []
    for i in range(2):
        eg_part[:, :, columns_of(i)] = emb_share(1 - core, i).astype(BF16)
        side_copies.append(push(span(eg_part, i), span(eg_side, i), twin))

    pairs = (pairs * (INV_TEMP / norms)).astype(BF16)
    grads = dot_nn(pairs, p_buf[:, :, :width].reshape(passages, width))
    qg_part[...] = grads.astype(BF16).reshape(nz, rows, width)
    one, last, two, other = 1, nz - 1, 2, nz - 2
    far = [push(qg_part.at[zs[4], pl.ds(0, half)], relay_half.at[0], place(zs[other], y, core))]
    far.append(push(qg_part.at[zs[4], pl.ds(half, half)], relay_half.at[1], place(zs[two], y, core)))
    far.append(push(qg_part.at[zs[nz - 3]], relay.at[0], place(zs[last], y, core)))
    far.append(push(qg_part.at[zs[3]], relay.at[1], place(zs[one], y, core)))
    near = [push(qg_part.at[zs[one]], qg_recv.at[0], place(zs[one], y, core))]
    near.append(push(qg_part.at[zs[last]], qg_recv.at[1], place(zs[last], y, core)))
    for i in range(2):
        eg_own[:, :, i * side_width : (i + 1) * side_width] = emb_share(core, i)

    def emb_sum(y_at, i):
        own_part = eg_own[y_at, :, i * side_width : (i + 1) * side_width]
        return own_part + eg_side[y_at, :, columns_of(i)].astype(F32)

    def along_parts(buf, at):
        parts = buf[at, :, :HEAD_DIM].astype(F32)
        return parts[:, 0:1] + parts[:, 1:2] + parts[:, 2:3]

    eg_copies = []
    for i in range(2):
        side_copies[i].wait_recv()
        copies = [None] * ny
        for k in far_first(ny):
            eg_out[k, :, columns_of(i)] = emb_sum(ys[k], i).astype(BF16)
            if i == 0:
                along = along_of(core, ys[k]) + along_parts(eg_side, ys[k])
                eg_out[k, :, :HEAD_DIM] = three_parts(along)
            copies[k] = push(
                span(eg_out.at[k], i), span(eg_recv.at[y], i), place(z, ys[k], core)
            )
        eg_copies.append(copies)
    along = along_of(core, y) + along_parts(eg_side, y)
    slope_copies = []
    slopes = []
    for i in range(2):
        emb_grad = emb_sum(y, i)
        for k in range(1, ny):
            eg_copies[i][k].wait_recv()
            emb_grad = emb_grad + eg_recv[ys[ny - k], :, columns_of(i)].astype(F32)
            if i == 0:
                along = along + along_parts(eg_recv, ys[ny - k])
        part = slice(i * side_width, (i + 1) * side_width)
        residual_grad = (emb_grad - embs[i] * along) / norm
        rgrad_ref[:, part] = residual_grad
        slopes.append(residual_grad.astype(BF16))
        slope_all[x, :, part] = slopes[-1]
        place_at = slope_all.at[:, :, pl.ds(i * side_width, side_width)]
        slope_copies.append(exchange(lambda k: place_at.at[x], place_at))

    save(rgrad_ref, rgrad_hbm)
    for copy in far:
        copy.wait_recv()
    for i, k in enumerate((other, two)):
        total = qg_part[zs[k]].astype(F32) + relay[i].astype(F32)
        extra = relay_half[i].astype(F32)
        parts = [total[:half], total[half:]]
        parts[i] = parts[i] + extra
        relay[i] = jnp.concatenate(parts, axis=0).astype(BF16)
        near.append(push(relay.at[i], qg_recv.at[2 + i], place(zs[k], y, core)))
    upstream = dot_nt(jnp.concatenate(slopes, axis=1), weight[0])
    for i in range(2):
        part = slice(i * side_width, (i + 1) * side_width)
        for k in sorted(range(1, nx), key=lambda k: min(k, nx - k)):
            t = received(slope_copies[i], k)
            upstream = upstream + dot_nt(slope_all[t, :, part], weight[nx - k, :, part])
    up_ref[...] = upstream.astype(BF16)
    save(up_ref, up_hbm)

    query_grad = qg_part[z].astype(F32)
    for i, copy in enumerate(near):
        copy.wait_recv()
        query_grad = query_grad + qg_recv[i].astype(F32)
    qgrad_ref[...] = query_grad
    save(qgrad_ref, qgrad_hbm)
    for copy in sent:
        copy.wait_send()
    for copy in saves:
        copy.wait()


def grouped(source, g, heads):
    first = g * heads
    return jnp.concatenate(
        [source[:, (first + h) * HEAD_DIM : (first + h + 1) * HEAD_DIM] for h in range(heads)],
        axis=0,
    )


def spread(source, groups, heads):
    parts = [grouped(source, g, heads) for g in range(groups)]
    empty = jnp.zeros_like(parts[0])
    lines = [
        jnp.concatenate([part if i == g else empty for i in range(groups)], axis=1)
        for g, part in enumerate(parts)
    ]
    return jnp.concatenate(lines, axis=0)


def backward(
    lastq_ref, up_ref, out_ref, key_ref, value_ref, probs_ref, loss_in, qgrad_in, rgrad_in,
    loss_ref, qgrad_ref, rgrad_ref, lgrad_ref, kgrad_ref, vgrad_ref,
):
    loss_ref[...] = loss_in[...]
    qgrad_ref[...] = qgrad_in[...]
    rgrad_ref[...] = rgrad_in[...]
    rows = lastq_ref.shape[0]
    heads = lastq_ref.shape[1] // HEAD_DIM
    scale = 1.0 / HEAD_DIM**0.5
    up = grouped(up_ref, 0, heads)
    mean = jnp.sum(up.astype(F32) * grouped(out_ref, 0, heads), axis=1, keepdims=True)
    probs = probs_ref[...]
    slopes = dot_nt(up, value_ref[...])
    score_slope = (probs.astype(F32) * (slopes - mean)).astype(BF16)
    vgrad_ref[...] = dot_tn(probs, up).astype(BF16)
    lastq = dot_nn(score_slope, key_ref[...]) * scale
    for h in range(heads):
        lgrad_ref[:, h * HEAD_DIM : (h + 1) * HEAD_DIM] = lastq[h * rows : (h + 1) * rows]
    kgrad_ref[...] = (dot_tn(score_slope, grouped(lastq_ref, 0, heads)) * scale).astype(BF16)


def on_device(
    sizes, last_query, key_cache, value_cache, residual, out_weight, query_emb, lengths, positives
):
    nz, ny, nx = sizes
    rows, width = query_emb.shape
    tokens, kv_width = key_cache.shape
    groups = kv_width // HEAD_DIM
    heads = width // kv_width
    inner = CORES * ny
    passages = inner * rows
    chunk = nz // nx * rows
    wide = width + HEAD_DIM
    vmem = pl.BlockSpec(memory_space=pltpu.VMEM)
    hbm = pl.BlockSpec(memory_space=pl.ANY)
    copies = 3 * (nz - 1) + 7 * ny + 8 * (nx - 1)
    loss, query_grad, residual_grad, upstream, attended, probs = pl.pallas_call(
        functools.partial(kernel, sizes),
        out_shape=(
            jax.ShapeDtypeStruct((1, rows), F32),
            jax.ShapeDtypeStruct((rows, width), F32),
            jax.ShapeDtypeStruct((rows, width), F32),
            jax.ShapeDtypeStruct((rows, width), BF16),
            jax.ShapeDtypeStruct((rows, width), F32),
            jax.ShapeDtypeStruct((groups * heads * rows, tokens), BF16),
        ),
        in_specs=[hbm, hbm, hbm, hbm, hbm, hbm, vmem, vmem],
        out_specs=(hbm,) * 6,
        scratch_shapes=[
            pltpu.VMEM((nz, rows, wide), BF16),
            pltpu.VMEM((inner, rows, wide), BF16),
            pltpu.VMEM((nx, width, width), BF16),
            pltpu.VMEM((tokens, kv_width), BF16),
            pltpu.VMEM((tokens, kv_width), BF16),
            pltpu.VMEM((rows, width), BF16),
            pltpu.VMEM((rows, width), BF16),
            pltpu.VMEM((2, rows, HEAD_DIM), jnp.int32),
            pltpu.VMEM((groups * heads * rows, tokens), F32),
            pltpu.VMEM((groups * heads * rows, tokens), BF16),
            pltpu.VMEM((nx, rows, width), BF16),
            pltpu.VMEM((nx, rows, width), BF16),
            pltpu.VMEM((nx, chunk, passages), F32),
            pltpu.VMEM((nx, chunk, passages), F32),
            pltpu.VMEM((nx, 8, passages), F32),
            pltpu.VMEM((passages, HEAD_DIM), F32),
            pltpu.VMEM((nz, 8, HEAD_DIM), F32),
            pltpu.VMEM((nx, chunk, passages), F32),
            pltpu.VMEM((nx * chunk, passages), BF16),
            pltpu.VMEM((nx, 8, HEAD_DIM), F32),
            pltpu.VMEM((ny, rows, wide), BF16),
            pltpu.VMEM((ny, rows, width), F32),
            pltpu.VMEM((ny, rows, wide), BF16),
            pltpu.VMEM((ny, rows, wide), BF16),
            pltpu.VMEM((ny, rows, wide), BF16),
            pltpu.VMEM((nx, rows, width), BF16),
            pltpu.VMEM((nz, rows, width), BF16),
            pltpu.VMEM((4, rows, width), BF16),
            pltpu.VMEM((2, rows, width), BF16),
            pltpu.VMEM((2, rows // 2, width), BF16),
            pltpu.VMEM((1, rows), F32),
            pltpu.VMEM((rows, width), F32),
            pltpu.VMEM((rows, width), F32),
            pltpu.VMEM((rows, width), BF16),
            pltpu.VMEM((rows, width), F32),
            pltpu.SemaphoreType.DMA((5 + nx,)),
            pltpu.SemaphoreType.DMA((6,)),
            pltpu.SemaphoreType.DMA((copies,)),
            pltpu.SemaphoreType.DMA((copies,)),
        ],
        compiler_params=pltpu.CompilerParams(
            collective_id=0, has_side_effects=True, vmem_limit_bytes=60 * 2**20
        ),
    )(
        last_query, key_cache, value_cache, residual, out_weight, query_emb,
        lengths, positives.reshape(1, rows),
    )
    side = heads * HEAD_DIM
    by_heads = pl.BlockSpec((rows, side), lambda g: (0, g))
    by_group = pl.BlockSpec((tokens, HEAD_DIM), lambda g: (0, g))
    line = pl.BlockSpec((1, rows), lambda g: (0, 0))
    loss, query_grad, residual_grad, lastq_grad, key_grad, value_grad = pl.pallas_call(
        backward,
        grid=(groups,),
        out_shape=(
            jax.ShapeDtypeStruct((1, rows), F32),
            jax.ShapeDtypeStruct((rows, width), F32),
            jax.ShapeDtypeStruct((rows, width), F32),
            jax.ShapeDtypeStruct((rows, width), F32),
            jax.ShapeDtypeStruct((tokens, kv_width), BF16),
            jax.ShapeDtypeStruct((tokens, kv_width), BF16),
        ),
        in_specs=[
            by_heads, by_heads, by_heads, by_group, by_group,
            pl.BlockSpec((heads * rows, tokens), lambda g: (g, 0)),
            line, by_heads, by_heads,
        ],
        out_specs=(line, by_heads, by_heads, by_heads, by_group, by_group),
        compiler_params=pltpu.CompilerParams(vmem_limit_bytes=60 * 2**20),
    )(
        last_query, upstream, attended, key_cache, value_cache, probs, loss, query_grad,
        residual_grad,
    )
    return (loss.reshape(rows), query_grad, residual_grad, lastq_grad, key_grad, value_grad)


def solution(mesh, nz=8, ny=4):
    in_specs = (
        P("dp", "mp"),
        P("dp", "mp"),
        P("dp", "mp"),
        P("dp", "mp"),
        P("mp", None),
        P("dp", "mp"),
        P("dp", None),
        P("dp"),
    )
    out_specs = (P("dp"), P("dp", "mp"), P("dp", "mp"), P("dp", "mp"), P("dp", "mp"), P("dp", "mp"))
    sizes = (nz, ny, mesh.shape["mp"])
    return jax.shard_map(
        functools.partial(on_device, sizes),
        mesh=mesh,
        in_specs=in_specs,
        out_specs=out_specs,
        check_vma=False,
    )
```

```python
import functools

import jax
import jax.numpy as jnp
from jax import lax
from jax.experimental import pallas as pl
from jax.experimental.pallas import tpu as pltpu
from jax.sharding import PartitionSpec as P

HEAD_DIM = 128
INV_TEMP = 50.0
EPSILON = 1e-06
CORES = 2
MESH = pl.DeviceIdType.MESH
F32 = jnp.float32
BF16 = jnp.bfloat16


def dot_nn(a, b):
    return lax.dot_general(a, b, (((1,), (0,)), ((), ())), preferred_element_type=F32)


def dot_nt(a, b):
    return lax.dot_general(a, b, (((1,), (1,)), ((), ())), preferred_element_type=F32)


def dot_tn(a, b):
    return lax.dot_general(a, b, (((0,), (0,)), ((), ())), preferred_element_type=F32)


def kernel(
    sizes,
    lastq_hbm, key_hbm, value_hbm, resid_hbm, weight_hbm, query_hbm, len_ref, pos_ref,
    loss_hbm, qgrad_hbm, rgrad_hbm, up_hbm, out_hbm, probs_hbm,
    q_buf, p_buf, weight, key, value, lastq, resid, ranges, attn, probs, y_part, y_recv, s_part, s_recv, sq_all, turned,
    stat, s_all, w_all, misc_all, eg_part, eg_own, eg_side, eg_out, eg_recv, slope_all, qg_part, qg_recv,
    relay, relay_half, loss_ref, qgrad_ref, rgrad_ref, up_ref, out_ref,
    load_sem, save_sem, send_sem, recv_sem,
):
    nz, ny, nx = sizes
    rows, width = query_hbm.shape
    tokens, kv_width = key_hbm.shape
    groups = kv_width // HEAD_DIM
    heads = width // kv_width
    inner = CORES * ny
    passages = inner * rows
    slots = nz // nx
    chunk = slots * rows
    scale = 1.0 / HEAD_DIM**0.5

    me = lax.axis_index("dp")
    x = lax.axis_index("mp")
    core = lax.rem(me, CORES)
    y = lax.rem(lax.div(me, CORES), ny)
    z = lax.div(me, inner)

    def place(z_at, y_at, core_at):
        return {"dp": (z_at * ny + y_at) * CORES + core_at}

    def around(at, step, size):
        return lax.rem(at + (step + size), size)

    def far_first(size):
        return sorted(range(1, size), key=lambda k: -min(k, size - k))

    xs = [around(x, k, nx) for k in range(nx)]
    ys = [around(y, k, ny) for k in range(ny)]
    zs = [around(z, k, nz) for k in range(nz)]
    twin = place(z, y, 1 - core)
    partners = [place(t, y, core) for t in zs[1:]] + [place(z, t, core) for t in ys[1:]]
    partners += [twin] + [{"mp": t} for t in xs[1:]]

    loads = [
        pltpu.make_async_copy(query_hbm, q_buf.at[z, :, pl.ds(0, width)], load_sem.at[0]),
        pltpu.make_async_copy(lastq_hbm, lastq, load_sem.at[1]),
        pltpu.make_async_copy(key_hbm, key, load_sem.at[2]),
        pltpu.make_async_copy(value_hbm, value, load_sem.at[3]),
        pltpu.make_async_copy(resid_hbm, resid, load_sem.at[4]),
    ]
    waits = {}
    for k in far_first(nx) + [0]:
        waits[k] = len(loads)
        columns = pl.ds(pl.multiple_of(xs[k] * width, width), width)
        loads.append(
            pltpu.make_async_copy(weight_hbm.at[:, columns], weight.at[k], load_sem.at[5 + k])
        )
    for load in loads[:4]:
        load.start()

    barrier = pltpu.get_barrier_semaphore()
    for partner in partners:
        pl.semaphore_signal(barrier, inc=1, device_id=partner, device_id_type=MESH)

    saves = []

    def save(source, target):
        saves.append(pltpu.make_async_copy(source, target, save_sem.at[len(saves)]))
        saves[-1].start()

    sent = []

    def push(src, dst, device):
        index = len(sent)
        copy = pltpu.make_async_remote_copy(
            src_ref=src,
            dst_ref=dst,
            send_sem=send_sem.at[index],
            recv_sem=recv_sem.at[index],
            device_id=device,
            device_id_type=MESH,
        )
        copy.start()
        sent.append(copy)
        return copy

    def exchange(src, dst):
        copies = [None] * nx
        for k in far_first(nx):
            copies[k] = push(src(k), dst.at[x], {"mp": xs[k]})
        return copies

    def received(copies, k):
        copies[k].wait_recv()
        return xs[nx - k]

    lane = lax.broadcasted_iota(jnp.int32, (rows, HEAD_DIM), 1)

    def three_parts(column):
        high = column.astype(BF16).astype(F32)
        middle = (column - high).astype(BF16).astype(F32)
        low = column - high - middle
        parts = jnp.where(lane == 0, high, jnp.where(lane == 1, middle, low))
        return jnp.where(lane < 3, parts, 0.0).astype(BF16)

    position = jnp.broadcast_to(pos_ref[...].astype(F32), (rows, rows))
    diagonal = lax.broadcasted_iota(jnp.int32, (rows, rows), 0) == lax.broadcasted_iota(
        jnp.int32, (rows, rows), 1
    )
    position = jnp.sum(jnp.where(diagonal, position, 0.0), axis=1, keepdims=True).astype(jnp.int32)
    high, low = lax.shift_right_logical(position, 6), position & 63
    digits = jnp.where(lane == 0, high, jnp.where(lane == 1, low, 0)).astype(F32).astype(BF16)
    q_buf[z, :, width:] = digits
    lengths = len_ref[...].astype(F32)
    passage = lax.broadcasted_iota(jnp.int32, (rows, rows), 0)
    which = lax.broadcasted_iota(jnp.int32, (rows, rows), 1)
    for i, before in enumerate((which < passage, which <= passage)):
        bound = jnp.sum(jnp.where(before, lengths, 0.0), axis=1, keepdims=True)
        ranges[i] = jnp.broadcast_to(bound, (rows, HEAD_DIM)).astype(jnp.int32)
    loads[0].wait()
    pl.semaphore_wait(barrier, len(partners))
    q_copies = {
        k: push(q_buf.at[z], q_buf.at[z], place(zs[k], y, core)) for k in (2, nz - 2, 1, nz - 1)
    }

    block = 16

    def softmax_rows(i, carry):
        at = pl.ds(pl.multiple_of(i * block, block), block)
        bounds = pl.ds(pl.multiple_of(lax.rem(i, rows // block) * block, block), block)
        token = lax.broadcasted_iota(jnp.int32, (block, tokens), 1)
        inside = (token >= ranges[0, bounds, :][:, :1]) & (token < ranges[1, bounds, :][:, :1])
        scores = jnp.where(inside, attn[at, :], -1e30)
        top = jnp.max(scores, axis=1, keepdims=True)
        powers = jnp.exp((scores - top) * scale)
        weights = powers * (1.0 / jnp.sum(powers, axis=1, keepdims=True))
        probs[at, :] = weights.astype(BF16)
        return carry

    for load in loads[1:4]:
        load.wait()
    for load in loads[4:]:
        load.start()
    group_rows = heads * rows
    blocks = groups * group_rows // block
    attn[...] = dot_nt(spread(lastq, groups, heads), key[...])
    lax.fori_loop(0, blocks, softmax_rows, 0, unroll=blocks)
    out = dot_nn(probs[...], value[...])
    attended = [
        out[g * group_rows + h * rows : g * group_rows + (h + 1) * rows, g * HEAD_DIM :][:, :HEAD_DIM]
        for g in range(groups)
        for h in range(heads)
    ]
    attended = jnp.concatenate(attended, axis=1)
    out_ref[...] = attended
    attended = attended.astype(BF16)

    side_width = width // 2
    sides = [slice(i * side_width, (i + 1) * side_width) for i in range(2)]

    def project(k, i):
        if i == 0:
            loads[waits[k]].wait()
        y_part[k, :, sides[i]] = dot_nn(attended, weight[k, :, sides[i]]).astype(BF16)
        return y_part.at[k, :, pl.ds(i * side_width, side_width)]

    y_copies = []
    for i in range(2):
        target = y_recv.at[:, :, pl.ds(i * side_width, side_width)]
        y_copies.append(exchange(lambda k: project(k, i), target))
    save(probs, probs_hbm)
    save(out_ref, out_hbm)
    loads[4].wait()
    loads[waits[0]].wait()
    hiddens = [
        dot_nn(attended, weight[0, :, part]) + resid[:, part].astype(F32) for part in sides
    ]
    half = rows // 2
    onward = []
    for k, first in ((2, 0), (nz - 2, half)):
        q_copies[k].wait_recv()
        step = 1 if k == 2 else nz - 1
        part = q_buf.at[zs[nz - k]]
        onward.append(push(part, part, place(zs[step], y, core)))
        part = q_buf.at[zs[nz - k], pl.ds(first, half)]
        onward.append(push(part, part, place(zs[k], y, core)))

    own = core * ny + y
    spans = (pl.ds(0, side_width), pl.ds(side_width, side_width + HEAD_DIM))
    p_copies = [[None] * ny, [None] * ny]
    passed = [[], []]
    for i, part in enumerate(sides):
        for k in range(1, nx):
            t = received(y_copies[i], k)
            hiddens[i] = hiddens[i] + y_recv[t, :, part].astype(F32)
        p_buf[own, :, part] = hiddens[i].astype(BF16)
        if i == 1:
            squares = [jnp.sum(hidden * hidden, axis=1, keepdims=True) for hidden in hiddens]
            p_buf[own, :, width:] = three_parts(squares[0] + squares[1])
        block_at = p_buf.at[own, :, spans[i]]
        for k in far_first(ny):
            p_copies[i][k] = push(block_at, block_at, place(z, ys[k], core))
        passed[i].append(push(block_at, block_at, twin))
    for i in range(2):
        for k in sorted(range(1, ny), key=lambda k: min(k, ny - k)):
            p_copies[i][k].wait_recv()
            block_at = p_buf.at[core * ny + ys[ny - k], :, spans[i]]
            passed[i].append(push(block_at, block_at, twin))
    for copy in [q_copies[1], q_copies[nz - 1]] + onward:
        copy.wait_recv()

    def partial_scores(t, i):
        part = q_buf[pl.ds(t * slots, slots), :, sides[i]].reshape(chunk, side_width)
        return dot_nt(part, p_buf[:, :, sides[i]].reshape(passages, side_width))

    for copy in passed[0]:
        copy.wait_recv()
    for k in range(nx):
        s_part[k] = partial_scores(xs[k], 0)
    for copy in passed[1]:
        copy.wait_recv()

    def send_scores(k):
        s_part[k] += partial_scores(xs[k], 1)
        return s_part.at[k]

    unit = (lax.broadcasted_iota(jnp.int32, (8, HEAD_DIM), 1) < 3).astype(F32).astype(BF16)
    sq_all[x] = dot_nt(unit, p_buf[:, :, width:].reshape(passages, HEAD_DIM))
    sq_copies = exchange(lambda k: sq_all.at[x], sq_all)
    s_copies = exchange(send_scores, s_recv)
    scores = s_part[0] + partial_scores(x, 1)
    squares = sq_all[x]
    for k in range(1, nx):
        squares = squares + sq_all[received(sq_copies, k)]
    norms = jnp.sqrt(squares[:1] + EPSILON)
    turned[...] = jnp.broadcast_to(norms, (HEAD_DIM, passages)).T
    norm = turned[pl.ds(pl.multiple_of(own * rows, rows), rows), :][:, :1]
    embs = [hidden / norm for hidden in hiddens]
    digits = q_buf[:, :, width:].reshape(nz * rows, HEAD_DIM).astype(F32)
    positive = (digits[:, 0:1] * 64.0 + digits[:, 1:2]).astype(jnp.int32)
    index = lax.broadcasted_iota(jnp.int32, (nz * rows, passages), 1)
    slot = lax.div(index, rows)
    cell = lax.rem(slot, ny) * CORES + lax.div(slot, ny)
    passage_of = (z * inner + cell) * rows + lax.rem(index, rows)
    match = positive == passage_of
    for k in range(1, nx):
        scores = scores + s_recv[received(s_copies, k)]
    scores = scores * (INV_TEMP / norms)

    top = jnp.max(scores, axis=1, keepdims=True)
    total = jnp.sum(jnp.exp(scores - top), axis=1, keepdims=True)
    own_digits = q_buf[pl.ds(x * slots, slots), :, width:].reshape(chunk, HEAD_DIM).astype(F32)
    own_positive = (own_digits[:, 0:1] * 64.0 + own_digits[:, 1:2]).astype(jnp.int32)
    own_match = own_positive == passage_of[:chunk]
    hit = jnp.sum(jnp.where(own_match, scores, 0.0), axis=1, keepdims=True)
    chunk_lane = lax.broadcasted_iota(jnp.int32, (chunk, HEAD_DIM), 1)
    columns = jnp.where(chunk_lane == 0, top, jnp.where(chunk_lane == 1, total, hit))
    stat[z] = jnp.concatenate([columns] * (HEAD_DIM // chunk), axis=0).T[:8]
    stat_copies = [push(stat.at[z], stat.at[z], place(zs[k], y, core)) for k in far_first(nz)]
    s_all[x] = scores
    all_copies = exchange(lambda k: s_all.at[x], s_all)
    for copy in stat_copies:
        copy.wait_recv()
    every = stat[...]
    top = jnp.max(every[:, 0:1], axis=0)
    total = jnp.sum(every[:, 1:2] * jnp.exp(every[:, 0:1] - top[None]), axis=0)
    lse = top + jnp.log(total)
    loss = lse - jnp.sum(every[:, 2:3], axis=0)
    line = lax.broadcasted_iota(jnp.int32, (8, HEAD_DIM), 0)
    misc_all[x] = jnp.where(line == 0, lse, loss)
    misc_copies = exchange(lambda k: misc_all.at[x], misc_all)
    for k in range(1, nx):
        received(all_copies, k)
    for k in range(1, nx):
        received(misc_copies, k)
    losses = misc_all[lax.div(z, slots)][1:2]
    own_loss = losses[:, :rows]
    for k in range(1, slots):
        own_loss = jnp.where(lax.rem(z, slots) == k, losses[:, k * rows : (k + 1) * rows], own_loss)
    loss_ref[...] = own_loss
    save(loss_ref, loss_hbm)

    lines = [misc_all[t][:1] for t in range(nx)] + [jnp.zeros((HEAD_DIM - nx, HEAD_DIM), F32)]
    turned_lse = jnp.concatenate(lines, axis=0).T
    lse = jnp.concatenate([turned_lse[:chunk, t : t + 1] for t in range(nx)], axis=0)
    scores = s_all[...].reshape(nx * chunk, passages)
    pairs = jnp.exp(scores - lse) - match.astype(F32)
    along = jnp.sum(pairs.astype(BF16).astype(F32) * scores, axis=0, keepdims=True)
    w_all[...] = pairs.astype(BF16)
    turned[...] = jnp.broadcast_to(along, (HEAD_DIM, passages)).T

    share = ny * rows
    spans = ((0, HEAD_DIM + side_width), (HEAD_DIM + side_width, side_width))

    def emb_share(core_at, i):
        part = w_all[:, pl.ds(pl.multiple_of(core_at * share, share), share)]
        queries = q_buf[:, :, i * side_width : (i + 1) * side_width].reshape(nz * rows, side_width)
        return (dot_tn(part, queries) * INV_TEMP).reshape(ny, rows, side_width)

    def along_of(core_at, y_at):
        first = pl.multiple_of((core_at * ny + y_at) * rows, rows)
        return turned[pl.ds(first, rows), :][:, :1]

    def columns_of(i):
        return slice(HEAD_DIM + i * side_width, HEAD_DIM + (i + 1) * side_width)

    def span(buf, i):
        return buf.at[:, pl.ds(*spans[i])] if len(buf.shape) == 2 else buf.at[:, :, pl.ds(*spans[i])]

    for j in range(ny):
        eg_part[j, :, :HEAD_DIM] = three_parts(along_of(1 - core, j))
    side_copies = []
    for i in range(2):
        eg_part[:, :, columns_of(i)] = emb_share(1 - core, i).astype(BF16)
        side_copies.append(push(span(eg_part, i), span(eg_side, i), twin))

    pairs = (pairs * (INV_TEMP / norms)).astype(BF16)
    grads = dot_nn(pairs, p_buf[:, :, :width].reshape(passages, width))
    qg_part[...] = grads.astype(BF16).reshape(nz, rows, width)
    one, last, two, other = 1, nz - 1, 2, nz - 2
    far = [push(qg_part.at[zs[4], pl.ds(0, half)], relay_half.at[0], place(zs[other], y, core))]
    far.append(push(qg_part.at[zs[4], pl.ds(half, half)], relay_half.at[1], place(zs[two], y, core)))
    far.append(push(qg_part.at[zs[nz - 3]], relay.at[0], place(zs[last], y, core)))
    far.append(push(qg_part.at[zs[3]], relay.at[1], place(zs[one], y, core)))
    near = [push(qg_part.at[zs[one]], qg_recv.at[0], place(zs[one], y, core))]
    near.append(push(qg_part.at[zs[last]], qg_recv.at[1], place(zs[last], y, core)))
    for i in range(2):
        eg_own[:, :, i * side_width : (i + 1) * side_width] = emb_share(core, i)

    def emb_sum(y_at, i):
        own_part = eg_own[y_at, :, i * side_width : (i + 1) * side_width]
        return own_part + eg_side[y_at, :, columns_of(i)].astype(F32)

    def along_parts(buf, at):
        parts = buf[at, :, :HEAD_DIM].astype(F32)
        return parts[:, 0:1] + parts[:, 1:2] + parts[:, 2:3]

    eg_copies = []
    for i in range(2):
        side_copies[i].wait_recv()
        copies = [None] * ny
        for k in far_first(ny):
            eg_out[k, :, columns_of(i)] = emb_sum(ys[k], i).astype(BF16)
            if i == 0:
                along = along_of(core, ys[k]) + along_parts(eg_side, ys[k])
                eg_out[k, :, :HEAD_DIM] = three_parts(along)
            copies[k] = push(
                span(eg_out.at[k], i), span(eg_recv.at[y], i), place(z, ys[k], core)
            )
        eg_copies.append(copies)
    along = along_of(core, y) + along_parts(eg_side, y)
    slope_copies = []
    slopes = []
    for i in range(2):
        emb_grad = emb_sum(y, i)
        for k in range(1, ny):
            eg_copies[i][k].wait_recv()
            emb_grad = emb_grad + eg_recv[ys[ny - k], :, columns_of(i)].astype(F32)
            if i == 0:
                along = along + along_parts(eg_recv, ys[ny - k])
        part = slice(i * side_width, (i + 1) * side_width)
        residual_grad = (emb_grad - embs[i] * along) / norm
        rgrad_ref[:, part] = residual_grad
        slopes.append(residual_grad.astype(BF16))
        slope_all[x, :, part] = slopes[-1]
        place_at = slope_all.at[:, :, pl.ds(i * side_width, side_width)]
        slope_copies.append(exchange(lambda k: place_at.at[x], place_at))

    save(rgrad_ref, rgrad_hbm)
    for copy in far:
        copy.wait_recv()
    for i, k in enumerate((other, two)):
        total = qg_part[zs[k]].astype(F32) + relay[i].astype(F32)
        extra = relay_half[i].astype(F32)
        parts = [total[:half], total[half:]]
        parts[i] = parts[i] + extra
        relay[i] = jnp.concatenate(parts, axis=0).astype(BF16)
        near.append(push(relay.at[i], qg_recv.at[2 + i], place(zs[k], y, core)))
    upstream = dot_nt(jnp.concatenate(slopes, axis=1), weight[0])
    for i in range(2):
        part = slice(i * side_width, (i + 1) * side_width)
        for k in sorted(range(1, nx), key=lambda k: min(k, nx - k)):
            t = received(slope_copies[i], k)
            upstream = upstream + dot_nt(slope_all[t, :, part], weight[nx - k, :, part])
    up_ref[...] = upstream.astype(BF16)
    save(up_ref, up_hbm)

    query_grad = qg_part[z].astype(F32)
    for i, copy in enumerate(near):
        copy.wait_recv()
        query_grad = query_grad + qg_recv[i].astype(F32)
    qgrad_ref[...] = query_grad
    save(qgrad_ref, qgrad_hbm)
    for copy in sent:
        copy.wait_send()
    for copy in saves:
        copy.wait()


def grouped(source, g, heads):
    first = g * heads
    return jnp.concatenate(
        [source[:, (first + h) * HEAD_DIM : (first + h + 1) * HEAD_DIM] for h in range(heads)],
        axis=0,
    )


def spread(source, groups, heads):
    parts = [grouped(source, g, heads) for g in range(groups)]
    empty = jnp.zeros_like(parts[0])
    lines = [
        jnp.concatenate([part if i == g else empty for i in range(groups)], axis=1)
        for g, part in enumerate(parts)
    ]
    return jnp.concatenate(lines, axis=0)


def backward(
    lastq_ref, up_ref, out_ref, key_ref, value_ref, probs_ref, loss_in, qgrad_in, rgrad_in,
    loss_ref, qgrad_ref, rgrad_ref, lgrad_ref, kgrad_ref, vgrad_ref,
):
    loss_ref[...] = loss_in[...]
    qgrad_ref[...] = qgrad_in[...]
    rgrad_ref[...] = rgrad_in[...]
    rows = lastq_ref.shape[0]
    heads = lastq_ref.shape[1] // HEAD_DIM
    scale = 1.0 / HEAD_DIM**0.5
    up = grouped(up_ref, 0, heads)
    mean = jnp.sum(up.astype(F32) * grouped(out_ref, 0, heads), axis=1, keepdims=True)
    probs = probs_ref[...]
    slopes = dot_nt(up, value_ref[...])
    score_slope = (probs.astype(F32) * (slopes - mean)).astype(BF16)
    vgrad_ref[...] = dot_tn(probs, up).astype(BF16)
    lastq = dot_nn(score_slope, key_ref[...]) * scale
    for h in range(heads):
        lgrad_ref[:, h * HEAD_DIM : (h + 1) * HEAD_DIM] = lastq[h * rows : (h + 1) * rows]
    kgrad_ref[...] = (dot_tn(score_slope, grouped(lastq_ref, 0, heads)) * scale).astype(BF16)


def on_device(
    sizes, last_query, key_cache, value_cache, residual, out_weight, query_emb, lengths, positives
):
    nz, ny, nx = sizes
    rows, width = query_emb.shape
    tokens, kv_width = key_cache.shape
    groups = kv_width // HEAD_DIM
    heads = width // kv_width
    inner = CORES * ny
    passages = inner * rows
    chunk = nz // nx * rows
    wide = width + HEAD_DIM
    vmem = pl.BlockSpec(memory_space=pltpu.VMEM)
    hbm = pl.BlockSpec(memory_space=pl.ANY)
    copies = 3 * (nz - 1) + 7 * ny + 8 * (nx - 1)
    loss, query_grad, residual_grad, upstream, attended, probs = pl.pallas_call(
        functools.partial(kernel, sizes),
        out_shape=(
            jax.ShapeDtypeStruct((1, rows), F32),
            jax.ShapeDtypeStruct((rows, width), F32),
            jax.ShapeDtypeStruct((rows, width), F32),
            jax.ShapeDtypeStruct((rows, width), BF16),
            jax.ShapeDtypeStruct((rows, width), F32),
            jax.ShapeDtypeStruct((groups * heads * rows, tokens), BF16),
        ),
        in_specs=[hbm, hbm, hbm, hbm, hbm, hbm, vmem, vmem],
        out_specs=(hbm,) * 6,
        scratch_shapes=[
            pltpu.VMEM((nz, rows, wide), BF16),
            pltpu.VMEM((inner, rows, wide), BF16),
            pltpu.VMEM((nx, width, width), BF16),
            pltpu.VMEM((tokens, kv_width), BF16),
            pltpu.VMEM((tokens, kv_width), BF16),
            pltpu.VMEM((rows, width), BF16),
            pltpu.VMEM((rows, width), BF16),
            pltpu.VMEM((2, rows, HEAD_DIM), jnp.int32),
            pltpu.VMEM((groups * heads * rows, tokens), F32),
            pltpu.VMEM((groups * heads * rows, tokens), BF16),
            pltpu.VMEM((nx, rows, width), BF16),
            pltpu.VMEM((nx, rows, width), BF16),
            pltpu.VMEM((nx, chunk, passages), F32),
            pltpu.VMEM((nx, chunk, passages), F32),
            pltpu.VMEM((nx, 8, passages), F32),
            pltpu.VMEM((passages, HEAD_DIM), F32),
            pltpu.VMEM((nz, 8, HEAD_DIM), F32),
            pltpu.VMEM((nx, chunk, passages), F32),
            pltpu.VMEM((nx * chunk, passages), BF16),
            pltpu.VMEM((nx, 8, HEAD_DIM), F32),
            pltpu.VMEM((ny, rows, wide), BF16),
            pltpu.VMEM((ny, rows, width), F32),
            pltpu.VMEM((ny, rows, wide), BF16),
            pltpu.VMEM((ny, rows, wide), BF16),
            pltpu.VMEM((ny, rows, wide), BF16),
            pltpu.VMEM((nx, rows, width), BF16),
            pltpu.VMEM((nz, rows, width), BF16),
            pltpu.VMEM((4, rows, width), BF16),
            pltpu.VMEM((2, rows, width), BF16),
            pltpu.VMEM((2, rows // 2, width), BF16),
            pltpu.VMEM((1, rows), F32),
            pltpu.VMEM((rows, width), F32),
            pltpu.VMEM((rows, width), F32),
            pltpu.VMEM((rows, width), BF16),
            pltpu.VMEM((rows, width), F32),
            pltpu.SemaphoreType.DMA((5 + nx,)),
            pltpu.SemaphoreType.DMA((6,)),
            pltpu.SemaphoreType.DMA((copies,)),
            pltpu.SemaphoreType.DMA((copies,)),
        ],
        compiler_params=pltpu.CompilerParams(
            collective_id=0, has_side_effects=True, vmem_limit_bytes=60 * 2**20
        ),
    )(
        last_query, key_cache, value_cache, residual, out_weight, query_emb,
        lengths, positives.reshape(1, rows),
    )
    side = heads * HEAD_DIM
    by_heads = pl.BlockSpec((rows, side), lambda g: (0, g))
    by_group = pl.BlockSpec((tokens, HEAD_DIM), lambda g: (0, g))
    line = pl.BlockSpec((1, rows), lambda g: (0, 0))
    loss, query_grad, residual_grad, lastq_grad, key_grad, value_grad = pl.pallas_call(
        backward,
        grid=(groups,),
        out_shape=(
            jax.ShapeDtypeStruct((1, rows), F32),
            jax.ShapeDtypeStruct((rows, width), F32),
            jax.ShapeDtypeStruct((rows, width), F32),
            jax.ShapeDtypeStruct((rows, width), F32),
            jax.ShapeDtypeStruct((tokens, kv_width), BF16),
            jax.ShapeDtypeStruct((tokens, kv_width), BF16),
        ),
        in_specs=[
            by_heads, by_heads, by_heads, by_group, by_group,
            pl.BlockSpec((heads * rows, tokens), lambda g: (g, 0)),
            line, by_heads, by_heads,
        ],
        out_specs=(line, by_heads, by_heads, by_heads, by_group, by_group),
        compiler_params=pltpu.CompilerParams(vmem_limit_bytes=60 * 2**20),
    )(
        last_query, upstream, attended, key_cache, value_cache, probs, loss, query_grad,
        residual_grad,
    )
    return (loss.reshape(rows), query_grad, residual_grad, lastq_grad, key_grad, value_grad)


def solution(mesh, nz=8, ny=4):
    in_specs = (
        P("dp", "mp"),
        P("dp", "mp"),
        P("dp", "mp"),
        P("dp", "mp"),
        P("mp", None),
        P("dp", "mp"),
        P("dp", None),
        P("dp"),
    )
    out_specs = (P("dp"), P("dp", "mp"), P("dp", "mp"), P("dp", "mp"), P("dp", "mp"), P("dp", "mp"))
    sizes = (nz, ny, mesh.shape["mp"])
    return jax.shard_map(
        functools.partial(on_device, sizes),
        mesh=mesh,
        in_specs=in_specs,
        out_specs=out_specs,
        check_vma=False,
    )
```

```python
import functools

import jax
import jax.numpy as jnp
from jax import lax
from jax.experimental import pallas as pl
from jax.experimental.pallas import tpu as pltpu
from jax.sharding import PartitionSpec as P

HEAD_DIM = 128
INV_TEMP = 50.0
EPSILON = 1e-06
CORES = 2
MESH = pl.DeviceIdType.MESH
F32 = jnp.float32
BF16 = jnp.bfloat16


def dot_nn(a, b):
    return lax.dot_general(a, b, (((1,), (0,)), ((), ())), preferred_element_type=F32)


def dot_nt(a, b):
    return lax.dot_general(a, b, (((1,), (1,)), ((), ())), preferred_element_type=F32)


def dot_tn(a, b):
    return lax.dot_general(a, b, (((0,), (0,)), ((), ())), preferred_element_type=F32)


def kernel(
    sizes,
    lastq_hbm, key_hbm, value_hbm, resid_hbm, weight_hbm, query_hbm, len_ref, pos_ref,
    loss_hbm, qgrad_hbm, rgrad_hbm, up_hbm, out_hbm, probs_hbm,
    q_buf, p_buf, weight, key, value, lastq, resid, ranges, attn, probs, y_part, y_recv, s_part, s_recv, sq_all, turned,
    stat, s_all, w_all, misc_all, eg_part, eg_own, eg_side, eg_out, eg_recv, slope_all, qg_part, qg_recv,
    relay, relay_half, loss_ref, qgrad_ref, rgrad_ref, up_ref, out_ref,
    load_sem, save_sem, send_sem, recv_sem,
):
    nz, ny, nx = sizes
    rows, width = query_hbm.shape
    tokens, kv_width = key_hbm.shape
    groups = kv_width // HEAD_DIM
    heads = width // kv_width
    inner = CORES * ny
    passages = inner * rows
    slots = nz // nx
    chunk = slots * rows
    scale = 1.0 / HEAD_DIM**0.5

    me = lax.axis_index("dp")
    x = lax.axis_index("mp")
    core = lax.rem(me, CORES)
    y = lax.rem(lax.div(me, CORES), ny)
    z = lax.div(me, inner)

    def place(z_at, y_at, core_at):
        return {"dp": (z_at * ny + y_at) * CORES + core_at}

    def around(at, step, size):
        return lax.rem(at + (step + size), size)

    def far_first(size):
        return sorted(range(1, size), key=lambda k: -min(k, size - k))

    xs = [around(x, k, nx) for k in range(nx)]
    ys = [around(y, k, ny) for k in range(ny)]
    zs = [around(z, k, nz) for k in range(nz)]
    twin = place(z, y, 1 - core)
    partners = [place(t, y, core) for t in zs[1:]] + [place(z, t, core) for t in ys[1:]]
    partners += [twin] + [{"mp": t} for t in xs[1:]]

    loads = [
        pltpu.make_async_copy(query_hbm, q_buf.at[z, :, pl.ds(0, width)], load_sem.at[0]),
        pltpu.make_async_copy(lastq_hbm, lastq, load_sem.at[1]),
        pltpu.make_async_copy(key_hbm, key, load_sem.at[2]),
        pltpu.make_async_copy(value_hbm, value, load_sem.at[3]),
        pltpu.make_async_copy(resid_hbm, resid, load_sem.at[4]),
    ]
    waits = {}
    for k in far_first(nx) + [0]:
        waits[k] = len(loads)
        columns = pl.ds(pl.multiple_of(xs[k] * width, width), width)
        loads.append(
            pltpu.make_async_copy(weight_hbm.at[:, columns], weight.at[k], load_sem.at[5 + k])
        )
    for load in loads[:4]:
        load.start()

    barrier = pltpu.get_barrier_semaphore()
    for partner in partners:
        pl.semaphore_signal(barrier, inc=1, device_id=partner, device_id_type=MESH)

    saves = []

    def save(source, target):
        saves.append(pltpu.make_async_copy(source, target, save_sem.at[len(saves)]))
        saves[-1].start()

    sent = []

    def push(src, dst, device):
        index = len(sent)
        copy = pltpu.make_async_remote_copy(
            src_ref=src,
            dst_ref=dst,
            send_sem=send_sem.at[index],
            recv_sem=recv_sem.at[index],
            device_id=device,
            device_id_type=MESH,
        )
        copy.start()
        sent.append(copy)
        return copy

    def exchange(src, dst):
        copies = [None] * nx
        for k in far_first(nx):
            copies[k] = push(src(k), dst.at[x], {"mp": xs[k]})
        return copies

    def received(copies, k):
        copies[k].wait_recv()
        return xs[nx - k]

    lane = lax.broadcasted_iota(jnp.int32, (rows, HEAD_DIM), 1)

    def three_parts(column):
        high = column.astype(BF16).astype(F32)
        middle = (column - high).astype(BF16).astype(F32)
        low = column - high - middle
        parts = jnp.where(lane == 0, high, jnp.where(lane == 1, middle, low))
        return jnp.where(lane < 3, parts, 0.0).astype(BF16)

    position = jnp.broadcast_to(pos_ref[...].astype(F32), (rows, rows))
    diagonal = lax.broadcasted_iota(jnp.int32, (rows, rows), 0) == lax.broadcasted_iota(
        jnp.int32, (rows, rows), 1
    )
    position = jnp.sum(jnp.where(diagonal, position, 0.0), axis=1, keepdims=True).astype(jnp.int32)
    high, low = lax.shift_right_logical(position, 6), position & 63
    digits = jnp.where(lane == 0, high, jnp.where(lane == 1, low, 0)).astype(F32).astype(BF16)
    q_buf[z, :, width:] = digits
    lengths = len_ref[...].astype(F32)
    passage = lax.broadcasted_iota(jnp.int32, (rows, rows), 0)
    which = lax.broadcasted_iota(jnp.int32, (rows, rows), 1)
    for i, before in enumerate((which < passage, which <= passage)):
        bound = jnp.sum(jnp.where(before, lengths, 0.0), axis=1, keepdims=True)
        ranges[i] = jnp.broadcast_to(bound, (rows, HEAD_DIM)).astype(jnp.int32)
    loads[0].wait()
    pl.semaphore_wait(barrier, len(partners))
    q_copies = {
        k: push(q_buf.at[z], q_buf.at[z], place(zs[k], y, core)) for k in (2, nz - 2, 1, nz - 1)
    }

    block = 16

    def softmax_rows(i, carry):
        at = pl.ds(pl.multiple_of(i * block, block), block)
        bounds = pl.ds(pl.multiple_of(lax.rem(i, rows // block) * block, block), block)
        token = lax.broadcasted_iota(jnp.int32, (block, tokens), 1)
        inside = (token >= ranges[0, bounds, :][:, :1]) & (token < ranges[1, bounds, :][:, :1])
        scores = jnp.where(inside, attn[at, :], -1e30)
        top = jnp.max(scores, axis=1, keepdims=True)
        powers = jnp.exp((scores - top) * scale)
        weights = powers * (1.0 / jnp.sum(powers, axis=1, keepdims=True))
        probs[at, :] = weights.astype(BF16)
        return carry

    for load in loads[1:3]:
        load.wait()
    for load in loads[4:]:
        load.start()
    group_rows = heads * rows
    blocks = groups * group_rows // block
    attn[...] = dot_nt(spread(lastq, groups, heads), key[...])
    lax.fori_loop(0, blocks, softmax_rows, 0, unroll=blocks)
    loads[3].wait()
    out = dot_nn(probs[...], value[...])
    attended = [
        out[g * group_rows + h * rows : g * group_rows + (h + 1) * rows, g * HEAD_DIM :][:, :HEAD_DIM]
        for g in range(groups)
        for h in range(heads)
    ]
    attended = jnp.concatenate(attended, axis=1)
    out_ref[...] = attended
    attended = attended.astype(BF16)

    side_width = width // 2
    sides = [slice(i * side_width, (i + 1) * side_width) for i in range(2)]

    def project(k, i):
        if i == 0:
            loads[waits[k]].wait()
        y_part[k, :, sides[i]] = dot_nn(attended, weight[k, :, sides[i]]).astype(BF16)
        return y_part.at[k, :, pl.ds(i * side_width, side_width)]

    y_copies = []
    for i in range(2):
        target = y_recv.at[:, :, pl.ds(i * side_width, side_width)]
        y_copies.append(exchange(lambda k: project(k, i), target))
    save(probs, probs_hbm)
    save(out_ref, out_hbm)
    loads[4].wait()
    loads[waits[0]].wait()
    hiddens = [
        dot_nn(attended, weight[0, :, part]) + resid[:, part].astype(F32) for part in sides
    ]
    half = rows // 2
    onward = []
    for k, first in ((2, 0), (nz - 2, half)):
        q_copies[k].wait_recv()
        step = 1 if k == 2 else nz - 1
        part = q_buf.at[zs[nz - k]]
        onward.append(push(part, part, place(zs[step], y, core)))
        part = q_buf.at[zs[nz - k], pl.ds(first, half)]
        onward.append(push(part, part, place(zs[k], y, core)))

    own = core * ny + y
    spans = (pl.ds(0, side_width), pl.ds(side_width, side_width + HEAD_DIM))
    p_copies = [[None] * ny, [None] * ny]
    passed = [[], []]
    for i, part in enumerate(sides):
        for k in range(1, nx):
            t = received(y_copies[i], k)
            hiddens[i] = hiddens[i] + y_recv[t, :, part].astype(F32)
        p_buf[own, :, part] = hiddens[i].astype(BF16)
        if i == 1:
            squares = [jnp.sum(hidden * hidden, axis=1, keepdims=True) for hidden in hiddens]
            p_buf[own, :, width:] = three_parts(squares[0] + squares[1])
        block_at = p_buf.at[own, :, spans[i]]
        for k in far_first(ny):
            p_copies[i][k] = push(block_at, block_at, place(z, ys[k], core))
        passed[i].append(push(block_at, block_at, twin))
    for i in range(2):
        for k in sorted(range(1, ny), key=lambda k: min(k, ny - k)):
            p_copies[i][k].wait_recv()
            block_at = p_buf.at[core * ny + ys[ny - k], :, spans[i]]
            passed[i].append(push(block_at, block_at, twin))
    for copy in [q_copies[1], q_copies[nz - 1]] + onward:
        copy.wait_recv()

    def partial_scores(t, i):
        part = q_buf[pl.ds(t * slots, slots), :, sides[i]].reshape(chunk, side_width)
        return dot_nt(part, p_buf[:, :, sides[i]].reshape(passages, side_width))

    for copy in passed[0]:
        copy.wait_recv()
    for k in range(nx):
        s_part[k] = partial_scores(xs[k], 0)
    for copy in passed[1]:
        copy.wait_recv()

    def send_scores(k):
        s_part[k] += partial_scores(xs[k], 1)
        return s_part.at[k]

    unit = (lax.broadcasted_iota(jnp.int32, (8, HEAD_DIM), 1) < 3).astype(F32).astype(BF16)
    sq_all[x] = dot_nt(unit, p_buf[:, :, width:].reshape(passages, HEAD_DIM))
    sq_copies = exchange(lambda k: sq_all.at[x], sq_all)
    s_copies = exchange(send_scores, s_recv)
    scores = s_part[0] + partial_scores(x, 1)
    squares = sq_all[x]
    for k in range(1, nx):
        squares = squares + sq_all[received(sq_copies, k)]
    norms = jnp.sqrt(squares[:1] + EPSILON)
    turned[...] = jnp.broadcast_to(norms, (HEAD_DIM, passages)).T
    norm = turned[pl.ds(pl.multiple_of(own * rows, rows), rows), :][:, :1]
    embs = [hidden / norm for hidden in hiddens]
    digits = q_buf[:, :, width:].reshape(nz * rows, HEAD_DIM).astype(F32)
    positive = (digits[:, 0:1] * 64.0 + digits[:, 1:2]).astype(jnp.int32)
    index = lax.broadcasted_iota(jnp.int32, (nz * rows, passages), 1)
    slot = lax.div(index, rows)
    cell = lax.rem(slot, ny) * CORES + lax.div(slot, ny)
    passage_of = (z * inner + cell) * rows + lax.rem(index, rows)
    match = positive == passage_of
    for k in range(1, nx):
        scores = scores + s_recv[received(s_copies, k)]
    scores = scores * (INV_TEMP / norms)

    top = jnp.max(scores, axis=1, keepdims=True)
    total = jnp.sum(jnp.exp(scores - top), axis=1, keepdims=True)
    own_digits = q_buf[pl.ds(x * slots, slots), :, width:].reshape(chunk, HEAD_DIM).astype(F32)
    own_positive = (own_digits[:, 0:1] * 64.0 + own_digits[:, 1:2]).astype(jnp.int32)
    own_match = own_positive == passage_of[:chunk]
    hit = jnp.sum(jnp.where(own_match, scores, 0.0), axis=1, keepdims=True)
    chunk_lane = lax.broadcasted_iota(jnp.int32, (chunk, HEAD_DIM), 1)
    columns = jnp.where(chunk_lane == 0, top, jnp.where(chunk_lane == 1, total, hit))
    stat[z] = jnp.concatenate([columns] * (HEAD_DIM // chunk), axis=0).T[:8]
    stat_copies = [push(stat.at[z], stat.at[z], place(zs[k], y, core)) for k in far_first(nz)]
    s_all[x] = scores
    all_copies = exchange(lambda k: s_all.at[x], s_all)
    for copy in stat_copies:
        copy.wait_recv()
    every = stat[...]
    top = jnp.max(every[:, 0:1], axis=0)
    total = jnp.sum(every[:, 1:2] * jnp.exp(every[:, 0:1] - top[None]), axis=0)
    lse = top + jnp.log(total)
    loss = lse - jnp.sum(every[:, 2:3], axis=0)
    line = lax.broadcasted_iota(jnp.int32, (8, HEAD_DIM), 0)
    misc_all[x] = jnp.where(line == 0, lse, loss)
    misc_copies = exchange(lambda k: misc_all.at[x], misc_all)
    for k in range(1, nx):
        received(all_copies, k)
    for k in range(1, nx):
        received(misc_copies, k)
    losses = misc_all[lax.div(z, slots)][1:2]
    own_loss = losses[:, :rows]
    for k in range(1, slots):
        own_loss = jnp.where(lax.rem(z, slots) == k, losses[:, k * rows : (k + 1) * rows], own_loss)
    loss_ref[...] = own_loss
    save(loss_ref, loss_hbm)

    lines = [misc_all[t][:1] for t in range(nx)] + [jnp.zeros((HEAD_DIM - nx, HEAD_DIM), F32)]
    turned_lse = jnp.concatenate(lines, axis=0).T
    lse = jnp.concatenate([turned_lse[:chunk, t : t + 1] for t in range(nx)], axis=0)
    scores = s_all[...].reshape(nx * chunk, passages)
    pairs = jnp.exp(scores - lse) - match.astype(F32)
    along = jnp.sum(pairs.astype(BF16).astype(F32) * scores, axis=0, keepdims=True)
    w_all[...] = pairs.astype(BF16)
    turned[...] = jnp.broadcast_to(along, (HEAD_DIM, passages)).T

    share = ny * rows
    spans = ((0, HEAD_DIM + side_width), (HEAD_DIM + side_width, side_width))

    def emb_share(core_at, i):
        part = w_all[:, pl.ds(pl.multiple_of(core_at * share, share), share)]
        queries = q_buf[:, :, i * side_width : (i + 1) * side_width].reshape(nz * rows, side_width)
        return (dot_tn(part, queries) * INV_TEMP).reshape(ny, rows, side_width)

    def along_of(core_at, y_at):
        first = pl.multiple_of((core_at * ny + y_at) * rows, rows)
        return turned[pl.ds(first, rows), :][:, :1]

    def columns_of(i):
        return slice(HEAD_DIM + i * side_width, HEAD_DIM + (i + 1) * side_width)

    def span(buf, i):
        return buf.at[:, pl.ds(*spans[i])] if len(buf.shape) == 2 else buf.at[:, :, pl.ds(*spans[i])]

    for j in range(ny):
        eg_part[j, :, :HEAD_DIM] = three_parts(along_of(1 - core, j))
    side_copies = []
    for i in range(2):
        eg_part[:, :, columns_of(i)] = emb_share(1 - core, i).astype(BF16)
        side_copies.append(push(span(eg_part, i), span(eg_side, i), twin))

    pairs = (pairs * (INV_TEMP / norms)).astype(BF16)
    grads = dot_nn(pairs, p_buf[:, :, :width].reshape(passages, width))
    qg_part[...] = grads.astype(BF16).reshape(nz, rows, width)
    one, last, two, other = 1, nz - 1, 2, nz - 2
    far = [push(qg_part.at[zs[4], pl.ds(0, half)], relay_half.at[0], place(zs[other], y, core))]
    far.append(push(qg_part.at[zs[4], pl.ds(half, half)], relay_half.at[1], place(zs[two], y, core)))
    far.append(push(qg_part.at[zs[nz - 3]], relay.at[0], place(zs[last], y, core)))
    far.append(push(qg_part.at[zs[3]], relay.at[1], place(zs[one], y, core)))
    near = [push(qg_part.at[zs[one]], qg_recv.at[0], place(zs[one], y, core))]
    near.append(push(qg_part.at[zs[last]], qg_recv.at[1], place(zs[last], y, core)))
    for i in range(2):
        eg_own[:, :, i * side_width : (i + 1) * side_width] = emb_share(core, i)

    def emb_sum(y_at, i):
        own_part = eg_own[y_at, :, i * side_width : (i + 1) * side_width]
        return own_part + eg_side[y_at, :, columns_of(i)].astype(F32)

    def along_parts(buf, at):
        parts = buf[at, :, :HEAD_DIM].astype(F32)
        return parts[:, 0:1] + parts[:, 1:2] + parts[:, 2:3]

    eg_copies = []
    for i in range(2):
        side_copies[i].wait_recv()
        copies = [None] * ny
        for k in far_first(ny):
            eg_out[k, :, columns_of(i)] = emb_sum(ys[k], i).astype(BF16)
            if i == 0:
                along = along_of(core, ys[k]) + along_parts(eg_side, ys[k])
                eg_out[k, :, :HEAD_DIM] = three_parts(along)
            copies[k] = push(
                span(eg_out.at[k], i), span(eg_recv.at[y], i), place(z, ys[k], core)
            )
        eg_copies.append(copies)
    along = along_of(core, y) + along_parts(eg_side, y)
    slope_copies = []
    slopes = []
    for i in range(2):
        emb_grad = emb_sum(y, i)
        for k in range(1, ny):
            eg_copies[i][k].wait_recv()
            emb_grad = emb_grad + eg_recv[ys[ny - k], :, columns_of(i)].astype(F32)
            if i == 0:
                along = along + along_parts(eg_recv, ys[ny - k])
        part = slice(i * side_width, (i + 1) * side_width)
        residual_grad = (emb_grad - embs[i] * along) / norm
        rgrad_ref[:, part] = residual_grad
        slopes.append(residual_grad.astype(BF16))
        slope_all[x, :, part] = slopes[-1]
        place_at = slope_all.at[:, :, pl.ds(i * side_width, side_width)]
        slope_copies.append(exchange(lambda k: place_at.at[x], place_at))

    save(rgrad_ref, rgrad_hbm)
    for copy in far:
        copy.wait_recv()
    for i, k in enumerate((other, two)):
        total = qg_part[zs[k]].astype(F32) + relay[i].astype(F32)
        extra = relay_half[i].astype(F32)
        parts = [total[:half], total[half:]]
        parts[i] = parts[i] + extra
        relay[i] = jnp.concatenate(parts, axis=0).astype(BF16)
        near.append(push(relay.at[i], qg_recv.at[2 + i], place(zs[k], y, core)))
    upstream = dot_nt(jnp.concatenate(slopes, axis=1), weight[0])
    for i in range(2):
        part = slice(i * side_width, (i + 1) * side_width)
        for k in sorted(range(1, nx), key=lambda k: min(k, nx - k)):
            t = received(slope_copies[i], k)
            upstream = upstream + dot_nt(slope_all[t, :, part], weight[nx - k, :, part])
    up_ref[...] = upstream.astype(BF16)
    save(up_ref, up_hbm)

    query_grad = qg_part[z].astype(F32)
    for i, copy in enumerate(near):
        copy.wait_recv()
        query_grad = query_grad + qg_recv[i].astype(F32)
    qgrad_ref[...] = query_grad
    save(qgrad_ref, qgrad_hbm)
    for copy in sent:
        copy.wait_send()
    for copy in saves:
        copy.wait()


def grouped(source, g, heads):
    first = g * heads
    return jnp.concatenate(
        [source[:, (first + h) * HEAD_DIM : (first + h + 1) * HEAD_DIM] for h in range(heads)],
        axis=0,
    )


def spread(source, groups, heads):
    parts = [grouped(source, g, heads) for g in range(groups)]
    empty = jnp.zeros_like(parts[0])
    lines = [
        jnp.concatenate([part if i == g else empty for i in range(groups)], axis=1)
        for g, part in enumerate(parts)
    ]
    return jnp.concatenate(lines, axis=0)


def backward(
    lastq_ref, up_ref, out_ref, key_ref, value_ref, probs_ref, loss_in, qgrad_in, rgrad_in,
    loss_ref, qgrad_ref, rgrad_ref, lgrad_ref, kgrad_ref, vgrad_ref,
):
    loss_ref[...] = loss_in[...]
    qgrad_ref[...] = qgrad_in[...]
    rgrad_ref[...] = rgrad_in[...]
    rows = lastq_ref.shape[0]
    heads = lastq_ref.shape[1] // HEAD_DIM
    scale = 1.0 / HEAD_DIM**0.5
    up = grouped(up_ref, 0, heads)
    mean = jnp.sum(up.astype(F32) * grouped(out_ref, 0, heads), axis=1, keepdims=True)
    probs = probs_ref[...]
    slopes = dot_nt(up, value_ref[...])
    score_slope = (probs.astype(F32) * (slopes - mean)).astype(BF16)
    vgrad_ref[...] = dot_tn(probs, up).astype(BF16)
    lastq = dot_nn(score_slope, key_ref[...]) * scale
    for h in range(heads):
        lgrad_ref[:, h * HEAD_DIM : (h + 1) * HEAD_DIM] = lastq[h * rows : (h + 1) * rows]
    kgrad_ref[...] = (dot_tn(score_slope, grouped(lastq_ref, 0, heads)) * scale).astype(BF16)


def on_device(
    sizes, last_query, key_cache, value_cache, residual, out_weight, query_emb, lengths, positives
):
    nz, ny, nx = sizes
    rows, width = query_emb.shape
    tokens, kv_width = key_cache.shape
    groups = kv_width // HEAD_DIM
    heads = width // kv_width
    inner = CORES * ny
    passages = inner * rows
    chunk = nz // nx * rows
    wide = width + HEAD_DIM
    vmem = pl.BlockSpec(memory_space=pltpu.VMEM)
    hbm = pl.BlockSpec(memory_space=pl.ANY)
    copies = 3 * (nz - 1) + 7 * ny + 8 * (nx - 1)
    loss, query_grad, residual_grad, upstream, attended, probs = pl.pallas_call(
        functools.partial(kernel, sizes),
        out_shape=(
            jax.ShapeDtypeStruct((1, rows), F32),
            jax.ShapeDtypeStruct((rows, width), F32),
            jax.ShapeDtypeStruct((rows, width), F32),
            jax.ShapeDtypeStruct((rows, width), BF16),
            jax.ShapeDtypeStruct((rows, width), F32),
            jax.ShapeDtypeStruct((groups * heads * rows, tokens), BF16),
        ),
        in_specs=[hbm, hbm, hbm, hbm, hbm, hbm, vmem, vmem],
        out_specs=(hbm,) * 6,
        scratch_shapes=[
            pltpu.VMEM((nz, rows, wide), BF16),
            pltpu.VMEM((inner, rows, wide), BF16),
            pltpu.VMEM((nx, width, width), BF16),
            pltpu.VMEM((tokens, kv_width), BF16),
            pltpu.VMEM((tokens, kv_width), BF16),
            pltpu.VMEM((rows, width), BF16),
            pltpu.VMEM((rows, width), BF16),
            pltpu.VMEM((2, rows, HEAD_DIM), jnp.int32),
            pltpu.VMEM((groups * heads * rows, tokens), F32),
            pltpu.VMEM((groups * heads * rows, tokens), BF16),
            pltpu.VMEM((nx, rows, width), BF16),
            pltpu.VMEM((nx, rows, width), BF16),
            pltpu.VMEM((nx, chunk, passages), F32),
            pltpu.VMEM((nx, chunk, passages), F32),
            pltpu.VMEM((nx, 8, passages), F32),
            pltpu.VMEM((passages, HEAD_DIM), F32),
            pltpu.VMEM((nz, 8, HEAD_DIM), F32),
            pltpu.VMEM((nx, chunk, passages), F32),
            pltpu.VMEM((nx * chunk, passages), BF16),
            pltpu.VMEM((nx, 8, HEAD_DIM), F32),
            pltpu.VMEM((ny, rows, wide), BF16),
            pltpu.VMEM((ny, rows, width), F32),
            pltpu.VMEM((ny, rows, wide), BF16),
            pltpu.VMEM((ny, rows, wide), BF16),
            pltpu.VMEM((ny, rows, wide), BF16),
            pltpu.VMEM((nx, rows, width), BF16),
            pltpu.VMEM((nz, rows, width), BF16),
            pltpu.VMEM((4, rows, width), BF16),
            pltpu.VMEM((2, rows, width), BF16),
            pltpu.VMEM((2, rows // 2, width), BF16),
            pltpu.VMEM((1, rows), F32),
            pltpu.VMEM((rows, width), F32),
            pltpu.VMEM((rows, width), F32),
            pltpu.VMEM((rows, width), BF16),
            pltpu.VMEM((rows, width), F32),
            pltpu.SemaphoreType.DMA((5 + nx,)),
            pltpu.SemaphoreType.DMA((6,)),
            pltpu.SemaphoreType.DMA((copies,)),
            pltpu.SemaphoreType.DMA((copies,)),
        ],
        compiler_params=pltpu.CompilerParams(
            collective_id=0, has_side_effects=True, vmem_limit_bytes=60 * 2**20
        ),
    )(
        last_query, key_cache, value_cache, residual, out_weight, query_emb,
        lengths, positives.reshape(1, rows),
    )
    side = heads * HEAD_DIM
    by_heads = pl.BlockSpec((rows, side), lambda g: (0, g))
    by_group = pl.BlockSpec((tokens, HEAD_DIM), lambda g: (0, g))
    line = pl.BlockSpec((1, rows), lambda g: (0, 0))
    loss, query_grad, residual_grad, lastq_grad, key_grad, value_grad = pl.pallas_call(
        backward,
        grid=(groups,),
        out_shape=(
            jax.ShapeDtypeStruct((1, rows), F32),
            jax.ShapeDtypeStruct((rows, width), F32),
            jax.ShapeDtypeStruct((rows, width), F32),
            jax.ShapeDtypeStruct((rows, width), F32),
            jax.ShapeDtypeStruct((tokens, kv_width), BF16),
            jax.ShapeDtypeStruct((tokens, kv_width), BF16),
        ),
        in_specs=[
            by_heads, by_heads, by_heads, by_group, by_group,
            pl.BlockSpec((heads * rows, tokens), lambda g: (g, 0)),
            line, by_heads, by_heads,
        ],
        out_specs=(line, by_heads, by_heads, by_heads, by_group, by_group),
        compiler_params=pltpu.CompilerParams(vmem_limit_bytes=60 * 2**20),
    )(
        last_query, upstream, attended, key_cache, value_cache, probs, loss, query_grad,
        residual_grad,
    )
    return (loss.reshape(rows), query_grad, residual_grad, lastq_grad, key_grad, value_grad)


def solution(mesh, nz=8, ny=4):
    in_specs = (
        P("dp", "mp"),
        P("dp", "mp"),
        P("dp", "mp"),
        P("dp", "mp"),
        P("mp", None),
        P("dp", "mp"),
        P("dp", None),
        P("dp"),
    )
    out_specs = (P("dp"), P("dp", "mp"), P("dp", "mp"), P("dp", "mp"), P("dp", "mp"), P("dp", "mp"))
    sizes = (nz, ny, mesh.shape["mp"])
    return jax.shard_map(
        functools.partial(on_device, sizes),
        mesh=mesh,
        in_specs=in_specs,
        out_specs=out_specs,
        check_vma=False,
    )
```

```python
import functools

import jax
import jax.numpy as jnp
from jax import lax
from jax.experimental import pallas as pl
from jax.experimental.pallas import tpu as pltpu
from jax.sharding import PartitionSpec as P

HEAD_DIM = 128
INV_TEMP = 50.0
EPSILON = 1e-06
CORES = 2
MESH = pl.DeviceIdType.MESH
F32 = jnp.float32
BF16 = jnp.bfloat16


def dot_nn(a, b):
    return lax.dot_general(a, b, (((1,), (0,)), ((), ())), preferred_element_type=F32)


def dot_nt(a, b):
    return lax.dot_general(a, b, (((1,), (1,)), ((), ())), preferred_element_type=F32)


def dot_tn(a, b):
    return lax.dot_general(a, b, (((0,), (0,)), ((), ())), preferred_element_type=F32)


def kernel(
    sizes,
    lastq_hbm, key_hbm, value_hbm, resid_hbm, weight_hbm, query_hbm, len_ref, pos_ref,
    loss_hbm, qgrad_hbm, rgrad_hbm, up_hbm, out_hbm, probs_hbm,
    q_buf, p_buf, weight, key, value, lastq, resid, ranges, attn, probs, y_part, y_recv, s_part, s_recv, sq_all, turned,
    stat, s_all, w_all, misc_all, eg_part, eg_own, eg_side, eg_out, eg_recv, slope_all, qg_part, qg_recv,
    relay, relay_half, loss_ref, qgrad_ref, rgrad_ref, up_ref, out_ref,
    load_sem, save_sem, send_sem, recv_sem,
):
    nz, ny, nx = sizes
    rows, width = query_hbm.shape
    tokens, kv_width = key_hbm.shape
    groups = kv_width // HEAD_DIM
    heads = width // kv_width
    inner = CORES * ny
    passages = inner * rows
    slots = nz // nx
    chunk = slots * rows
    scale = 1.0 / HEAD_DIM**0.5

    me = lax.axis_index("dp")
    x = lax.axis_index("mp")
    core = lax.rem(me, CORES)
    y = lax.rem(lax.div(me, CORES), ny)
    z = lax.div(me, inner)

    def place(z_at, y_at, core_at):
        return {"dp": (z_at * ny + y_at) * CORES + core_at}

    def around(at, step, size):
        return lax.rem(at + (step + size), size)

    def far_first(size):
        return sorted(range(1, size), key=lambda k: -min(k, size - k))

    xs = [around(x, k, nx) for k in range(nx)]
    ys = [around(y, k, ny) for k in range(ny)]
    zs = [around(z, k, nz) for k in range(nz)]
    twin = place(z, y, 1 - core)
    partners = [place(t, y, core) for t in zs[1:]] + [place(z, t, core) for t in ys[1:]]
    partners += [twin] + [{"mp": t} for t in xs[1:]]

    loads = [
        pltpu.make_async_copy(query_hbm, q_buf.at[z, :, pl.ds(0, width)], load_sem.at[0]),
        pltpu.make_async_copy(lastq_hbm, lastq, load_sem.at[1]),
        pltpu.make_async_copy(key_hbm, key, load_sem.at[2]),
        pltpu.make_async_copy(value_hbm, value, load_sem.at[3]),
        pltpu.make_async_copy(resid_hbm, resid, load_sem.at[4]),
    ]
    waits = {}
    for k in far_first(nx) + [0]:
        waits[k] = len(loads)
        columns = pl.ds(pl.multiple_of(xs[k] * width, width), width)
        loads.append(
            pltpu.make_async_copy(weight_hbm.at[:, columns], weight.at[k], load_sem.at[5 + k])
        )
    for load in loads[:4]:
        load.start()

    barrier = pltpu.get_barrier_semaphore()
    for partner in partners:
        pl.semaphore_signal(barrier, inc=1, device_id=partner, device_id_type=MESH)

    saves = []

    def save(source, target):
        saves.append(pltpu.make_async_copy(source, target, save_sem.at[len(saves)]))
        saves[-1].start()

    sent = []

    def push(src, dst, device):
        index = len(sent)
        copy = pltpu.make_async_remote_copy(
            src_ref=src,
            dst_ref=dst,
            send_sem=send_sem.at[index],
            recv_sem=recv_sem.at[index],
            device_id=device,
            device_id_type=MESH,
        )
        copy.start()
        sent.append(copy)
        return copy

    def exchange(src, dst):
        copies = [None] * nx
        for k in far_first(nx):
            copies[k] = push(src(k), dst.at[x], {"mp": xs[k]})
        return copies

    def received(copies, k):
        copies[k].wait_recv()
        return xs[nx - k]

    lane = lax.broadcasted_iota(jnp.int32, (rows, HEAD_DIM), 1)

    def three_parts(column):
        high = column.astype(BF16).astype(F32)
        middle = (column - high).astype(BF16).astype(F32)
        low = column - high - middle
        parts = jnp.where(lane == 0, high, jnp.where(lane == 1, middle, low))
        return jnp.where(lane < 3, parts, 0.0).astype(BF16)

    position = jnp.broadcast_to(pos_ref[...].astype(F32), (rows, rows))
    diagonal = lax.broadcasted_iota(jnp.int32, (rows, rows), 0) == lax.broadcasted_iota(
        jnp.int32, (rows, rows), 1
    )
    position = jnp.sum(jnp.where(diagonal, position, 0.0), axis=1, keepdims=True).astype(jnp.int32)
    high, low = lax.shift_right_logical(position, 6), position & 63
    digits = jnp.where(lane == 0, high, jnp.where(lane == 1, low, 0)).astype(F32).astype(BF16)
    q_buf[z, :, width:] = digits
    lengths = len_ref[...].astype(F32)
    passage = lax.broadcasted_iota(jnp.int32, (rows, rows), 0)
    which = lax.broadcasted_iota(jnp.int32, (rows, rows), 1)
    for i, before in enumerate((which < passage, which <= passage)):
        bound = jnp.sum(jnp.where(before, lengths, 0.0), axis=1, keepdims=True)
        ranges[i] = jnp.broadcast_to(bound, (rows, HEAD_DIM)).astype(jnp.int32)
    loads[0].wait()
    pl.semaphore_wait(barrier, len(partners))
    q_copies = {
        k: push(q_buf.at[z], q_buf.at[z], place(zs[k], y, core)) for k in (2, nz - 2, 1, nz - 1)
    }

    block = 16

    def softmax_rows(i, carry):
        at = pl.ds(pl.multiple_of(i * block, block), block)
        bounds = pl.ds(pl.multiple_of(lax.rem(i, rows // block) * block, block), block)
        token = lax.broadcasted_iota(jnp.int32, (block, tokens), 1)
        inside = (token >= ranges[0, bounds, :][:, :1]) & (token < ranges[1, bounds, :][:, :1])
        scores = jnp.where(inside, attn[at, :], -1e30)
        top = jnp.max(scores, axis=1, keepdims=True)
        powers = jnp.exp((scores - top) * scale)
        weights = powers * (1.0 / jnp.sum(powers, axis=1, keepdims=True))
        probs[at, :] = weights.astype(BF16)
        return carry

    for load in loads[1:4]:
        load.wait()
    for load in loads[4:]:
        load.start()
    group_rows = heads * rows
    blocks = groups * group_rows // block
    attn[...] = dot_nt(spread(lastq, groups, heads), key[...])
    lax.fori_loop(0, blocks, softmax_rows, 0, unroll=blocks)
    out = dot_nn(probs[...], value[...])
    attended = [
        out[g * group_rows + h * rows : g * group_rows + (h + 1) * rows, g * HEAD_DIM :][:, :HEAD_DIM]
        for g in range(groups)
        for h in range(heads)
    ]
    attended = jnp.concatenate(attended, axis=1)
    out_ref[...] = attended
    attended = attended.astype(BF16)

    side_width = width // 2
    sides = [slice(i * side_width, (i + 1) * side_width) for i in range(2)]

    def project(k, i):
        if i == 0:
            loads[waits[k]].wait()
        y_part[k, :, sides[i]] = dot_nn(attended, weight[k, :, sides[i]]).astype(BF16)
        return y_part.at[k, :, pl.ds(i * side_width, side_width)]

    y_copies = []
    for i in range(2):
        target = y_recv.at[:, :, pl.ds(i * side_width, side_width)]
        y_copies.append(exchange(lambda k: project(k, i), target))
    save(probs, probs_hbm)
    save(out_ref, out_hbm)
    loads[4].wait()
    loads[waits[0]].wait()
    hiddens = [
        dot_nn(attended, weight[0, :, part]) + resid[:, part].astype(F32) for part in sides
    ]
    half = rows // 2
    onward = []
    for k, first in ((2, 0), (nz - 2, half)):
        q_copies[k].wait_recv()
        step = 1 if k == 2 else nz - 1
        part = q_buf.at[zs[nz - k]]
        onward.append(push(part, part, place(zs[step], y, core)))
        part = q_buf.at[zs[nz - k], pl.ds(first, half)]
        onward.append(push(part, part, place(zs[k], y, core)))

    own = core * ny + y
    spans = (pl.ds(0, side_width), pl.ds(side_width, side_width + HEAD_DIM))
    p_copies = [[None] * ny, [None] * ny]
    passed = [[], []]
    for i, part in enumerate(sides):
        for k in range(1, nx):
            t = received(y_copies[i], k)
            hiddens[i] = hiddens[i] + y_recv[t, :, part].astype(F32)
        p_buf[own, :, part] = hiddens[i].astype(BF16)
        if i == 1:
            squares = [jnp.sum(hidden * hidden, axis=1, keepdims=True) for hidden in hiddens]
            p_buf[own, :, width:] = three_parts(squares[0] + squares[1])
        block_at = p_buf.at[own, :, spans[i]]
        for k in far_first(ny):
            p_copies[i][k] = push(block_at, block_at, place(z, ys[k], core))
        passed[i].append(push(block_at, block_at, twin))
    for i in range(2):
        for k in sorted(range(1, ny), key=lambda k: min(k, ny - k)):
            p_copies[i][k].wait_recv()
            block_at = p_buf.at[core * ny + ys[ny - k], :, spans[i]]
            passed[i].append(push(block_at, block_at, twin))
    for copy in [q_copies[1], q_copies[nz - 1]] + onward:
        copy.wait_recv()

    def partial_scores(t, i):
        part = q_buf[pl.ds(t * slots, slots), :, sides[i]].reshape(chunk, side_width)
        return dot_nt(part, p_buf[:, :, sides[i]].reshape(passages, side_width))

    for copy in passed[0]:
        copy.wait_recv()
    for k in range(nx):
        s_part[k] = partial_scores(xs[k], 0)
    for copy in passed[1]:
        copy.wait_recv()

    def send_scores(k):
        s_part[k] += partial_scores(xs[k], 1)
        return s_part.at[k]

    unit = (lax.broadcasted_iota(jnp.int32, (8, HEAD_DIM), 1) < 3).astype(F32).astype(BF16)
    sq_all[x] = dot_nt(unit, p_buf[:, :, width:].reshape(passages, HEAD_DIM))
    sq_copies = exchange(lambda k: sq_all.at[x], sq_all)
    s_copies = exchange(send_scores, s_recv)
    scores = s_part[0] + partial_scores(x, 1)
    squares = sq_all[x]
    for k in range(1, nx):
        squares = squares + sq_all[received(sq_copies, k)]
    norms = jnp.sqrt(squares[:1] + EPSILON)
    turned[...] = jnp.broadcast_to(norms, (HEAD_DIM, passages)).T
    norm = turned[pl.ds(pl.multiple_of(own * rows, rows), rows), :][:, :1]
    embs = [hidden / norm for hidden in hiddens]
    digits = q_buf[:, :, width:].reshape(nz * rows, HEAD_DIM).astype(F32)
    positive = (digits[:, 0:1] * 64.0 + digits[:, 1:2]).astype(jnp.int32)
    index = lax.broadcasted_iota(jnp.int32, (nz * rows, passages), 1)
    slot = lax.div(index, rows)
    cell = lax.rem(slot, ny) * CORES + lax.div(slot, ny)
    passage_of = (z * inner + cell) * rows + lax.rem(index, rows)
    match = positive == passage_of
    for k in range(1, nx):
        scores = scores + s_recv[received(s_copies, k)]
    scores = scores * (INV_TEMP / norms)

    top = jnp.max(scores, axis=1, keepdims=True)
    total = jnp.sum(jnp.exp(scores - top), axis=1, keepdims=True)
    own_digits = q_buf[pl.ds(x * slots, slots), :, width:].reshape(chunk, HEAD_DIM).astype(F32)
    own_positive = (own_digits[:, 0:1] * 64.0 + own_digits[:, 1:2]).astype(jnp.int32)
    own_match = own_positive == passage_of[:chunk]
    hit = jnp.sum(jnp.where(own_match, scores, 0.0), axis=1, keepdims=True)
    chunk_lane = lax.broadcasted_iota(jnp.int32, (chunk, HEAD_DIM), 1)
    columns = jnp.where(chunk_lane == 0, top, jnp.where(chunk_lane == 1, total, hit))
    stat[z] = jnp.concatenate([columns] * (HEAD_DIM // chunk), axis=0).T[:8]
    stat_copies = [push(stat.at[z], stat.at[z], place(zs[k], y, core)) for k in far_first(nz)]
    s_all[x] = scores
    all_copies = exchange(lambda k: s_all.at[x], s_all)
    for copy in stat_copies:
        copy.wait_recv()
    every = stat[...]
    top = jnp.max(every[:, 0:1], axis=0)
    total = jnp.sum(every[:, 1:2] * jnp.exp(every[:, 0:1] - top[None]), axis=0)
    lse = top + jnp.log(total)
    loss = lse - jnp.sum(every[:, 2:3], axis=0)
    line = lax.broadcasted_iota(jnp.int32, (8, HEAD_DIM), 0)
    misc_all[x] = jnp.where(line == 0, lse, loss)
    misc_copies = exchange(lambda k: misc_all.at[x], misc_all)
    for k in range(1, nx):
        received(all_copies, k)
    for k in range(1, nx):
        received(misc_copies, k)
    losses = misc_all[lax.div(z, slots)][1:2]
    own_loss = losses[:, :rows]
    for k in range(1, slots):
        own_loss = jnp.where(lax.rem(z, slots) == k, losses[:, k * rows : (k + 1) * rows], own_loss)
    loss_ref[...] = own_loss
    save(loss_ref, loss_hbm)

    lines = [misc_all[t][:1] for t in range(nx)] + [jnp.zeros((HEAD_DIM - nx, HEAD_DIM), F32)]
    turned_lse = jnp.concatenate(lines, axis=0).T
    lse = jnp.concatenate([turned_lse[:chunk, t : t + 1] for t in range(nx)], axis=0)
    scores = s_all[...].reshape(nx * chunk, passages)
    pairs = jnp.exp(scores - lse) - match.astype(F32)
    along = jnp.sum(pairs.astype(BF16).astype(F32) * scores, axis=0, keepdims=True)
    w_all[...] = pairs.astype(BF16)
    turned[...] = jnp.broadcast_to(along, (HEAD_DIM, passages)).T

    share = ny * rows
    spans = ((0, HEAD_DIM + side_width), (HEAD_DIM + side_width, side_width))

    def emb_share(core_at, i):
        part = w_all[:, pl.ds(pl.multiple_of(core_at * share, share), share)]
        queries = q_buf[:, :, i * side_width : (i + 1) * side_width].reshape(nz * rows, side_width)
        return (dot_tn(part, queries) * INV_TEMP).reshape(ny, rows, side_width)

    def along_of(core_at, y_at):
        first = pl.multiple_of((core_at * ny + y_at) * rows, rows)
        return turned[pl.ds(first, rows), :][:, :1]

    def columns_of(i):
        return slice(HEAD_DIM + i * side_width, HEAD_DIM + (i + 1) * side_width)

    def span(buf, i):
        return buf.at[:, pl.ds(*spans[i])] if len(buf.shape) == 2 else buf.at[:, :, pl.ds(*spans[i])]

    for j in range(ny):
        eg_part[j, :, :HEAD_DIM] = three_parts(along_of(1 - core, j))
    side_copies = []
    for i in range(2):
        eg_part[:, :, columns_of(i)] = emb_share(1 - core, i).astype(BF16)
        side_copies.append(push(span(eg_part, i), span(eg_side, i), twin))

    pairs = (pairs * (INV_TEMP / norms)).astype(BF16)
    grads = dot_nn(pairs, p_buf[:, :, :width].reshape(passages, width))
    qg_part[...] = grads.astype(BF16).reshape(nz, rows, width)
    one, last, two, other = 1, nz - 1, 2, nz - 2
    far = [push(qg_part.at[zs[4], pl.ds(0, half)], relay_half.at[0], place(zs[other], y, core))]
    far.append(push(qg_part.at[zs[4], pl.ds(half, half)], relay_half.at[1], place(zs[two], y, core)))
    far.append(push(qg_part.at[zs[nz - 3]], relay.at[0], place(zs[last], y, core)))
    far.append(push(qg_part.at[zs[3]], relay.at[1], place(zs[one], y, core)))
    near = [push(qg_part.at[zs[one]], qg_recv.at[0], place(zs[one], y, core))]
    near.append(push(qg_part.at[zs[last]], qg_recv.at[1], place(zs[last], y, core)))
    for i in range(2):
        eg_own[:, :, i * side_width : (i + 1) * side_width] = emb_share(core, i)

    def emb_sum(y_at, i):
        own_part = eg_own[y_at, :, i * side_width : (i + 1) * side_width]
        return own_part + eg_side[y_at, :, columns_of(i)].astype(F32)

    def along_parts(buf, at):
        parts = buf[at, :, :HEAD_DIM].astype(F32)
        return parts[:, 0:1] + parts[:, 1:2] + parts[:, 2:3]

    eg_copies = []
    for i in range(2):
        side_copies[i].wait_recv()
        copies = [None] * ny
        for k in far_first(ny):
            eg_out[k, :, columns_of(i)] = emb_sum(ys[k], i).astype(BF16)
            if i == 0:
                along = along_of(core, ys[k]) + along_parts(eg_side, ys[k])
                eg_out[k, :, :HEAD_DIM] = three_parts(along)
            copies[k] = push(
                span(eg_out.at[k], i), span(eg_recv.at[y], i), place(z, ys[k], core)
            )
        eg_copies.append(copies)
    along = along_of(core, y) + along_parts(eg_side, y)
    def pass_on():
        for copy in far:
            copy.wait_recv()
        for i, k in enumerate((other, two)):
            total = qg_part[zs[k]].astype(F32) + relay[i].astype(F32)
            extra = relay_half[i].astype(F32)
            parts = [total[:half], total[half:]]
            parts[i] = parts[i] + extra
            relay[i] = jnp.concatenate(parts, axis=0).astype(BF16)
            near.append(push(relay.at[i], qg_recv.at[2 + i], place(zs[k], y, core)))

    slope_copies = []
    slopes = []
    for i in range(2):
        emb_grad = emb_sum(y, i)
        for k in range(1, ny):
            eg_copies[i][k].wait_recv()
            emb_grad = emb_grad + eg_recv[ys[ny - k], :, columns_of(i)].astype(F32)
            if i == 0:
                along = along + along_parts(eg_recv, ys[ny - k])
        part = slice(i * side_width, (i + 1) * side_width)
        residual_grad = (emb_grad - embs[i] * along) / norm
        rgrad_ref[:, part] = residual_grad
        slopes.append(residual_grad.astype(BF16))
        slope_all[x, :, part] = slopes[-1]
        place_at = slope_all.at[:, :, pl.ds(i * side_width, side_width)]
        slope_copies.append(exchange(lambda k: place_at.at[x], place_at))
        if i == 0:
            pass_on()

    save(rgrad_ref, rgrad_hbm)
    upstream = dot_nt(jnp.concatenate(slopes, axis=1), weight[0])
    for i in range(2):
        part = slice(i * side_width, (i + 1) * side_width)
        for k in sorted(range(1, nx), key=lambda k: min(k, nx - k)):
            t = received(slope_copies[i], k)
            upstream = upstream + dot_nt(slope_all[t, :, part], weight[nx - k, :, part])
    up_ref[...] = upstream.astype(BF16)
    save(up_ref, up_hbm)

    query_grad = qg_part[z].astype(F32)
    for i, copy in enumerate(near):
        copy.wait_recv()
        query_grad = query_grad + qg_recv[i].astype(F32)
    qgrad_ref[...] = query_grad
    save(qgrad_ref, qgrad_hbm)
    for copy in sent:
        copy.wait_send()
    for copy in saves:
        copy.wait()


def grouped(source, g, heads):
    first = g * heads
    return jnp.concatenate(
        [source[:, (first + h) * HEAD_DIM : (first + h + 1) * HEAD_DIM] for h in range(heads)],
        axis=0,
    )


def spread(source, groups, heads):
    parts = [grouped(source, g, heads) for g in range(groups)]
    empty = jnp.zeros_like(parts[0])
    lines = [
        jnp.concatenate([part if i == g else empty for i in range(groups)], axis=1)
        for g, part in enumerate(parts)
    ]
    return jnp.concatenate(lines, axis=0)


def backward(
    lastq_ref, up_ref, out_ref, key_ref, value_ref, probs_ref, loss_in, qgrad_in, rgrad_in,
    loss_ref, qgrad_ref, rgrad_ref, lgrad_ref, kgrad_ref, vgrad_ref,
):
    loss_ref[...] = loss_in[...]
    qgrad_ref[...] = qgrad_in[...]
    rgrad_ref[...] = rgrad_in[...]
    rows = lastq_ref.shape[0]
    heads = lastq_ref.shape[1] // HEAD_DIM
    scale = 1.0 / HEAD_DIM**0.5
    up = grouped(up_ref, 0, heads)
    mean = jnp.sum(up.astype(F32) * grouped(out_ref, 0, heads), axis=1, keepdims=True)
    probs = probs_ref[...]
    slopes = dot_nt(up, value_ref[...])
    score_slope = (probs.astype(F32) * (slopes - mean)).astype(BF16)
    vgrad_ref[...] = dot_tn(probs, up).astype(BF16)
    lastq = dot_nn(score_slope, key_ref[...]) * scale
    for h in range(heads):
        lgrad_ref[:, h * HEAD_DIM : (h + 1) * HEAD_DIM] = lastq[h * rows : (h + 1) * rows]
    kgrad_ref[...] = (dot_tn(score_slope, grouped(lastq_ref, 0, heads)) * scale).astype(BF16)


def on_device(
    sizes, last_query, key_cache, value_cache, residual, out_weight, query_emb, lengths, positives
):
    nz, ny, nx = sizes
    rows, width = query_emb.shape
    tokens, kv_width = key_cache.shape
    groups = kv_width // HEAD_DIM
    heads = width // kv_width
    inner = CORES * ny
    passages = inner * rows
    chunk = nz // nx * rows
    wide = width + HEAD_DIM
    vmem = pl.BlockSpec(memory_space=pltpu.VMEM)
    hbm = pl.BlockSpec(memory_space=pl.ANY)
    copies = 3 * (nz - 1) + 7 * ny + 8 * (nx - 1)
    loss, query_grad, residual_grad, upstream, attended, probs = pl.pallas_call(
        functools.partial(kernel, sizes),
        out_shape=(
            jax.ShapeDtypeStruct((1, rows), F32),
            jax.ShapeDtypeStruct((rows, width), F32),
            jax.ShapeDtypeStruct((rows, width), F32),
            jax.ShapeDtypeStruct((rows, width), BF16),
            jax.ShapeDtypeStruct((rows, width), F32),
            jax.ShapeDtypeStruct((groups * heads * rows, tokens), BF16),
        ),
        in_specs=[hbm, hbm, hbm, hbm, hbm, hbm, vmem, vmem],
        out_specs=(hbm,) * 6,
        scratch_shapes=[
            pltpu.VMEM((nz, rows, wide), BF16),
            pltpu.VMEM((inner, rows, wide), BF16),
            pltpu.VMEM((nx, width, width), BF16),
            pltpu.VMEM((tokens, kv_width), BF16),
            pltpu.VMEM((tokens, kv_width), BF16),
            pltpu.VMEM((rows, width), BF16),
            pltpu.VMEM((rows, width), BF16),
            pltpu.VMEM((2, rows, HEAD_DIM), jnp.int32),
            pltpu.VMEM((groups * heads * rows, tokens), F32),
            pltpu.VMEM((groups * heads * rows, tokens), BF16),
            pltpu.VMEM((nx, rows, width), BF16),
            pltpu.VMEM((nx, rows, width), BF16),
            pltpu.VMEM((nx, chunk, passages), F32),
            pltpu.VMEM((nx, chunk, passages), F32),
            pltpu.VMEM((nx, 8, passages), F32),
            pltpu.VMEM((passages, HEAD_DIM), F32),
            pltpu.VMEM((nz, 8, HEAD_DIM), F32),
            pltpu.VMEM((nx, chunk, passages), F32),
            pltpu.VMEM((nx * chunk, passages), BF16),
            pltpu.VMEM((nx, 8, HEAD_DIM), F32),
            pltpu.VMEM((ny, rows, wide), BF16),
            pltpu.VMEM((ny, rows, width), F32),
            pltpu.VMEM((ny, rows, wide), BF16),
            pltpu.VMEM((ny, rows, wide), BF16),
            pltpu.VMEM((ny, rows, wide), BF16),
            pltpu.VMEM((nx, rows, width), BF16),
            pltpu.VMEM((nz, rows, width), BF16),
            pltpu.VMEM((4, rows, width), BF16),
            pltpu.VMEM((2, rows, width), BF16),
            pltpu.VMEM((2, rows // 2, width), BF16),
            pltpu.VMEM((1, rows), F32),
            pltpu.VMEM((rows, width), F32),
            pltpu.VMEM((rows, width), F32),
            pltpu.VMEM((rows, width), BF16),
            pltpu.VMEM((rows, width), F32),
            pltpu.SemaphoreType.DMA((5 + nx,)),
            pltpu.SemaphoreType.DMA((6,)),
            pltpu.SemaphoreType.DMA((copies,)),
            pltpu.SemaphoreType.DMA((copies,)),
        ],
        compiler_params=pltpu.CompilerParams(
            collective_id=0, has_side_effects=True, vmem_limit_bytes=60 * 2**20
        ),
    )(
        last_query, key_cache, value_cache, residual, out_weight, query_emb,
        lengths, positives.reshape(1, rows),
    )
    side = heads * HEAD_DIM
    by_heads = pl.BlockSpec((rows, side), lambda g: (0, g))
    by_group = pl.BlockSpec((tokens, HEAD_DIM), lambda g: (0, g))
    line = pl.BlockSpec((1, rows), lambda g: (0, 0))
    loss, query_grad, residual_grad, lastq_grad, key_grad, value_grad = pl.pallas_call(
        backward,
        grid=(groups,),
        out_shape=(
            jax.ShapeDtypeStruct((1, rows), F32),
            jax.ShapeDtypeStruct((rows, width), F32),
            jax.ShapeDtypeStruct((rows, width), F32),
            jax.ShapeDtypeStruct((rows, width), F32),
            jax.ShapeDtypeStruct((tokens, kv_width), BF16),
            jax.ShapeDtypeStruct((tokens, kv_width), BF16),
        ),
        in_specs=[
            by_heads, by_heads, by_heads, by_group, by_group,
            pl.BlockSpec((heads * rows, tokens), lambda g: (g, 0)),
            line, by_heads, by_heads,
        ],
        out_specs=(line, by_heads, by_heads, by_heads, by_group, by_group),
        compiler_params=pltpu.CompilerParams(vmem_limit_bytes=60 * 2**20),
    )(
        last_query, upstream, attended, key_cache, value_cache, probs, loss, query_grad,
        residual_grad,
    )
    return (loss.reshape(rows), query_grad, residual_grad, lastq_grad, key_grad, value_grad)


def solution(mesh, nz=8, ny=4):
    in_specs = (
        P("dp", "mp"),
        P("dp", "mp"),
        P("dp", "mp"),
        P("dp", "mp"),
        P("mp", None),
        P("dp", "mp"),
        P("dp", None),
        P("dp"),
    )
    out_specs = (P("dp"), P("dp", "mp"), P("dp", "mp"), P("dp", "mp"), P("dp", "mp"), P("dp", "mp"))
    sizes = (nz, ny, mesh.shape["mp"])
    return jax.shard_map(
        functools.partial(on_device, sizes),
        mesh=mesh,
        in_specs=in_specs,
        out_specs=out_specs,
        check_vma=False,
    )
```
